128 devices in a mesh: replica: 2 (over x_hi), fsdp: 64 (over x_lo, y, z, core).
Axes of the slice: x: 4 (x_hi: 2, x_lo: 2; x = x_hi * 2 + x_lo), y: 4, z: 4, core: 2. Of those that a mesh axis runs over, the one named last changes fastest.
Arguments:
- tokens: bfloat16 [16384, 2048], P(('replica', 'fsdp')), may hold values from -6 to 6
- doc_ids: int32 [16384], P(('replica', 'fsdp')), may hold values from 0 to 31, as said below
- first_gain: bfloat16 [2048], P('fsdp'), may hold values from 0.5 to 1.5
- query_weight: bfloat16 [2048, 2048], P('fsdp'), may hold values from -0.125 to 0.125
- key_weight: bfloat16 [2048, 256], P('fsdp'), may hold values from -0.125 to 0.125
- value_weight: bfloat16 [2048, 256], P('fsdp'), may hold values from -0.125 to 0.125
- out_weight: bfloat16 [2048, 2048], P('fsdp'), may hold values from -0.5 to 0.5
- second_gain: bfloat16 [2048], P('fsdp'), may hold values from 0.5 to 1.5
- gate_weight: bfloat16 [2048, 5632], P('fsdp'), may hold values from -0.125 to 0.125
- up_weight: bfloat16 [2048, 5632], P('fsdp'), may hold values from -0.125 to 0.125
- down_weight: bfloat16 [5632, 2048], P('fsdp'), may hold values from -0.078125 to 0.078125
- cotangent: bfloat16 [16384, 2048], P(('replica', 'fsdp')), may hold values from -6 to 6
Outputs:
- output: bfloat16 [16384, 2048], P(('replica', 'fsdp'))
- tokens_grad: float32 [16384, 2048], P(('replica', 'fsdp'))
- first_gain_grad: float32 [2048], P('fsdp')
- query_grad: float32 [2048, 2048], P('fsdp')
- key_grad: float32 [2048, 256], P('fsdp')
- value_grad: float32 [2048, 256], P('fsdp')
- out_grad: float32 [2048, 2048], P('fsdp')
- second_gain_grad: float32 [2048], P('fsdp')
- gate_grad: float32 [2048, 5632], P('fsdp')
- up_grad: float32 [2048, 5632], P('fsdp')
- down_grad: float32 [5632, 2048], P('fsdp')
The draws below stay inside these ranges and needn't reach their ends.
Inputs may be any that keep to these rules, and one draw needn't show every extreme that they name: `doc_ids`: within each aligned block of 128 tokens (one device's), ids start at 0 and rise by 0 or 1 from one token to the next, rising only at positions that are multiples of 4 within the block; a sequence is the tokens of one block that share an id; in some block all 128 tokens form one sequence.
All inputs are finite; a program needn't handle non-finite values.
Results may differ from the reference program's by a relative error of at most 0.015.
Values may be sent and summed in bfloat16 or wider, within the bound.
No kernel may reach another device: no remote copies, remote signals or barrier semaphores. Data moves between devices by JAX's collectives and lax.ppermute only.
A program may use at most 576 MiB of HBM per device.

```python
import jax
import jax.numpy as jnp
from jax import lax

D = 2048
HEADS = 32
KV_HEADS = 4
HDIM = 64
FF = 5632
CAP = 128
GROUP = 8
TOKENS = 16384


def draw_doc_ids(key, part):
    key = jax.random.fold_in(key, 11)
    first, second, third, fourth = jax.random.split(key, 4)
    blocks = TOKENS // CAP
    level = jax.random.randint(first, (blocks, 1), 0, 5)
    single = jax.random.randint(third, (), 0, blocks)
    dense = (single + 1 + jax.random.randint(fourth, (), 0, blocks - 1)) % blocks
    block_index = jnp.arange(blocks)[:, None]
    level = jnp.where(block_index == dense, 0, level)
    divisor = jnp.left_shift(jnp.int32(1), level)
    ticket = jax.random.randint(second, (blocks, CAP), 0, 1 << 20)
    position = jnp.arange(CAP)[None, :]
    starts = (position % 4 == 0) & (ticket % divisor == 0)
    starts = jnp.where(block_index == single, False, starts)
    counts = jnp.cumsum(starts[:, 1:].astype(jnp.int32), axis=1)
    ids = jnp.concatenate([jnp.zeros((blocks, 1), jnp.int32), counts], axis=1)
    return ids.reshape(-1).astype(jnp.int32)


def level_of(own_key, shape, shards, low, high):
    loudness = 1.0
    for dim, blocks in shards:
        heights = jax.random.uniform(jax.random.fold_in(jax.random.fold_in(own_key, 6), dim), (blocks,), jnp.float32, low / len(shards), high / len(shards))
        loudness = loudness * jnp.repeat(jnp.exp(heights), shape[dim] // blocks).reshape((-1,) + (1,) * (len(shape) - 1 - dim))
    return loudness


def centred(own_key, dims, deviation, reach, cuts=(), held_as=jnp.bfloat16):
    gain = level_of(own_key, dims, cuts, -0.22, 0.18) if cuts else 1.0
    array = jax.random.normal(own_key, dims, jnp.float32) * deviation * gain
    return jnp.minimum(jnp.maximum(array, -reach), reach).astype(held_as)


def setup_inputs(seed: int = 0) -> dict:
    splits = jax.random.split(jax.random.key(seed), 13)
    tokens = centred(splits[0], (TOKENS, D), 1.0, 6.0, ((0, 128),))
    doc_ids = draw_doc_ids(jax.random.fold_in(splits[12], 71), 0)
    first_gain = jnp.clip(1.0 + 0.1 * jax.random.normal(splits[2], (D,), jnp.float32), 0.5, 1.5).astype(jnp.bfloat16)
    query_weight = centred(splits[3], (D, D), D ** -0.5, 0.125, ((0, 64),))
    key_weight = centred(splits[4], (D, KV_HEADS * HDIM), D ** -0.5, 0.125, ((0, 64),))
    value_weight = centred(splits[5], (D, KV_HEADS * HDIM), D ** -0.5, 0.125, ((0, 64),))
    out_weight = centred(splits[6], (D, D), (D // 16) ** -0.5, 0.5, ((0, 64),))
    second_gain = jnp.clip(1.0 + 0.1 * jax.random.normal(splits[7], (D,), jnp.float32), 0.5, 1.5).astype(jnp.bfloat16)
    gate_weight = centred(splits[8], (D, FF), D ** -0.5, 0.125, ((0, 64),))
    up_weight = centred(splits[9], (D, FF), D ** -0.5, 0.125, ((0, 64),))
    down_weight = centred(splits[10], (FF, D), FF ** -0.5, 0.078125, ((0, 64),))
    cotangent = centred(splits[11], (TOKENS, D), 1.0, 6.0, ((0, 128),))
    return dict(tokens=tokens, doc_ids=doc_ids, first_gain=first_gain, query_weight=query_weight, key_weight=key_weight, value_weight=value_weight, out_weight=out_weight, second_gain=second_gain, gate_weight=gate_weight, up_weight=up_weight, down_weight=down_weight, cotangent=cotangent)


@jax.custom_vjp
def low(v):
    return lax.optimization_barrier(v.astype(jnp.bfloat16)).astype(jnp.float32)

@jax.custom_vjp
def low_back(v):
    return v

def low_keep(v):
    return (low(v), None)

def low_pass(kept, grad):
    return (grad,)

def back_keep(v):
    return (v, None)

def back_low(kept, grad):
    return (low(grad),)
low.defvjp(low_keep, low_pass)
low_back.defvjp(back_keep, back_low)
norm_eps = 1e-05

def turn(u):
    half = u.shape[-1] // 2
    return jnp.concatenate([-u[..., half:], u[..., :half]], axis=-1)

def tables(blocked):
    order = jnp.arange(CAP)
    same = blocked[:, :, None] == blocked[:, None, :]
    earlier = order[None, :] < order[:, None]
    place = lax.optimization_barrier(jnp.sum(jnp.where(same & earlier[None], 1.0, 0.0), axis=2)).astype(jnp.float32)
    half = HDIM // 2
    inverse = 10000.0 ** (jnp.arange(half, dtype=jnp.float32) * (-2.0 / HDIM))
    angle = place[..., None] * inverse
    angle = jnp.concatenate([angle, angle], axis=-1)
    allowed = same & (order[None, :] <= order[:, None])[None]
    return (jnp.cos(angle), jnp.sin(angle), allowed)

def layer(rows, first_gain, query_weight, key_weight, value_weight, out_weight, second_gain, gate_weight, up_weight, down_weight, cosine, sine, allowed):
    highest = lax.Precision.HIGHEST
    blocks = rows.shape[0] // CAP
    first_scale = lax.rsqrt(lax.optimization_barrier(jnp.mean(rows * rows, axis=-1, keepdims=True)) + norm_eps)
    normed = low(rows * first_scale * first_gain)
    queries = low_back(jnp.dot(normed, query_weight, precision=highest))
    keys = low_back(jnp.dot(normed, key_weight, precision=highest))
    values = low(low_back(jnp.dot(normed, value_weight, precision=highest)))
    queries = queries.reshape(blocks, CAP, HEADS, HDIM)
    keys = keys.reshape(blocks, CAP, KV_HEADS, HDIM)
    values = values.reshape(blocks, CAP, KV_HEADS, HDIM)
    rot_queries = low(queries * cosine[:, :, None] + turn(queries) * sine[:, :, None])
    rot_keys = low(keys * cosine[:, :, None] + turn(keys) * sine[:, :, None])
    grouped = rot_queries.reshape(blocks, CAP, KV_HEADS, GROUP, HDIM)
    scores = low_back(jnp.einsum('bikgd,bjkd->bkgij', grouped, rot_keys, precision=highest) * HDIM ** (-0.5))
    scores = jnp.where(allowed[:, None, None], scores, -1e+30)
    probs = low(jax.nn.softmax(scores, axis=-1))
    mixed = jnp.einsum('bkgij,bjkd->bikgd', probs, values, precision=highest)
    mixed = low(low_back(mixed.reshape(blocks * CAP, D)))
    midway = rows + low_back(jnp.dot(mixed, out_weight, precision=highest))
    second_scale = lax.rsqrt(lax.optimization_barrier(jnp.mean(midway * midway, axis=-1, keepdims=True)) + norm_eps)
    normed_two = low(midway * second_scale * second_gain)
    gate_act = low_back(jnp.dot(normed_two, gate_weight, precision=highest))
    up_act = low_back(jnp.dot(normed_two, up_weight, precision=highest))
    hidden = low(jax.nn.silu(gate_act) * up_act)
    return midway + low_back(jnp.dot(hidden, down_weight, precision=highest))

def reference(tokens, doc_ids, first_gain, query_weight, key_weight, value_weight, out_weight, second_gain, gate_weight, up_weight, down_weight, cotangent):
    cosine, sine, allowed = tables(doc_ids.reshape(-1, CAP))
    floats = tuple((item.astype(jnp.float32) for item in (tokens, first_gain, query_weight, key_weight, value_weight, out_weight, second_gain, gate_weight, up_weight, down_weight)))

    def forward(*params):
        return layer(*params, cosine, sine, allowed)
    result, pullback = jax.vjp(forward, *floats)
    grads = pullback(cotangent.astype(jnp.float32))
    return (result.astype(jnp.bfloat16), grads[0], grads[1], grads[2], grads[3], grads[4], grads[5], grads[6], grads[7], grads[8], grads[9])
```

```python
import jax
import jax.numpy as jnp
from jax import lax
from jax.sharding import Mesh, PartitionSpec as P

D = 2048
HEADS = 32
KV_HEADS = 4
HDIM = 64
FF = 5632
CAP = 128
TP = 8
LOCAL_HEADS = HEADS // TP
LOCAL_FF = FF // TP
SEGMENT = LOCAL_FF // 4
PADDED = 192
WIDE = 4 * PADDED
BF16 = jnp.bfloat16
F32 = jnp.float32

norm_eps = 1e-05

RING = ("xh", "xl")
SWAP = [(0, 1), (1, 0)]


def turn(u):
    half = u.shape[-1] // 2
    return jnp.concatenate([-u[..., half:], u[..., :half]], axis=-1)


def turn_back(u):
    half = u.shape[-1] // 2
    return jnp.concatenate([u[..., half:], -u[..., :half]], axis=-1)


def times(left, right):
    return jnp.dot(left, right, preferred_element_type=F32)


def times_t(left, right):
    return lax.dot_general(left, right, (((1,), (1,)), ((), ())), preferred_element_type=F32)


def t_times(left, right):
    return lax.dot_general(left, right, (((0,), (0,)), ((), ())), preferred_element_type=F32)


def rms_scale(rows):
    return lax.rsqrt(jnp.mean(rows * rows, axis=-1, keepdims=True) + norm_eps)


def norm_back(rows, scale, inner):
    return scale * inner - rows * (scale * scale * scale) * jnp.mean(
        inner * rows, axis=-1, keepdims=True
    )


def rotary(ids):
    order = jnp.arange(CAP)
    same = ids[:, :, None] == ids[:, None, :]
    earlier = order[None, :] < order[:, None]
    place = jnp.sum(jnp.where(same & earlier[None], 1.0, 0.0), axis=2).astype(F32)
    half = HDIM // 2
    inverse = 10000.0 ** (jnp.arange(half, dtype=F32) * (-2.0 / HDIM))
    angle = place[..., None] * inverse
    angle = jnp.concatenate([angle, angle], axis=-1)
    allowed = same & (order[None, :] <= order[:, None])[None]
    return jnp.cos(angle), jnp.sin(angle), allowed


def from_ring(item, step):
    return lax.ppermute(item, RING, [(i, (i - step) % 4) for i in range(4)])


def to_ring(item, step):
    return lax.ppermute(item, RING, [(i, (i + step) % 4) for i in range(4)])


def swap(item, axis):
    return lax.ppermute(item, axis, SWAP)


def share(item):
    mine = [item] + [from_ring(item, step) for step in (1, 2, 3)]
    return jnp.concatenate(mine + [swap(part, "c") for part in mine], axis=0)


def collect(left, right, product):
    far = product(left[4 * CAP :], right).astype(BF16)
    near = product(left[: 4 * CAP], right)
    near = near + swap(far, "c").astype(F32)
    total = near[:CAP]
    for step in (1, 2, 3):
        total = total + to_ring(near[step * CAP : (step + 1) * CAP].astype(BF16), step).astype(F32)
    return total


def spread_columns(chunks, xl, c):
    mine = [jnp.where(c == 0, pair[0], pair[1]) for pair in chunks]
    away = [jnp.where(c == 0, pair[1], pair[0]) for pair in chunks]
    came = swap(jnp.concatenate(away, axis=0), "c")
    rows = mine[0].shape[0]
    both = []
    for k in range(2):
        other = came[k * rows : (k + 1) * rows]
        both.append(
            jnp.concatenate(
                [jnp.where(c == 0, mine[k], other), jnp.where(c == 0, other, mine[k])], axis=0
            )
        )
    kept = jnp.where(xl == 0, both[0], both[1])
    came = swap(jnp.where(xl == 0, both[1], both[0]), "xl")
    return jnp.stack([jnp.where(xl == 0, kept, came), jnp.where(xl == 0, came, kept)])


def return_columns(item, xl, c):
    kept = jnp.where(xl == 0, item[0], item[1])
    came = swap(jnp.where(xl == 0, item[1], item[0]), "xl")
    first = jnp.where(xl == 0, kept, came)
    second = jnp.where(xl == 0, came, kept)
    rows = first.shape[0] // 2
    both = jnp.stack([first, second])
    mine = jnp.where(c == 0, both[:, :rows], both[:, rows:])
    came = swap(jnp.where(c == 0, both[:, rows:], both[:, :rows]), "c")
    zero = jnp.where(c == 0, mine, came)
    one = jnp.where(c == 0, came, mine)
    return zero, one


def column_part(item, width, xh):
    out = []
    for k in range(2):
        start = 2 * width * k
        out.append(
            jnp.where(
                xh == 0, item[:, start : start + width], item[:, start + width : start + 2 * width]
            )
        )
    return out


def on_device(
    tokens,
    doc_ids,
    first_gain,
    query_weight,
    key_weight,
    value_weight,
    out_weight,
    second_gain,
    gate_weight,
    up_weight,
    down_weight,
    cotangent,
):
    xh, xl, y, z, c = (lax.axis_index(name) for name in ("xh", "xl", "y", "z", "c"))
    first_col = first_gain.astype(F32)[:, None]
    second_col = second_gain.astype(F32)[:, None]

    def scaled(item, gain):
        return (item.astype(F32) * gain).astype(BF16)

    q_parts = column_part(scaled(query_weight, first_col), 512, xh)
    k_parts = column_part(scaled(key_weight, first_col), 64, xh)
    v_parts = column_part(scaled(value_weight, first_col), 64, xh)
    chunks = [
        [
            jnp.concatenate([q_parts[k][:, 256 * j : 256 * (j + 1)], k_parts[k], v_parts[k]], axis=1)
            for j in range(2)
        ]
        for k in range(2)
    ]
    qkv_full = lax.all_gather(spread_columns(chunks, xl, c), ("y", "z"), axis=1, tiled=True)
    qkv_full = qkv_full.reshape(D, 384)

    source = 2 * xh + c
    pair_rows = jnp.concatenate([out_weight, down_weight], axis=0)
    came = swap(pair_rows, "c")
    low = jnp.where(c == 0, pair_rows, came)
    high = jnp.where(c == 0, came, pair_rows)
    out_pair = jnp.concatenate([low[:32], high[:32]], axis=0).reshape(4, 16, D)
    down_pair = jnp.concatenate([low[32:], high[32:], jnp.zeros((16, D), BF16)], axis=0)
    quarters = jnp.concatenate([out_pair, down_pair.reshape(4, 48, D)], axis=1)
    piece = lax.dynamic_index_in_dim(quarters, y, 0, keepdims=False)
    for step in (1, 2, 3):
        sent = lax.dynamic_index_in_dim(quarters, (y + step) % 4, 0, keepdims=False)
        pairs = []
        for a in range(2):
            for b in range(4):
                for e in range(2):
                    if b == 2 * a + e:
                        pairs.append(((a * 4 + b) * 2 + e, (a * 4 + (b + step) % 4) * 2 + e))
        came = lax.ppermute(sent, ("xh", "y", "c"), pairs)
        piece = jnp.where((source + step) % 4 == y, came, piece)
    out_full = lax.all_gather(piece[:16], ("z", "y"), axis=0, tiled=True)

    g_parts = column_part(scaled(gate_weight, second_col), 1408, xh)
    u_parts = column_part(scaled(up_weight, second_col), 1408, xh)

    def widened(item):
        item = item.reshape(32, 8, SEGMENT)
        item = jnp.pad(item, ((0, 0), (0, 0), (0, PADDED - SEGMENT)))
        return item.reshape(32, 2 * WIDE)

    chunks = []
    for k in range(2):
        g_wide, u_wide = widened(g_parts[k]), widened(u_parts[k])
        chunks.append(
            [
                jnp.concatenate(
                    [g_wide[:, j * WIDE : (j + 1) * WIDE], u_wide[:, j * WIDE : (j + 1) * WIDE]], axis=1
                )
                for j in range(2)
            ]
        )
    feed_full = lax.all_gather(spread_columns(chunks, xl, c), ("y", "z"), axis=1, tiled=True)
    feed_full = feed_full.reshape(D, 2 * WIDE)
    down_full = lax.all_gather(piece[16:], ("z", "y"), axis=0, tiled=True)

    ids = share(doc_ids[None])
    cosine, sine, allowed = rotary(ids)
    cosine = cosine.reshape(TP * CAP, 1, HDIM)
    sine = sine.reshape(TP * CAP, 1, HDIM)
    rows = tokens.astype(F32)
    first_scale = rms_scale(rows)
    normed = share((rows * first_scale).astype(BF16))
    qkv = times(normed, qkv_full)
    queries = qkv[:, :256].reshape(TP * CAP, LOCAL_HEADS, HDIM)
    keys = qkv[:, 256:320].reshape(TP * CAP, 1, HDIM)
    values = qkv[:, 320:].astype(BF16).reshape(TP, CAP, HDIM)
    rot_queries = (queries * cosine + turn(queries) * sine).astype(BF16)
    rot_queries = rot_queries.reshape(TP, CAP, LOCAL_HEADS, HDIM)
    rot_keys = (keys * cosine + turn(keys) * sine).astype(BF16).reshape(TP, CAP, HDIM)
    scores = jnp.einsum("bigd,bjd->bgij", rot_queries, rot_keys, preferred_element_type=F32)
    scores = jnp.where(allowed[:, None], scores * HDIM ** (-0.5), -1e30)
    peak = jnp.max(scores, axis=-1, keepdims=True)
    expo = jnp.exp(scores - peak)
    probs = expo / jnp.sum(expo, axis=-1, keepdims=True)
    probs_low = probs.astype(BF16)
    mixed = jnp.einsum("bgij,bjd->bigd", probs_low, values, preferred_element_type=F32)
    mixed = mixed.reshape(TP * CAP, LOCAL_HEADS * HDIM).astype(BF16)
    midway = rows + collect(mixed, out_full, times)

    second_scale = rms_scale(midway)
    normed_two = share((midway * second_scale).astype(BF16))
    upstream = share(cotangent)
    gate_act = times(normed_two, feed_full[:, :WIDE])
    up_act = times(normed_two, feed_full[:, WIDE:])
    sigmoid_gate = jax.nn.sigmoid(gate_act)
    silu_gate = gate_act * sigmoid_gate
    hidden = (silu_gate * up_act).astype(BF16)
    grad_hidden = times_t(upstream, down_full)
    grad_gate = grad_hidden * up_act * (sigmoid_gate * (1.0 + gate_act * (1.0 - sigmoid_gate)))
    grad_up = grad_hidden * silu_gate
    grad_feed = jnp.concatenate([grad_gate.astype(BF16), grad_up.astype(BF16)], axis=1)
    inner_two = collect(grad_feed, feed_full, times_t)
    grad_mid = cotangent.astype(F32) + norm_back(midway, second_scale, inner_two)
    output = (midway + collect(hidden, down_full, times)).astype(BF16)

    feed_term = t_times(normed_two, grad_feed).astype(BF16).reshape(2, D // 2, 2 * WIDE)
    feed_part = lax.psum_scatter(feed_term, ("y", "z"), scatter_dimension=1, tiled=True)
    down_term = t_times(hidden, upstream).astype(BF16)
    down_part = lax.psum_scatter(down_term, ("z", "y"), scatter_dimension=0, tiled=True)

    grad_attn = share(grad_mid.astype(BF16))
    grad_mixed = times_t(grad_attn, out_full).astype(BF16)
    out_term = t_times(mixed, grad_attn).astype(BF16)
    out_part = lax.psum_scatter(out_term, ("z", "y"), scatter_dimension=0, tiled=True)
    grad_heads = grad_mixed.reshape(TP, CAP, LOCAL_HEADS, HDIM)
    grad_probs = jnp.einsum("bigd,bjd->bgij", grad_heads, values, preferred_element_type=F32)
    delta = jnp.sum(probs * grad_probs, axis=-1, keepdims=True)
    grad_scores = (probs * (grad_probs - delta)).astype(BF16)
    grad_rot_queries = jnp.einsum("bgij,bjd->bigd", grad_scores, rot_keys, preferred_element_type=F32)
    grad_rot_keys = jnp.einsum("bgij,bigd->bjd", grad_scores, rot_queries, preferred_element_type=F32)
    grad_values = jnp.einsum("bgij,bigd->bjd", probs_low, grad_heads, preferred_element_type=F32)
    grad_rot_queries = (grad_rot_queries * HDIM ** (-0.5)).reshape(TP * CAP, LOCAL_HEADS, HDIM)
    grad_rot_keys = (grad_rot_keys * HDIM ** (-0.5)).reshape(TP * CAP, 1, HDIM)
    grad_queries = grad_rot_queries * cosine + turn_back(grad_rot_queries * sine)
    grad_keys = grad_rot_keys * cosine + turn_back(grad_rot_keys * sine)
    grad_qkv = jnp.concatenate(
        [
            grad_queries.reshape(TP * CAP, LOCAL_HEADS * HDIM).astype(BF16),
            grad_keys.reshape(TP * CAP, HDIM).astype(BF16),
            grad_values.reshape(TP * CAP, HDIM).astype(BF16),
        ],
        axis=1,
    )
    qkv_term = t_times(normed, grad_qkv).astype(BF16).reshape(2, D // 2, 384)
    qkv_part = lax.psum_scatter(qkv_term, ("y", "z"), scatter_dimension=1, tiled=True)
    inner_one = collect(grad_qkv, qkv_full, times_t)
    tokens_grad = grad_mid + norm_back(rows, first_scale, inner_one)

    def both_halves(item):
        came = swap(item, "xh")
        return jnp.where(xh == 0, item, came), jnp.where(xh == 0, came, item)

    zero, one = return_columns(qkv_part, xl, c)
    pair_kv = (zero[:, :, 256:].astype(F32) + one[:, :, 256:].astype(F32)).astype(BF16)
    pack = jnp.concatenate([zero[:, :, :256], one[:, :, :256], pair_kv], axis=2)
    halves = both_halves(pack)
    query_raw = jnp.concatenate(
        [halves[h][k][:, :512] for k in range(2) for h in range(2)], axis=1
    ).astype(F32)
    key_raw = jnp.concatenate(
        [halves[h][k][:, 512:576] for k in range(2) for h in range(2)], axis=1
    ).astype(F32)
    value_raw = jnp.concatenate(
        [halves[h][k][:, 576:] for k in range(2) for h in range(2)], axis=1
    ).astype(F32)
    first_grad = (
        jnp.sum(query_raw * query_weight.astype(F32), axis=1)
        + jnp.sum(key_raw * key_weight.astype(F32), axis=1)
        + jnp.sum(value_raw * value_weight.astype(F32), axis=1)
    )

    def narrowed(item):
        item = item.reshape(32, 4, PADDED)[:, :, :SEGMENT]
        return item.reshape(32, LOCAL_FF)

    zero, one = return_columns(feed_part, xl, c)
    halves = both_halves(jnp.stack([zero, one]))

    def feed_columns(start):
        return jnp.concatenate(
            [
                narrowed(halves[h][j, k, :, start : start + WIDE])
                for k in range(2)
                for h in range(2)
                for j in range(2)
            ],
            axis=1,
        ).astype(F32)

    gate_raw = feed_columns(0)
    up_raw = feed_columns(WIDE)
    second_grad = jnp.sum(gate_raw * gate_weight.astype(F32), axis=1) + jnp.sum(
        up_raw * up_weight.astype(F32), axis=1
    )

    piece = jnp.concatenate([out_part, down_part], axis=0)
    parts = [piece]
    for step in (1, 2, 3):
        pairs = []
        for a in range(2):
            for b in range(4):
                for e in range(2):
                    if b == 2 * a + e:
                        pairs.append(((a * 4 + (b + step) % 4) * 2 + e, (a * 4 + b) * 2 + e))
        parts.append(lax.ppermute(piece, ("xh", "y", "c"), pairs))
    ordered = []
    for q in range(4):
        item = parts[0]
        for step in (1, 2, 3):
            item = jnp.where((y + step) % 4 == q, parts[step], item)
        ordered.append(item)
    out_rows = jnp.concatenate([item[:16] for item in ordered], axis=0)
    down_rows = jnp.concatenate([item[16:] for item in ordered], axis=0)
    low = jnp.concatenate([out_rows[:32], down_rows[:88]], axis=0)
    high = jnp.concatenate([out_rows[32:], down_rows[88:176]], axis=0)
    came = swap(jnp.where(c == 0, high, low), "c")
    owned = jnp.where(y % 2 == c, jnp.where(c == 0, low, high), came)
    came = swap(owned, "xh")
    owned = jnp.where(y // 2 == xh, owned, came).astype(F32)

    return (
        output,
        tokens_grad,
        first_grad,
        query_raw * first_col,
        key_raw * first_col,
        value_raw * first_col,
        owned[:32],
        second_grad,
        gate_raw * second_col,
        up_raw * second_col,
        owned[32:],
    )


def solution(mesh):
    fine = Mesh(mesh.devices.reshape(2, 2, 4, 4, 2), ("xh", "xl", "y", "z", "c"))
    everyone = ("xh", "xl", "y", "z", "c")
    group = ("xl", "y", "z", "c")
    in_specs = (
        P(everyone, None),
        P(everyone),
        P(group),
        P(group, None),
        P(group, None),
        P(group, None),
        P(group, None),
        P(group),
        P(group, None),
        P(group, None),
        P(group, None),
        P(everyone, None),
    )
    out_specs = (
        P(everyone, None),
        P(everyone, None),
        P(group),
        P(group, None),
        P(group, None),
        P(group, None),
        P(group, None),
        P(group),
        P(group, None),
        P(group, None),
        P(group, None),
    )
    return jax.shard_map(
        on_device, mesh=fine, in_specs=in_specs, out_specs=out_specs, check_vma=False
    )
```

```python
import jax
import jax.numpy as jnp
from jax import lax
from jax.sharding import Mesh, PartitionSpec as P

D = 2048
HEADS = 32
KV_HEADS = 4
HDIM = 64
FF = 5632
CAP = 128
TP = 8
LOCAL_HEADS = HEADS // TP
WIDE = 768
BF16 = jnp.bfloat16
F32 = jnp.float32

norm_eps = 1e-05

RING = ("xh", "xl")
SWAP = [(0, 1), (1, 0)]


def turn(u):
    half = u.shape[-1] // 2
    return jnp.concatenate([-u[..., half:], u[..., :half]], axis=-1)


def turn_back(u):
    half = u.shape[-1] // 2
    return jnp.concatenate([u[..., half:], -u[..., :half]], axis=-1)


def times(left, right):
    return jnp.dot(left, right, preferred_element_type=F32)


def times_t(left, right):
    return lax.dot_general(left, right, (((1,), (1,)), ((), ())), preferred_element_type=F32)


def t_times(left, right):
    return lax.dot_general(left, right, (((0,), (0,)), ((), ())), preferred_element_type=F32)


def rms_scale(rows):
    return lax.rsqrt(jnp.mean(rows * rows, axis=-1, keepdims=True) + norm_eps)


def norm_back(rows, scale, inner):
    return scale * inner - rows * (scale * scale * scale) * jnp.mean(
        inner * rows, axis=-1, keepdims=True
    )


def rotary(ids):
    order = jnp.arange(CAP)
    same = ids[:, :, None] == ids[:, None, :]
    earlier = order[None, :] < order[:, None]
    place = jnp.sum(jnp.where(same & earlier[None], 1.0, 0.0), axis=2).astype(F32)
    half = HDIM // 2
    inverse = 10000.0 ** (jnp.arange(half, dtype=F32) * (-2.0 / HDIM))
    angle = place[..., None] * inverse
    angle = jnp.concatenate([angle, angle], axis=-1)
    allowed = same & (order[None, :] <= order[:, None])[None]
    return jnp.cos(angle), jnp.sin(angle), allowed


def from_ring(item, step):
    return lax.ppermute(item, RING, [(i, (i - step) % 4) for i in range(4)])


def to_ring(item, step):
    return lax.ppermute(item, RING, [(i, (i + step) % 4) for i in range(4)])


def swap(item, axis):
    return lax.ppermute(item, axis, SWAP)


def share(item):
    mine = [item] + [from_ring(item, step) for step in (1, 2, 3)]
    return jnp.concatenate(mine + [swap(part, "c") for part in mine], axis=0)


def collect(left, right, product):
    far = product(left[4 * CAP :], right).astype(BF16)
    near = product(left[: 4 * CAP], right)
    near = near + swap(far, "c").astype(F32)
    total = near[:CAP]
    for step in (1, 2, 3):
        total = total + to_ring(near[step * CAP : (step + 1) * CAP].astype(BF16), step).astype(F32)
    return total


def spread_columns(chunks, xl, c):
    mine = [jnp.where(c == 0, pair[0], pair[1]) for pair in chunks]
    away = [jnp.where(c == 0, pair[1], pair[0]) for pair in chunks]
    came = swap(jnp.concatenate(away, axis=0), "c")
    rows = mine[0].shape[0]
    both = []
    for k in range(2):
        other = came[k * rows : (k + 1) * rows]
        both.append(
            jnp.concatenate(
                [jnp.where(c == 0, mine[k], other), jnp.where(c == 0, other, mine[k])], axis=0
            )
        )
    kept = jnp.where(xl == 0, both[0], both[1])
    came = swap(jnp.where(xl == 0, both[1], both[0]), "xl")
    return jnp.stack([jnp.where(xl == 0, kept, came), jnp.where(xl == 0, came, kept)])


def return_columns(item, xh, xl, c, reduce):
    rows = item.shape[1] // 2
    mine = jnp.where(c == 0, item[:, :rows], item[:, rows:])
    came = swap(jnp.where(c == 0, item[:, rows:], item[:, :rows]), "c")
    both = reduce(jnp.where(c == 0, mine, came), jnp.where(c == 0, came, mine))
    here = jnp.where(xl == 0, both[0], both[1])
    there = jnp.where(xl == 0, both[1], both[0])
    parts = [here, to_ring(there, 1), to_ring(here, 2), to_ring(there, 3)]
    spot = 2 * xh + xl
    stacked = jnp.stack(parts)
    return [
        [
            lax.dynamic_index_in_dim(stacked, (spot - (2 * h + k)) % 4, 0, keepdims=False)
            for h in range(2)
        ]
        for k in range(2)
    ]


def gather_four(item, axis, spot, dim):
    shape = item.shape[:dim] + (4,) + item.shape[dim:]
    out = jnp.zeros(shape, item.dtype)
    out = lax.dynamic_update_index_in_dim(out, item, spot, dim)
    for step in (1, 2, 3):
        came = lax.ppermute(item, axis, [(i, (i - step) % 4) for i in range(4)])
        out = lax.dynamic_update_index_in_dim(out, came, (spot + step) % 4, dim)
    return out


def scatter_four(item, axis, spot, dim):
    total = lax.dynamic_index_in_dim(item, spot, dim, keepdims=False).astype(F32)
    for step in (1, 2, 3):
        sent = lax.dynamic_index_in_dim(item, (spot + step) % 4, dim, keepdims=False)
        total = total + lax.ppermute(sent, axis, [(i, (i + step) % 4) for i in range(4)]).astype(F32)
    return total


def row_pairs(step, back):
    pairs = []
    for h in range(2):
        for e in range(2):
            first = 2 * h + e
            one = (h * 4 + first) * 2 + e
            other = (h * 4 + (first + step) % 4) * 2 + e
            pairs.append((other, one) if back else (one, other))
    return pairs


def after(item, *others):
    return lax.optimization_barrier((item,) + others)[0]


def order_of_columns(xh):
    place = jnp.arange(768)
    core, owner, row = place // 384, (place % 384) // 48, place % 48
    origin = jnp.where(row < 44, 176 * owner + 88 * core + 44 * xh + row, -1)
    return (jnp.arange(1408)[:, None] == origin[None, :]).astype(BF16)


def column_part(item, width, xh):
    out = []
    for k in range(2):
        start = 2 * width * k
        out.append(
            jnp.where(
                xh == 0, item[:, start : start + width], item[:, start + width : start + 2 * width]
            )
        )
    return out


def on_device(
    tokens,
    doc_ids,
    first_gain,
    query_weight,
    key_weight,
    value_weight,
    out_weight,
    second_gain,
    gate_weight,
    up_weight,
    down_weight,
    cotangent,
):
    xh, xl, y, z, c = (lax.axis_index(name) for name in ("xh", "xl", "y", "z", "c"))
    first_col = first_gain.astype(F32)[:, None]
    second_col = second_gain.astype(F32)[:, None]

    def scaled(item, gain):
        return (item.astype(F32) * gain).astype(BF16)

    q_parts = column_part(scaled(query_weight, first_col), 512, xh)
    k_parts = column_part(scaled(key_weight, first_col), 64, xh)
    v_parts = column_part(scaled(value_weight, first_col), 64, xh)
    chunks = [
        [
            jnp.concatenate([q_parts[k][:, 256 * j : 256 * (j + 1)], k_parts[k], v_parts[k]], axis=1)
            for j in range(2)
        ]
        for k in range(2)
    ]
    spread = spread_columns(chunks, xl, c)
    qkv_full = gather_four(gather_four(spread, "z", z, 1), "y", y, 1).reshape(D, 384)

    source = 2 * xh + c
    came = swap(out_weight, "c")
    out_pair = jnp.concatenate(
        [jnp.where(c == 0, out_weight, came), jnp.where(c == 0, came, out_weight)], axis=0
    )
    quarters = out_pair.reshape(4, 16, D)
    piece = lax.dynamic_index_in_dim(quarters, y, 0, keepdims=False)
    for step in (1, 2, 3):
        sent = lax.dynamic_index_in_dim(quarters, (y + step) % 4, 0, keepdims=False)
        came = lax.ppermute(sent, ("xh", "y", "c"), row_pairs(step, False))
        piece = jnp.where((source + step) % 4 == y, came, piece)
    out_full = gather_four(gather_four(piece, "y", y, 0), "z", z, 0).reshape(256, D)

    wide = jnp.stack([scaled(gate_weight, second_col), scaled(up_weight, second_col)])
    blocks = jnp.concatenate([wide[:, :, 1408 * k : 1408 * (k + 1)] for k in range(4)], axis=0)
    sorted_columns = times(blocks.reshape(256, 1408), order_of_columns(xh)).astype(BF16)
    sorted_columns = sorted_columns.reshape(2, 2, 2, 32, 768)
    chunks = [
        [
            jnp.concatenate(
                [
                    sorted_columns[k, h, item, :, 384 * j : 384 * (j + 1)]
                    for item in range(2)
                    for h in range(2)
                ],
                axis=1,
            )
            for j in range(2)
        ]
        for k in range(2)
    ]
    feed_full = lax.all_gather(spread_columns(chunks, xl, c), ("y", "z"), axis=1, tiled=True)
    feed_full = feed_full.reshape(D, 2 * WIDE)
    down_half = jnp.where(xh == 0, down_weight[:44], down_weight[44:])
    down_half = jnp.pad(down_half, ((0, 4), (0, 0)))
    down_full = lax.all_gather(down_half, ("y", "z"), axis=0, tiled=True)

    ids = share(doc_ids[None])
    cosine, sine, allowed = rotary(ids)
    cosine = cosine.reshape(TP * CAP, 1, HDIM)
    sine = sine.reshape(TP * CAP, 1, HDIM)
    rows = tokens.astype(F32)
    first_scale = rms_scale(rows)
    normed = share((rows * first_scale).astype(BF16))
    upstream = share(after(cotangent, normed))
    qkv = times(normed, qkv_full)
    queries = qkv[:, :256].reshape(TP * CAP, LOCAL_HEADS, HDIM)
    keys = qkv[:, 256:320].reshape(TP * CAP, 1, HDIM)
    values = qkv[:, 320:].astype(BF16).reshape(TP, CAP, HDIM)
    rot_queries = (queries * cosine + turn(queries) * sine).astype(BF16)
    rot_queries = rot_queries.reshape(TP, CAP, LOCAL_HEADS, HDIM)
    rot_keys = (keys * cosine + turn(keys) * sine).astype(BF16).reshape(TP, CAP, HDIM)
    scores = jnp.einsum("bigd,bjd->bgij", rot_queries, rot_keys, preferred_element_type=F32)
    scores = jnp.where(allowed[:, None], scores * HDIM ** (-0.5), -1e30)
    peak = jnp.max(scores, axis=-1, keepdims=True)
    expo = jnp.exp(scores - peak)
    probs = expo / jnp.sum(expo, axis=-1, keepdims=True)
    probs_low = probs.astype(BF16)
    mixed = jnp.einsum("bgij,bjd->bigd", probs_low, values, preferred_element_type=F32)
    mixed = mixed.reshape(TP * CAP, LOCAL_HEADS * HDIM).astype(BF16)
    midway = rows + collect(mixed, out_full, times)

    second_scale = rms_scale(midway)
    normed_two = share((midway * second_scale).astype(BF16))
    gate_act = times(normed_two, feed_full[:, :WIDE])
    up_act = times(normed_two, feed_full[:, WIDE:])
    sigmoid_gate = jax.nn.sigmoid(gate_act)
    silu_gate = gate_act * sigmoid_gate
    hidden = (silu_gate * up_act).astype(BF16)
    grad_hidden = times_t(upstream, down_full)
    grad_gate = grad_hidden * up_act * (sigmoid_gate * (1.0 + gate_act * (1.0 - sigmoid_gate)))
    grad_up = grad_hidden * silu_gate
    grad_feed = jnp.concatenate([grad_gate.astype(BF16), grad_up.astype(BF16)], axis=1)
    inner_two = collect(grad_feed, feed_full, times_t)
    grad_mid = cotangent.astype(F32) + norm_back(midway, second_scale, inner_two)
    feed_term = t_times(normed_two, grad_feed).astype(BF16).reshape(2, 16, 64, 2 * WIDE)
    feed_term = feed_term.swapaxes(0, 1).reshape(16, 128, 2 * WIDE)
    down_term = t_times(hidden, upstream).astype(BF16).reshape(16, 48, D)
    corner = jnp.concatenate(
        [down_term[:, 16 * k : 16 * (k + 1), 2 * WIDE :] for k in range(3)], axis=2
    )
    pack = jnp.concatenate([feed_term, down_term[:, :, : 2 * WIDE], corner], axis=1)
    pack = pack.reshape(16 * 192, 2 * WIDE)
    pack = lax.psum_scatter(pack, ("y", "z"), scatter_dimension=0, tiled=True)
    feed_part = pack[:128].reshape(2, 64, 2 * WIDE)
    corner = pack[176:]
    corner = jnp.concatenate([corner[:, 512 * k : 512 * (k + 1)] for k in range(3)], axis=0)
    down_part = jnp.concatenate([pack[128:176], corner], axis=1)

    grad_attn = share(grad_mid.astype(BF16))
    grad_mixed = times_t(grad_attn, out_full).astype(BF16)
    out_term = t_times(mixed, grad_attn).astype(BF16)
    out_part = scatter_four(out_term.reshape(4, 4, 16, D), "z", z, 0).astype(BF16)
    out_part = scatter_four(out_part, "y", y, 0).astype(BF16)
    output = midway + collect(after(hidden, grad_attn), down_full, times)
    output = output.astype(BF16)
    grad_heads = grad_mixed.reshape(TP, CAP, LOCAL_HEADS, HDIM)
    grad_probs = jnp.einsum("bigd,bjd->bgij", grad_heads, values, preferred_element_type=F32)
    delta = jnp.sum(probs * grad_probs, axis=-1, keepdims=True)
    grad_scores = (probs * (grad_probs - delta)).astype(BF16)
    grad_rot_queries = jnp.einsum("bgij,bjd->bigd", grad_scores, rot_keys, preferred_element_type=F32)
    grad_rot_keys = jnp.einsum("bgij,bigd->bjd", grad_scores, rot_queries, preferred_element_type=F32)
    grad_values = jnp.einsum("bgij,bigd->bjd", probs_low, grad_heads, preferred_element_type=F32)
    grad_rot_queries = (grad_rot_queries * HDIM ** (-0.5)).reshape(TP * CAP, LOCAL_HEADS, HDIM)
    grad_rot_keys = (grad_rot_keys * HDIM ** (-0.5)).reshape(TP * CAP, 1, HDIM)
    grad_queries = grad_rot_queries * cosine + turn_back(grad_rot_queries * sine)
    grad_keys = grad_rot_keys * cosine + turn_back(grad_rot_keys * sine)
    grad_qkv = jnp.concatenate(
        [
            grad_queries.reshape(TP * CAP, LOCAL_HEADS * HDIM).astype(BF16),
            grad_keys.reshape(TP * CAP, HDIM).astype(BF16),
            grad_values.reshape(TP * CAP, HDIM).astype(BF16),
        ],
        axis=1,
    )
    qkv_term = t_times(normed, grad_qkv).astype(BF16).reshape(2, D // 2, 384)
    qkv_part = scatter_four(qkv_term.reshape(2, 4, 4, 64, 384), "y", y, 1).astype(BF16)
    qkv_part = scatter_four(qkv_part, "z", z, 1).astype(BF16)
    inner_one = collect(grad_qkv, qkv_full, times_t)
    tokens_grad = grad_mid + norm_back(rows, first_scale, inner_one)

    def with_pair(zero, one):
        pair = zero[:, :, 256:].astype(F32) + one[:, :, 256:].astype(F32)
        return jnp.concatenate([zero[:, :, :256], one[:, :, :256], pair.astype(BF16)], axis=2)

    parts = return_columns(qkv_part, xh, xl, c, with_pair)

    def joined(start, end):
        return jnp.concatenate(
            [parts[k][h][:, start:end] for k in range(2) for h in range(2)], axis=1
        ).astype(F32)

    query_raw, key_raw, value_raw = joined(0, 512), joined(512, 576), joined(576, 640)
    first_grad = (
        jnp.sum(query_raw * query_weight.astype(F32), axis=1)
        + jnp.sum(key_raw * key_weight.astype(F32), axis=1)
        + jnp.sum(value_raw * value_weight.astype(F32), axis=1)
    )

    parts = return_columns(
        feed_part, xh, xl, c, lambda zero, one: jnp.concatenate([zero, one], axis=2)
    )
    shuffle = jnp.concatenate([order_of_columns(0), order_of_columns(1)], axis=1)
    rows_of = []
    for item in range(2):
        for k in range(2):
            for half in range(2):
                start = item * WIDE + half * 384
                rows_of.append(
                    jnp.concatenate(
                        [
                            parts[k][h][:, e * 2 * WIDE + start : e * 2 * WIDE + start + 384]
                            for h in range(2)
                            for e in range(2)
                        ],
                        axis=1,
                    )
                )
    unsorted = times_t(jnp.concatenate(rows_of, axis=0), shuffle).reshape(2, 4, 32, 1408)
    gate_raw = jnp.concatenate([unsorted[0, k] for k in range(4)], axis=1)
    up_raw = jnp.concatenate([unsorted[1, k] for k in range(4)], axis=1)
    second_grad = jnp.sum(gate_raw * gate_weight.astype(F32), axis=1) + jnp.sum(
        up_raw * up_weight.astype(F32), axis=1
    )

    came = swap(down_part, "xh")
    down_grad = jnp.concatenate(
        [jnp.where(xh == 0, down_part, came)[:44], jnp.where(xh == 0, came, down_part)[:44]], axis=0
    ).astype(F32)

    parts = [out_part]
    for step in (1, 2, 3):
        parts.append(lax.ppermute(out_part, ("xh", "y", "c"), row_pairs(step, True)))
    ordered = []
    for q in range(4):
        item = parts[0]
        for step in (1, 2, 3):
            item = jnp.where((y + step) % 4 == q, parts[step], item)
        ordered.append(item)
    low = jnp.concatenate(ordered[:2], axis=0)
    high = jnp.concatenate(ordered[2:], axis=0)
    came = swap(jnp.where(c == 0, high, low), "c")
    owned = jnp.where(y % 2 == c, jnp.where(c == 0, low, high), came)
    came = swap(owned, "xh")
    out_grad = jnp.where(y // 2 == xh, owned, came).astype(F32)

    return (
        output,
        tokens_grad,
        first_grad,
        query_raw * first_col,
        key_raw * first_col,
        value_raw * first_col,
        out_grad,
        second_grad,
        gate_raw * second_col,
        up_raw * second_col,
        down_grad,
    )


def solution(mesh):
    fine = Mesh(mesh.devices.reshape(2, 2, 4, 4, 2), ("xh", "xl", "y", "z", "c"))
    everyone = ("xh", "xl", "y", "z", "c")
    group = ("xl", "y", "z", "c")
    in_specs = (
        P(everyone, None),
        P(everyone),
        P(group),
        P(group, None),
        P(group, None),
        P(group, None),
        P(group, None),
        P(group),
        P(group, None),
        P(group, None),
        P(group, None),
        P(everyone, None),
    )
    out_specs = (
        P(everyone, None),
        P(everyone, None),
        P(group),
        P(group, None),
        P(group, None),
        P(group, None),
        P(group, None),
        P(group),
        P(group, None),
        P(group, None),
        P(group, None),
    )
    return jax.shard_map(
        on_device, mesh=fine, in_specs=in_specs, out_specs=out_specs, check_vma=False
    )
```

```python
import jax
import jax.numpy as jnp
import ml_dtypes
import numpy as np
from jax import lax
from jax.experimental import pallas as pl
from jax.experimental.pallas import tpu as pltpu
from jax.sharding import Mesh, PartitionSpec as P

D = 2048
HDIM = 64
CAP = 128
WIDE = 768
BF16 = jnp.bfloat16
F32 = jnp.float32

norm_eps = 1e-05

RING = ("xh", "xl")
SWAP = [(0, 1), (1, 0)]


def dot_nn(left, right):
    return lax.dot_general(left, right, (((1,), (0,)), ((), ())), preferred_element_type=F32)


def dot_nt(left, right):
    return lax.dot_general(left, right, (((1,), (1,)), ((), ())), preferred_element_type=F32)


def dot_tn(left, right):
    return lax.dot_general(left, right, (((0,), (0,)), ((), ())), preferred_element_type=F32)


ANY = pl.BlockSpec(memory_space=pl.ANY)


def part_copies(parts, whole, sems):
    copies, start = [], 0
    for k, part in enumerate(parts):
        rows = min(part.shape[0] // CAP, 2) * CAP
        copies.append(
            pltpu.make_async_copy(part.at[pl.ds(0, rows)], whole.at[pl.ds(start, rows)], sems.at[k])
        )
        start += rows
    return copies


def feed_copies(packed, feed, sems):
    copies = []
    for k in range(16):
        for h in range(2):
            copies.append(
                pltpu.make_async_copy(
                    packed.at[pl.ds(192 * k + 64 * h, 64)],
                    feed.at[pl.ds(1024 * h + 64 * k, 64)],
                    sems.at[2 * k + h],
                )
            )
    return copies


def down_copies(packed, down, sems):
    copies = []
    for k in range(16):
        copies.append(
            pltpu.make_async_copy(
                packed.at[pl.ds(192 * k + 128, 48)],
                down.at[pl.ds(48 * k, 48), pl.ds(0, 1536)],
                sems.at[4 * k],
            )
        )
        for h in range(3):
            copies.append(
                pltpu.make_async_copy(
                    packed.at[pl.ds(192 * k + 176, 16), pl.ds(512 * h, 512)],
                    down.at[pl.ds(48 * k + 16 * h, 16), pl.ds(1536, 512)],
                    sems.at[4 * k + 1 + h],
                )
            )
    return copies


def feed_kernel(*refs):
    x_parts, c_parts, packed = refs[:7], refs[7:14], refs[14]
    hidden, grads, far, near = refs[15:19]
    x, c, feed, down, x_sems, c_sems, f_sems, d_sems = refs[19:]
    step = pl.program_id(0)

    @pl.when(step == 0)
    def _():
        first = part_copies(x_parts, x, x_sems)
        second = feed_copies(packed, feed, f_sems)
        third = part_copies(c_parts, c, c_sems)
        fourth = down_copies(packed, down, d_sems)
        for group in (first, second, third, fourth):
            for copy in group:
                copy.start()
        for copy in first + second:
            copy.wait()

    rows = pl.ds(pl.multiple_of(((step + 2) % 4) * 256, 256), 256)
    block = x[rows, :]
    gate = dot_nn(block, feed[:, :WIDE])
    up = dot_nn(block, feed[:, WIDE:])

    @pl.when(step == 0)
    def _():
        third = part_copies(c_parts, c, c_sems)
        fourth = down_copies(packed, down, d_sems)
        for copy in third + fourth:
            copy.wait()

    back = dot_nt(c[rows, :], down[...])
    sig = jax.nn.sigmoid(gate)
    silu = gate * sig
    hidden[...] = (silu * up).astype(BF16)
    grad_gate = (back * up * (sig * (1.0 + gate * (1.0 - sig)))).astype(BF16)
    grad_up = (back * silu).astype(BF16)
    grads[:, :WIDE] = grad_gate
    grads[:, WIDE:] = grad_up
    inner = dot_nt(grads[...], feed[...])

    @pl.when(step < 2)
    def _():
        far[...] = inner.astype(BF16)

    @pl.when(step >= 2)
    def _():
        near[...] = inner


def feed_forward(x_parts, c_parts, packed):
    row = lambda i: ((i + 2) % 4, 0)
    return pl.pallas_call(
        feed_kernel,
        grid=(4,),
        in_specs=[ANY] * 15,
        out_specs=[
            pl.BlockSpec((256, WIDE), row),
            pl.BlockSpec((256, 2 * WIDE), row),
            pl.BlockSpec((256, D), lambda i: (jnp.minimum(i, 1), 0)),
            pl.BlockSpec((256, D), lambda i: (jnp.maximum(i - 2, 0), 0)),
        ],
        out_shape=[
            jax.ShapeDtypeStruct((1024, WIDE), BF16),
            jax.ShapeDtypeStruct((1024, 2 * WIDE), BF16),
            jax.ShapeDtypeStruct((512, D), BF16),
            jax.ShapeDtypeStruct((512, D), F32),
        ],
        scratch_shapes=[
            pltpu.VMEM((1024, D), BF16),
            pltpu.VMEM((1024, D), BF16),
            pltpu.VMEM((D, 2 * WIDE), BF16),
            pltpu.VMEM((WIDE, D), BF16),
            pltpu.SemaphoreType.DMA((7,)),
            pltpu.SemaphoreType.DMA((7,)),
            pltpu.SemaphoreType.DMA((32,)),
            pltpu.SemaphoreType.DMA((64,)),
        ],
        compiler_params=pltpu.CompilerParams(vmem_limit_bytes=50 * 1024 * 1024),
        cost_estimate=pl.CostEstimate(
            flops=2 * 1024 * D * WIDE * 5, bytes_accessed=28 * 2**20, transcendentals=1024 * WIDE
        ),
    )(*x_parts, *c_parts, packed)


def grads_kernel(*refs):
    x_parts, c_parts, hidden_hbm, grads_hbm = refs[:7], refs[7:14], refs[14], refs[15]
    out = refs[16]
    x, c, hidden, grads, pack, x_sems, c_sems, in_sems, sems = refs[17:]
    first = part_copies(x_parts, x, x_sems)
    second = part_copies(c_parts, c, c_sems)
    loads = [
        pltpu.make_async_copy(grads_hbm, grads, in_sems.at[0]),
        pltpu.make_async_copy(hidden_hbm, hidden, in_sems.at[1]),
    ]
    for copy in first + loads + second:
        copy.start()
    for copy in first + loads[:1]:
        copy.wait()
    stores = []

    def store(row, rows):
        copy = pltpu.make_async_copy(
            pack.at[pl.ds(row, rows)], out.at[pl.ds(row, rows)], sems.at[len(stores)]
        )
        copy.start()
        stores.append(copy)

    for k in range(8):
        tile = dot_tn(x[:, 256 * k : 256 * (k + 1)], grads[...]).astype(BF16)
        half, spot = k // 4, (k % 4) * 4
        for j in range(4):
            row = 192 * (spot + j) + 64 * half
            pack[row : row + 64, :] = tile[64 * j : 64 * (j + 1)]
            store(row, 64)
    for copy in second + loads[1:]:
        copy.wait()
    for k in range(2):
        tile = dot_tn(hidden[:, 384 * k : 384 * (k + 1)], c[...]).astype(BF16)
        for j in range(8):
            row = 192 * (8 * k + j) + 128
            piece = tile[48 * j : 48 * (j + 1)]
            pack[row : row + 48, :] = piece[:, :1536]
            for h in range(3):
                pack[row + 48 : row + 64, 512 * h : 512 * (h + 1)] = piece[
                    16 * h : 16 * (h + 1), 1536:
                ]
            store(row, 64)
    for copy in stores:
        copy.wait()


def feed_grads(x_parts, c_parts, hidden, grads):
    return pl.pallas_call(
        grads_kernel,
        in_specs=[ANY] * 16,
        out_specs=ANY,
        out_shape=jax.ShapeDtypeStruct((3072, 1536), BF16),
        scratch_shapes=[
            pltpu.VMEM((1024, D), BF16),
            pltpu.VMEM((1024, D), BF16),
            pltpu.VMEM((1024, WIDE), BF16),
            pltpu.VMEM((1024, 2 * WIDE), BF16),
            pltpu.VMEM((3072, 2 * WIDE), BF16),
            pltpu.SemaphoreType.DMA((7,)),
            pltpu.SemaphoreType.DMA((7,)),
            pltpu.SemaphoreType.DMA((2,)),
            pltpu.SemaphoreType.DMA((48,)),
        ],
        compiler_params=pltpu.CompilerParams(vmem_limit_bytes=50 * 1024 * 1024),
        cost_estimate=pl.CostEstimate(
            flops=2 * 1024 * D * WIDE * 3, bytes_accessed=22 * 2**20, transcendentals=0
        ),
    )(*x_parts, *c_parts, hidden, grads)


def rotary_table():
    place = np.arange(CAP, dtype=np.float32)[:, None]
    inverse = np.float32(10000.0) ** (np.arange(32, dtype=np.float32) * np.float32(-2.0 / HDIM))
    angle = (place * inverse).astype(np.float32)
    cosine, sine = np.cos(angle), np.sin(angle)
    zero, one = np.zeros((CAP, 64), np.float32), np.ones((CAP, 64), np.float32)
    straight = np.concatenate([cosine, cosine] * 5 + [one], axis=1)
    down = np.concatenate([-sine, zero[:, :32]] * 5 + [zero], axis=1)
    up = np.concatenate([zero[:, :32], sine] * 5 + [zero], axis=1)
    table = np.concatenate([straight, down, up], axis=1)
    high = table.astype(ml_dtypes.bfloat16)
    rest = (table - high.astype(np.float32)).astype(ml_dtypes.bfloat16)
    return jnp.asarray(np.stack([high, rest]))


def id_copies(parts, ids, sems):
    copies, spot = [], 0
    for k, part in enumerate(parts):
        for j in range(part.shape[0] // 144):
            copies.append(
                pltpu.make_async_copy(
                    part.at[pl.ds(144 * j + CAP, 16), pl.ds(0, CAP)], ids.at[spot], sems.at[spot]
                )
            )
            spot += 1
    return copies


def long_copies(parts, whole, sems):
    copies, spot = [], 0
    for part in parts:
        for j in range(part.shape[0] // 144):
            copies.append(
                pltpu.make_async_copy(
                    part.at[pl.ds(144 * j, CAP)], whole.at[pl.ds(CAP * spot, CAP)], sems.at[spot]
                )
            )
            spot += 1
    return copies


def lane_of(shape, dim):
    return lax.broadcasted_iota(jnp.int32, shape, dim)


def block_tables(ids, table):
    row = jnp.broadcast_to(ids.astype(F32)[:1], (CAP, CAP))
    same = row == row.T
    to, frm = lane_of((CAP, CAP), 0), lane_of((CAP, CAP), 1)
    place = jnp.sum(jnp.where(same & (frm < to), 1.0, 0.0), axis=1, keepdims=True)
    chosen = (frm.astype(F32) == place).astype(BF16)
    factors = dot_nn(chosen, table[0]) + dot_nn(chosen, table[1])
    return same & (frm <= to), factors


def turned(item, factors, sign):
    other = (
        pltpu.roll(item, 352, 1) * factors[:, 384:768] + pltpu.roll(item, 32, 1) * factors[:, 768:]
    )
    return item * factors[:, :384] + sign * other


def stack_heads(item):
    head = lane_of((CAP, 256), 1) // 64
    return jnp.concatenate([jnp.where(head == h, item, 0).astype(BF16) for h in range(4)], axis=0)


def spreads():
    lane, own = lane_of((CAP, 256), 1) % 64, lane_of((CAP, 256), 0)
    return (lane == own).astype(BF16), (lane + 64 == own).astype(BF16)


def softmax_heads(queries, keys, allowed):
    scores = dot_nt(stack_heads(queries), keys) * 0.125
    out = []
    for h in range(4):
        part = jnp.where(allowed, scores[CAP * h : CAP * (h + 1)], -1e30)
        expo = jnp.exp(part - jnp.max(part, axis=1, keepdims=True))
        out.append(expo / jnp.sum(expo, axis=1, keepdims=True))
    return out


def attend_kernel(*refs):
    parts, table, w_hbm, o_hbm = refs[:7], refs[7], refs[8], refs[9]
    queries, key_values, mixed, far, near = refs[10:15]
    x, ids, w, o, x_sems, i_sems, w_sems = refs[15:]
    step = pl.program_id(0)
    loads = [
        pltpu.make_async_copy(w_hbm, w, w_sems.at[0]),
        pltpu.make_async_copy(o_hbm, o, w_sems.at[1]),
    ]

    @pl.when(step == 0)
    def _():
        copies = long_copies(parts, x, x_sems) + id_copies(parts, ids, i_sems) + loads
        for copy in copies:
            copy.start()
        for copy in copies:
            copy.wait()

    half = 1 - step
    rows = pl.ds(pl.multiple_of(half * 512, 512), 512)
    qkv = dot_nn(x[rows, :], w[...])
    to_key, to_value = spreads()
    for k in range(4):
        allowed, factors = block_tables(ids[half * 4 + k], table)
        block = turned(qkv[CAP * k : CAP * (k + 1)], factors, 1.0).astype(BF16)
        here = slice(CAP * k, CAP * (k + 1))
        queries[here, :] = block[:, :256]
        key_values[here, :] = block[:, 256:]
        keys = dot_nn(block[:, 256:], to_key).astype(BF16)
        values = dot_nn(block[:, 256:], to_value).astype(BF16)
        probs = softmax_heads(block[:, :256], keys, allowed)
        probs = jnp.concatenate([item.astype(BF16) for item in probs], axis=1)
        mixed[here, :] = dot_nn(probs, stack_heads(values)).astype(BF16)
    total = dot_nn(mixed[...], o[...])

    @pl.when(step == 0)
    def _():
        far[...] = total.astype(BF16)

    @pl.when(step == 1)
    def _():
        near[...] = total


def attend(parts, table, qkv_full, out_full):
    row = lambda i: (1 - i, 0)
    still = lambda i: (0, 0)
    return pl.pallas_call(
        attend_kernel,
        grid=(2,),
        in_specs=[ANY] * 7 + [pl.BlockSpec((2, CAP, 1152), lambda i: (0, 0, 0))] + [ANY] * 2,
        out_specs=[
            pl.BlockSpec((512, 256), row),
            pl.BlockSpec((512, CAP), row),
            pl.BlockSpec((512, 256), row),
            pl.BlockSpec((512, D), still),
            pl.BlockSpec((512, D), still),
        ],
        out_shape=[
            jax.ShapeDtypeStruct((1024, 256), BF16),
            jax.ShapeDtypeStruct((1024, CAP), BF16),
            jax.ShapeDtypeStruct((1024, 256), BF16),
            jax.ShapeDtypeStruct((512, D), BF16),
            jax.ShapeDtypeStruct((512, D), F32),
        ],
        scratch_shapes=[
            pltpu.VMEM((1024, D), BF16),
            pltpu.VMEM((8, 16, CAP), BF16),
            pltpu.VMEM((D, 384), BF16),
            pltpu.VMEM((256, D), BF16),
            pltpu.SemaphoreType.DMA((8,)),
            pltpu.SemaphoreType.DMA((8,)),
            pltpu.SemaphoreType.DMA((2,)),
        ],
        compiler_params=pltpu.CompilerParams(vmem_limit_bytes=40 * 1024 * 1024),
        cost_estimate=pl.CostEstimate(
            flops=2 * 1024 * D * 640 * 2, bytes_accessed=15 * 2**20, transcendentals=2**19
        ),
    )(*parts, table, qkv_full, out_full)


def attend_back_kernel(*refs):
    parts, id_parts, table, w_hbm, o_hbm, queries, key_values = (
        refs[:7],
        refs[7:14],
        refs[14],
        refs[15],
        refs[16],
        refs[17],
        refs[18],
    )
    grads, far, near = refs[19:22]
    g, ids, w, o, g_sems, i_sems, w_sems = refs[22:]
    step = pl.program_id(0)
    loads = [
        pltpu.make_async_copy(w_hbm, w, w_sems.at[0]),
        pltpu.make_async_copy(o_hbm, o, w_sems.at[1]),
    ]

    @pl.when(step == 0)
    def _():
        copies = part_copies(parts, g, g_sems) + id_copies(id_parts, ids, i_sems) + loads
        for copy in copies:
            copy.start()
        for copy in copies:
            copy.wait()

    half = 1 - step
    rows = pl.ds(pl.multiple_of(half * 512, 512), 512)
    grad_mixed = dot_nt(g[rows, :], o[...]).astype(BF16)
    to_key, to_value = spreads()
    for k in range(4):
        allowed, factors = block_tables(ids[half * 4 + k], table)
        here = slice(CAP * k, CAP * (k + 1))
        query, both = queries[here, :], key_values[here, :]
        keys = dot_nn(both, to_key).astype(BF16)
        values = dot_nn(both, to_value).astype(BF16)
        probs = softmax_heads(query, keys, allowed)
        grad_heads = stack_heads(grad_mixed[here])
        grad_probs = dot_nt(grad_heads, values)
        scores = []
        for h in range(4):
            part = grad_probs[CAP * h : CAP * (h + 1)]
            delta = jnp.sum(probs[h] * part, axis=1, keepdims=True)
            scores.append((probs[h] * (part - delta)).astype(BF16))
        grad_query = dot_nn(jnp.concatenate(scores, axis=1), stack_heads(keys)) * 0.125
        folded = dot_nt(stack_heads(query), to_key).astype(BF16)
        grad_folded = dot_nt(grad_heads, to_value).astype(BF16)
        low = jnp.concatenate([item.astype(BF16) for item in probs], axis=0)
        grad_both = dot_tn(jnp.concatenate(scores, axis=0), folded) * 0.125 + dot_tn(low, grad_folded)
        item = jnp.concatenate([grad_query, grad_both], axis=1)
        grads[here, :] = turned(item, factors, -1.0).astype(BF16)
    total = dot_nt(grads[...], w[...])

    @pl.when(step == 0)
    def _():
        far[...] = total.astype(BF16)

    @pl.when(step == 1)
    def _():
        near[...] = total


def attend_back(parts, id_parts, table, qkv_full, out_full, queries, key_values):
    row = lambda i: (1 - i, 0)
    still = lambda i: (0, 0)
    return pl.pallas_call(
        attend_back_kernel,
        grid=(2,),
        in_specs=[ANY] * 14
        + [pl.BlockSpec((2, CAP, 1152), lambda i: (0, 0, 0))]
        + [ANY] * 2
        + [pl.BlockSpec((512, 256), row), pl.BlockSpec((512, CAP), row)],
        out_specs=[
            pl.BlockSpec((512, 384), row),
            pl.BlockSpec((512, D), still),
            pl.BlockSpec((512, D), still),
        ],
        out_shape=[
            jax.ShapeDtypeStruct((1024, 384), BF16),
            jax.ShapeDtypeStruct((512, D), BF16),
            jax.ShapeDtypeStruct((512, D), F32),
        ],
        scratch_shapes=[
            pltpu.VMEM((1024, D), BF16),
            pltpu.VMEM((8, 16, CAP), BF16),
            pltpu.VMEM((D, 384), BF16),
            pltpu.VMEM((256, D), BF16),
            pltpu.SemaphoreType.DMA((7,)),
            pltpu.SemaphoreType.DMA((8,)),
            pltpu.SemaphoreType.DMA((2,)),
        ],
        compiler_params=pltpu.CompilerParams(vmem_limit_bytes=40 * 1024 * 1024),
        cost_estimate=pl.CostEstimate(
            flops=2 * 1024 * D * 640 * 2, bytes_accessed=15 * 2**20, transcendentals=2**19
        ),
    )(*parts, *id_parts, table, qkv_full, out_full, queries, key_values)


def small_grads_kernel(*refs):
    x_parts, g_parts, mixed_hbm, grads_hbm = refs[:7], refs[7:14], refs[14], refs[15]
    qkv_term, out_term = refs[16:18]
    x, g, mixed, grads, x_sems, g_sems, in_sems = refs[18:]
    first = long_copies(x_parts, x, x_sems)
    second = part_copies(g_parts, g, g_sems)
    loads = [
        pltpu.make_async_copy(grads_hbm, grads, in_sems.at[0]),
        pltpu.make_async_copy(mixed_hbm, mixed, in_sems.at[1]),
    ]
    for copy in first + loads + second:
        copy.start()
    for copy in first + loads[:1]:
        copy.wait()
    for k in range(8):
        here = slice(256 * k, 256 * (k + 1))
        qkv_term[here, :] = dot_tn(x[:, here], grads[...]).astype(BF16)
    for copy in second + loads[1:]:
        copy.wait()
    out_term[...] = dot_tn(mixed[...], g[...]).astype(BF16)


def small_grads(x_parts, g_parts, mixed, grads):
    whole = pl.BlockSpec(memory_space=pltpu.VMEM)
    return pl.pallas_call(
        small_grads_kernel,
        in_specs=[ANY] * 16,
        out_specs=[whole, whole],
        out_shape=[jax.ShapeDtypeStruct((D, 384), BF16), jax.ShapeDtypeStruct((256, D), BF16)],
        scratch_shapes=[
            pltpu.VMEM((1024, D), BF16),
            pltpu.VMEM((1024, D), BF16),
            pltpu.VMEM((1024, 256), BF16),
            pltpu.VMEM((1024, 384), BF16),
            pltpu.SemaphoreType.DMA((8,)),
            pltpu.SemaphoreType.DMA((7,)),
            pltpu.SemaphoreType.DMA((2,)),
        ],
        compiler_params=pltpu.CompilerParams(vmem_limit_bytes=40 * 1024 * 1024),
        cost_estimate=pl.CostEstimate(
            flops=2 * 1024 * D * 640, bytes_accessed=12 * 2**20, transcendentals=0
        ),
    )(*x_parts, *g_parts, mixed, grads)


def times(left, right):
    return jnp.dot(left, right, preferred_element_type=F32)


def times_t(left, right):
    return lax.dot_general(left, right, (((1,), (1,)), ((), ())), preferred_element_type=F32)


def t_times(left, right):
    return lax.dot_general(left, right, (((0,), (0,)), ((), ())), preferred_element_type=F32)


def rms_scale(rows):
    return lax.rsqrt(jnp.mean(rows * rows, axis=-1, keepdims=True) + norm_eps)


def norm_back(rows, scale, inner):
    return scale * inner - rows * (scale * scale * scale) * jnp.mean(
        inner * rows, axis=-1, keepdims=True
    )


def from_ring(item, step):
    return lax.ppermute(item, RING, [(i, (i - step) % 4) for i in range(4)])


def to_ring(item, step):
    return lax.ppermute(item, RING, [(i, (i + step) % 4) for i in range(4)])


def swap(item, axis):
    return lax.ppermute(item, axis, SWAP)


STEPS = (0, 1, 3, 2)


def share_parts(item):
    one, three, two = (from_ring(item, step) for step in (1, 3, 2))
    own = swap(item, "c")
    near = swap(jnp.concatenate([one, three], axis=0), "c")
    far = swap(two, "c")
    return [item, one, three, two, own, near, far]


def pair_sum(far, near):
    return near + swap(far, "c").astype(F32)


def ring_sum(near):
    total = near[:CAP]
    sent = [
        to_ring(near[spot * CAP : (spot + 1) * CAP].astype(BF16), STEPS[spot]) for spot in (1, 2, 3)
    ]
    for item in sent:
        total = total + item.astype(F32)
    return total


def spread_columns(chunks, xl, c):
    mine = [jnp.where(c == 0, pair[0], pair[1]) for pair in chunks]
    away = [jnp.where(c == 0, pair[1], pair[0]) for pair in chunks]
    came = swap(jnp.concatenate(away, axis=0), "c")
    rows = mine[0].shape[0]
    both = []
    for k in range(2):
        other = came[k * rows : (k + 1) * rows]
        both.append(
            jnp.concatenate(
                [jnp.where(c == 0, mine[k], other), jnp.where(c == 0, other, mine[k])], axis=0
            )
        )
    kept = jnp.where(xl == 0, both[0], both[1])
    came = swap(jnp.where(xl == 0, both[1], both[0]), "xl")
    return jnp.stack([jnp.where(xl == 0, kept, came), jnp.where(xl == 0, came, kept)])


def return_columns(item, xh, xl, c, reduce):
    rows = item.shape[1] // 2
    mine = jnp.where(c == 0, item[:, :rows], item[:, rows:])
    came = swap(jnp.where(c == 0, item[:, rows:], item[:, :rows]), "c")
    both = reduce(jnp.where(c == 0, mine, came), jnp.where(c == 0, came, mine))
    here = jnp.where(xl == 0, both[0], both[1])
    there = jnp.where(xl == 0, both[1], both[0])
    parts = [here, to_ring(there, 1), to_ring(here, 2), to_ring(there, 3)]
    spot = 2 * xh + xl
    stacked = jnp.stack(parts)
    return [
        [
            lax.dynamic_index_in_dim(stacked, (spot - (2 * h + k)) % 4, 0, keepdims=False)
            for h in range(2)
        ]
        for k in range(2)
    ]


def gather_four(item, axis, spot, dim):
    parts = [item]
    for step in (1, 2, 3):
        parts.append(lax.ppermute(item, axis, [(i, (i - step) % 4) for i in range(4)]))
    return jnp.stack([pick(parts, (q - spot) % 4) for q in range(4)], axis=dim)


def pick(parts, which):
    out = parts[0]
    for k in range(1, len(parts)):
        out = jnp.where(which == k, parts[k], out)
    return out


def scatter_four(item, axis, spot, dim):
    total = lax.dynamic_index_in_dim(item, spot, dim, keepdims=False).astype(F32)
    for step in (1, 2, 3):
        sent = lax.dynamic_index_in_dim(item, (spot + step) % 4, dim, keepdims=False)
        total = total + lax.ppermute(sent, axis, [(i, (i + step) % 4) for i in range(4)]).astype(F32)
    return total


def row_pairs(step, back):
    pairs = []
    for h in range(2):
        for e in range(2):
            first = 2 * h + e
            one = (h * 4 + first) * 2 + e
            other = (h * 4 + (first + step) % 4) * 2 + e
            pairs.append((other, one) if back else (one, other))
    return pairs


def after(item, *others):
    return lax.optimization_barrier((item,) + others)[0]


def order_of_columns(xh):
    place = jnp.arange(768)
    core, owner, row = place // 384, (place % 384) // 48, place % 48
    origin = jnp.where(row < 44, 176 * owner + 88 * core + 44 * xh + row, -1)
    return (jnp.arange(1408)[:, None] == origin[None, :]).astype(BF16)


def column_part(item, width, xh):
    out = []
    for k in range(2):
        start = 2 * width * k
        out.append(
            jnp.where(
                xh == 0, item[:, start : start + width], item[:, start + width : start + 2 * width]
            )
        )
    return out


def on_device(
    tokens,
    doc_ids,
    first_gain,
    query_weight,
    key_weight,
    value_weight,
    out_weight,
    second_gain,
    gate_weight,
    up_weight,
    down_weight,
    cotangent,
):
    xh, xl, y, z, c = (lax.axis_index(name) for name in ("xh", "xl", "y", "z", "c"))
    first_col = first_gain.astype(F32)[:, None]
    second_col = second_gain.astype(F32)[:, None]

    def scaled(item, gain):
        return (item.astype(F32) * gain).astype(BF16)

    q_parts = column_part(scaled(query_weight, first_col), 512, xh)
    k_parts = column_part(scaled(key_weight, first_col), 64, xh)
    v_parts = column_part(scaled(value_weight, first_col), 64, xh)
    chunks = [
        [
            jnp.concatenate([q_parts[k][:, 256 * j : 256 * (j + 1)], k_parts[k], v_parts[k]], axis=1)
            for j in range(2)
        ]
        for k in range(2)
    ]
    spread = spread_columns(chunks, xl, c)
    qkv_full = gather_four(gather_four(spread, "z", z, 1), "y", y, 1).reshape(D, 384)

    source = 2 * xh + c
    came = swap(out_weight, "c")
    head = jnp.concatenate(
        [jnp.where(c == 0, out_weight, came), jnp.where(c == 0, came, out_weight)], axis=0
    )
    parts = [head]
    for step in (1, 2, 3):
        parts.append(lax.ppermute(head, ("xh", "y", "c"), row_pairs(step, False)))
    out_full = gather_four(pick(parts, (y - source) % 4), "z", z, 0).reshape(256, D)

    wide = jnp.stack([scaled(gate_weight, second_col), scaled(up_weight, second_col)])
    blocks = jnp.concatenate([wide[:, :, 1408 * k : 1408 * (k + 1)] for k in range(4)], axis=0)
    sorted_columns = times(blocks.reshape(256, 1408), order_of_columns(xh)).astype(BF16)
    sorted_columns = sorted_columns.reshape(2, 2, 2, 32, 768)
    chunks = [
        [
            jnp.concatenate(
                [
                    sorted_columns[k, h, item, :, 384 * j : 384 * (j + 1)]
                    for item in range(2)
                    for h in range(2)
                ],
                axis=1,
            )
            for j in range(2)
        ]
        for k in range(2)
    ]
    down_half = jnp.where(xh == 0, down_weight[:44], down_weight[44:])
    down_half = jnp.pad(down_half, ((0, 4), (0, 0)))
    corner = jnp.concatenate(
        [down_half[16 * k : 16 * (k + 1), 2 * WIDE :] for k in range(3)], axis=1
    )
    spread = spread_columns(chunks, xl, c).reshape(128, 2 * WIDE)
    packed = jnp.concatenate([spread, down_half[:, : 2 * WIDE], corner], axis=0)
    packed = lax.all_gather(packed, ("y", "z"), axis=0, tiled=True)

    table = rotary_table()
    rows = tokens.astype(F32)
    first_scale = rms_scale(rows)
    id_rows = jnp.pad(doc_ids.astype(BF16)[None], ((0, 15), (0, D - CAP)))
    normed = share_parts(jnp.concatenate([(rows * first_scale).astype(BF16), id_rows], axis=0))
    upstream = share_parts(after(cotangent, *normed[1:4]))
    queries, key_values, mixed, far, near = attend(normed, table, qkv_full, out_full)
    midway = rows + ring_sum(pair_sum(far, near))

    second_scale = rms_scale(midway)
    normed_two = share_parts((midway * second_scale).astype(BF16))
    hidden, grad_feed, far, near = feed_forward(normed_two, upstream, packed)
    inner_two = ring_sum(pair_sum(far, near))
    grad_mid = cotangent.astype(F32) + norm_back(midway, second_scale, inner_two)
    grad_attn = share_parts(grad_mid.astype(BF16))

    pack = feed_grads(normed_two, upstream, hidden, grad_feed)
    pack = lax.psum_scatter(pack, ("y", "z"), scatter_dimension=0, tiled=True)
    feed_part = pack[:128].reshape(2, 64, 2 * WIDE)
    corner = pack[176:]
    corner = jnp.concatenate([corner[:, 512 * k : 512 * (k + 1)] for k in range(3)], axis=0)
    down_part = jnp.concatenate([pack[128:176], corner], axis=1)

    blocks = packed.reshape(16, 192, 2 * WIDE)
    corner = jnp.concatenate(
        [blocks[:, 176:, 512 * k : 512 * (k + 1)] for k in range(3)], axis=1
    )
    down_full = jnp.concatenate([blocks[:, 128:176], corner], axis=2).reshape(WIDE, D)
    out_sum = pair_sum(times(hidden[512:], down_full).astype(BF16), times(hidden[:512], down_full))
    output = (midway + ring_sum(after(out_sum, *grad_attn[1:4]))).astype(BF16)

    grad_qkv, far, near = attend_back(
        grad_attn, normed, table, qkv_full, out_full, queries, key_values
    )
    inner_one = ring_sum(pair_sum(far, near))
    tokens_grad = grad_mid + norm_back(rows, first_scale, inner_one)
    qkv_term, out_term = small_grads(normed, grad_attn, mixed, grad_qkv)
    qkv_part = scatter_four(qkv_term.reshape(2, 4, 4, 64, 384), "y", y, 1).astype(BF16)
    qkv_part = scatter_four(qkv_part, "z", z, 1).astype(BF16)
    out_part = scatter_four(out_term.reshape(4, 64, D), "z", z, 0)

    def with_pair(zero, one):
        pair = zero[:, :, 256:].astype(F32) + one[:, :, 256:].astype(F32)
        return jnp.concatenate([zero[:, :, :256], one[:, :, :256], pair.astype(BF16)], axis=2)

    parts = return_columns(qkv_part, xh, xl, c, with_pair)

    def joined(start, end):
        return jnp.concatenate(
            [parts[k][h][:, start:end] for k in range(2) for h in range(2)], axis=1
        ).astype(F32)

    query_raw, key_raw, value_raw = joined(0, 512), joined(512, 576), joined(576, 640)
    first_grad = (
        jnp.sum(query_raw * query_weight.astype(F32), axis=1)
        + jnp.sum(key_raw * key_weight.astype(F32), axis=1)
        + jnp.sum(value_raw * value_weight.astype(F32), axis=1)
    )

    parts = return_columns(
        feed_part, xh, xl, c, lambda zero, one: jnp.concatenate([zero, one], axis=2)
    )
    shuffle = jnp.concatenate([order_of_columns(0), order_of_columns(1)], axis=1)
    rows_of = []
    for item in range(2):
        for k in range(2):
            for half in range(2):
                start = item * WIDE + half * 384
                rows_of.append(
                    jnp.concatenate(
                        [
                            parts[k][h][:, e * 2 * WIDE + start : e * 2 * WIDE + start + 384]
                            for h in range(2)
                            for e in range(2)
                        ],
                        axis=1,
                    )
                )
    unsorted = times_t(jnp.concatenate(rows_of, axis=0), shuffle).reshape(2, 4, 32, 1408)
    gate_raw = jnp.concatenate([unsorted[0, k] for k in range(4)], axis=1)
    up_raw = jnp.concatenate([unsorted[1, k] for k in range(4)], axis=1)
    second_grad = jnp.sum(gate_raw * gate_weight.astype(F32), axis=1) + jnp.sum(
        up_raw * up_weight.astype(F32), axis=1
    )

    came = swap(down_part, "xh")
    down_grad = jnp.concatenate(
        [jnp.where(xh == 0, down_part, came)[:44], jnp.where(xh == 0, came, down_part)[:44]], axis=0
    ).astype(F32)

    sent = out_part.astype(BF16)
    for step in (1, 2, 3):
        out_part = out_part + lax.ppermute(sent, ("xh", "y", "c"), row_pairs(step, True)).astype(F32)
    out_part = out_part.astype(BF16)
    low, high = out_part[:32], out_part[32:]
    came = swap(jnp.where(c == 0, high, low), "c")
    owned = jnp.where(y % 2 == c, jnp.where(c == 0, low, high), came)
    came = swap(owned, "xh")
    out_grad = jnp.where(y // 2 == xh, owned, came).astype(F32)

    return (
        output,
        tokens_grad,
        first_grad,
        query_raw * first_col,
        key_raw * first_col,
        value_raw * first_col,
        out_grad,
        second_grad,
        gate_raw * second_col,
        up_raw * second_col,
        down_grad,
    )


def solution(mesh):
    fine = Mesh(mesh.devices.reshape(2, 2, 4, 4, 2), ("xh", "xl", "y", "z", "c"))
    everyone = ("xh", "xl", "y", "z", "c")
    group = ("xl", "y", "z", "c")
    in_specs = (
        P(everyone, None),
        P(everyone),
        P(group),
        P(group, None),
        P(group, None),
        P(group, None),
        P(group, None),
        P(group),
        P(group, None),
        P(group, None),
        P(group, None),
        P(everyone, None),
    )
    out_specs = (
        P(everyone, None),
        P(everyone, None),
        P(group),
        P(group, None),
        P(group, None),
        P(group, None),
        P(group, None),
        P(group),
        P(group, None),
        P(group, None),
        P(group, None),
    )
    return jax.shard_map(
        on_device, mesh=fine, in_specs=in_specs, out_specs=out_specs, check_vma=False
    )
```

```python
import jax
import jax.numpy as jnp
import ml_dtypes
import numpy as np
from jax import lax
from jax.experimental import pallas as pl
from jax.experimental.pallas import tpu as pltpu
from jax.sharding import Mesh, PartitionSpec as P

D = 2048
HDIM = 64
CAP = 128
WIDE = 768
BF16 = jnp.bfloat16
F32 = jnp.float32

norm_eps = 1e-05

RING = ("xh", "xl")
SWAP = [(0, 1), (1, 0)]
STEPS = (0, 1, 3, 2)


def dot_nn(left, right):
    return lax.dot_general(left, right, (((1,), (0,)), ((), ())), preferred_element_type=F32)


def dot_nt(left, right):
    return lax.dot_general(left, right, (((1,), (1,)), ((), ())), preferred_element_type=F32)


def dot_tn(left, right):
    return lax.dot_general(left, right, (((0,), (0,)), ((), ())), preferred_element_type=F32)


HBM = pl.BlockSpec(memory_space=pltpu.HBM)


def block_copies(parts, whole, sems):
    return [
        pltpu.make_async_copy(
            part.at[pl.ds(0, CAP)], whole.at[pl.ds(CAP * spot, CAP)], sems.at[spot]
        )
        for spot, part in enumerate(parts)
    ]


def id_copies(parts, ids, sems):
    return [
        pltpu.make_async_copy(part.at[pl.ds(CAP, 16), pl.ds(0, CAP)], ids.at[spot], sems.at[spot])
        for spot, part in enumerate(parts)
    ]


def feed_copies(packed, feed, sems):
    copies = []
    for k in range(16):
        for h in range(2):
            copies.append(
                pltpu.make_async_copy(
                    packed.at[pl.ds(192 * k + 64 * h, 64)],
                    feed.at[pl.ds(1024 * h + 64 * k, 64)],
                    sems.at[2 * k + h],
                )
            )
    return copies


def down_copies(packed, down, sems):
    copies = []
    for k in range(16):
        copies.append(
            pltpu.make_async_copy(
                packed.at[pl.ds(192 * k + 128, 48)],
                down.at[pl.ds(48 * k, 48), pl.ds(0, 1536)],
                sems.at[4 * k],
            )
        )
        for h in range(3):
            copies.append(
                pltpu.make_async_copy(
                    packed.at[pl.ds(192 * k + 176, 16), pl.ds(512 * h, 512)],
                    down.at[pl.ds(48 * k + 16 * h, 16), pl.ds(1536, 512)],
                    sems.at[4 * k + 1 + h],
                )
            )
    return copies


def feed_kernel(*refs):
    x_parts, c_parts, packed = refs[:8], refs[8:16], refs[16]
    hidden, grads, far, near = refs[17:21]
    x, c, feed, down, x_sems, c_sems, f_sems, d_sems = refs[21:]
    step = pl.program_id(0)

    @pl.when(step == 0)
    def _():
        first = block_copies(x_parts, x, x_sems)
        second = feed_copies(packed, feed, f_sems)
        third = block_copies(c_parts, c, c_sems)
        fourth = down_copies(packed, down, d_sems)
        for group in (first, second, third, fourth):
            for copy in group:
                copy.start()
        for copy in first + second:
            copy.wait()

    rows = pl.ds(pl.multiple_of(((step + 2) % 4) * 256, 256), 256)
    block = x[rows, :]
    gate = dot_nn(block, feed[:, :WIDE])
    up = dot_nn(block, feed[:, WIDE:])

    @pl.when(step == 0)
    def _():
        third = block_copies(c_parts, c, c_sems)
        fourth = down_copies(packed, down, d_sems)
        for copy in third + fourth:
            copy.wait()

    back = dot_nt(c[rows, :], down[...])
    sig = jax.nn.sigmoid(gate)
    silu = gate * sig
    hidden[...] = (silu * up).astype(BF16)
    grad_gate = (back * up * (sig * (1.0 + gate * (1.0 - sig)))).astype(BF16)
    grad_up = (back * silu).astype(BF16)
    grads[:, :WIDE] = grad_gate
    grads[:, WIDE:] = grad_up
    inner = dot_nt(grads[...], feed[...])

    @pl.when(step < 2)
    def _():
        far[...] = inner.astype(BF16)

    @pl.when(step >= 2)
    def _():
        near[...] = inner


def feed_forward(x_parts, c_parts, packed):
    row = lambda i: ((i + 2) % 4, 0)
    return pl.pallas_call(
        feed_kernel,
        grid=(4,),
        in_specs=[HBM] * 17,
        out_specs=[
            pl.BlockSpec((256, WIDE), row),
            pl.BlockSpec((256, 2 * WIDE), row),
            pl.BlockSpec((256, D), lambda i: (jnp.minimum(i, 1), 0)),
            pl.BlockSpec((256, D), lambda i: (jnp.maximum(i - 2, 0), 0)),
        ],
        out_shape=[
            jax.ShapeDtypeStruct((1024, WIDE), BF16),
            jax.ShapeDtypeStruct((1024, 2 * WIDE), BF16),
            jax.ShapeDtypeStruct((512, D), BF16),
            jax.ShapeDtypeStruct((512, D), F32),
        ],
        scratch_shapes=[
            pltpu.VMEM((1024, D), BF16),
            pltpu.VMEM((1024, D), BF16),
            pltpu.VMEM((D, 2 * WIDE), BF16),
            pltpu.VMEM((WIDE, D), BF16),
            pltpu.SemaphoreType.DMA((8,)),
            pltpu.SemaphoreType.DMA((8,)),
            pltpu.SemaphoreType.DMA((32,)),
            pltpu.SemaphoreType.DMA((64,)),
        ],
        compiler_params=pltpu.CompilerParams(vmem_limit_bytes=60 * 1024 * 1024),
        cost_estimate=pl.CostEstimate(
            flops=2 * 1024 * D * WIDE * 5, bytes_accessed=28 * 2**20, transcendentals=1024 * WIDE
        ),
    )(*x_parts, *c_parts, packed)


def grads_kernel(*refs):
    x_parts, c_parts, hidden_hbm, grads_hbm = refs[:8], refs[8:16], refs[16], refs[17]
    out = refs[18]
    x, c, hidden, grads, pack, x_sems, c_sems, in_sems, sems = refs[19:]
    first = block_copies(x_parts, x, x_sems)
    second = block_copies(c_parts, c, c_sems)
    loads = [
        pltpu.make_async_copy(grads_hbm, grads, in_sems.at[0]),
        pltpu.make_async_copy(hidden_hbm, hidden, in_sems.at[1]),
    ]
    for copy in first + loads + second:
        copy.start()
    for copy in first + loads[:1]:
        copy.wait()
    stores = []

    def store(row, rows):
        copy = pltpu.make_async_copy(
            pack.at[pl.ds(row, rows)], out.at[pl.ds(row, rows)], sems.at[len(stores)]
        )
        copy.start()
        stores.append(copy)

    for k in range(8):
        tile = dot_tn(x[:, 256 * k : 256 * (k + 1)], grads[...]).astype(BF16)
        half, spot = k // 4, (k % 4) * 4
        for j in range(4):
            row = 192 * (spot + j) + 64 * half
            pack[row : row + 64, :] = tile[64 * j : 64 * (j + 1)]
            store(row, 64)
    for copy in second + loads[1:]:
        copy.wait()
    for k in range(2):
        tile = dot_tn(hidden[:, 384 * k : 384 * (k + 1)], c[...]).astype(BF16)
        for j in range(8):
            row = 192 * (8 * k + j) + 128
            piece = tile[48 * j : 48 * (j + 1)]
            pack[row : row + 48, :] = piece[:, :1536]
            for h in range(3):
                pack[row + 48 : row + 64, 512 * h : 512 * (h + 1)] = piece[
                    16 * h : 16 * (h + 1), 1536:
                ]
            store(row, 64)
    for copy in stores:
        copy.wait()


def feed_grads(x_parts, c_parts, hidden, grads):
    return pl.pallas_call(
        grads_kernel,
        in_specs=[HBM] * 18,
        out_specs=HBM,
        out_shape=jax.ShapeDtypeStruct((3072, 1536), BF16),
        scratch_shapes=[
            pltpu.VMEM((1024, D), BF16),
            pltpu.VMEM((1024, D), BF16),
            pltpu.VMEM((1024, WIDE), BF16),
            pltpu.VMEM((1024, 2 * WIDE), BF16),
            pltpu.VMEM((3072, 2 * WIDE), BF16),
            pltpu.SemaphoreType.DMA((8,)),
            pltpu.SemaphoreType.DMA((8,)),
            pltpu.SemaphoreType.DMA((2,)),
            pltpu.SemaphoreType.DMA((48,)),
        ],
        compiler_params=pltpu.CompilerParams(vmem_limit_bytes=60 * 1024 * 1024),
        cost_estimate=pl.CostEstimate(
            flops=2 * 1024 * D * WIDE * 3, bytes_accessed=22 * 2**20, transcendentals=0
        ),
    )(*x_parts, *c_parts, hidden, grads)


def output_kernel(hidden, packed, far, near, down, sems):
    copies = down_copies(packed, down, sems)
    for copy in copies:
        copy.start()
    for copy in copies:
        copy.wait()
    far[...] = dot_nn(hidden[512:], down[...]).astype(BF16)
    near[...] = dot_nn(hidden[:512], down[...])


def output_product(hidden, packed):
    whole = pl.BlockSpec(memory_space=pltpu.VMEM)
    return pl.pallas_call(
        output_kernel,
        in_specs=[whole, HBM],
        out_specs=[whole, whole],
        out_shape=[jax.ShapeDtypeStruct((512, D), BF16), jax.ShapeDtypeStruct((512, D), F32)],
        scratch_shapes=[pltpu.VMEM((WIDE, D), BF16), pltpu.SemaphoreType.DMA((64,))],
        compiler_params=pltpu.CompilerParams(vmem_limit_bytes=60 * 1024 * 1024),
        cost_estimate=pl.CostEstimate(
            flops=2 * 1024 * D * WIDE, bytes_accessed=11 * 2**20, transcendentals=0
        ),
    )(hidden, packed)


def rotary_table():
    place = np.arange(CAP, dtype=np.float32)[:, None]
    inverse = np.float32(10000.0) ** (np.arange(32, dtype=np.float32) * np.float32(-2.0 / HDIM))
    angle = (place * inverse).astype(np.float32)
    cosine, sine = np.cos(angle), np.sin(angle)
    zero, one = np.zeros((CAP, 64), np.float32), np.ones((CAP, 64), np.float32)
    straight = np.concatenate([cosine, cosine] * 5 + [one], axis=1)
    down = np.concatenate([-sine, zero[:, :32]] * 5 + [zero], axis=1)
    up = np.concatenate([zero[:, :32], sine] * 5 + [zero], axis=1)
    table = np.concatenate([straight, down, up], axis=1)
    high = table.astype(ml_dtypes.bfloat16)
    rest = (table - high.astype(np.float32)).astype(ml_dtypes.bfloat16)
    return jnp.asarray(np.stack([high, rest]))


def lane_of(shape, dim):
    return lax.broadcasted_iota(jnp.int32, shape, dim)


def block_tables(ids, table):
    row = jnp.broadcast_to(ids.astype(F32)[:1], (CAP, CAP))
    same = row == row.T
    to, frm = lane_of((CAP, CAP), 0), lane_of((CAP, CAP), 1)
    place = jnp.sum(jnp.where(same & (frm < to), 1.0, 0.0), axis=1, keepdims=True)
    chosen = (frm.astype(F32) == place).astype(BF16)
    factors = dot_nn(chosen, table[0]) + dot_nn(chosen, table[1])
    return same & (frm <= to), factors


def turned(item, factors, sign):
    other = (
        pltpu.roll(item, 352, 1) * factors[:, 384:768] + pltpu.roll(item, 32, 1) * factors[:, 768:]
    )
    return item * factors[:, :384] + sign * other


def stack_heads(item):
    head = lane_of((CAP, 256), 1) // 64
    return jnp.concatenate([jnp.where(head == h, item, 0).astype(BF16) for h in range(4)], axis=0)


def spreads():
    lane, own = lane_of((CAP, 256), 1) % 64, lane_of((CAP, 256), 0)
    return (lane == own).astype(BF16), (lane + 64 == own).astype(BF16)


def softmax_heads(queries, keys, allowed):
    scores = dot_nt(stack_heads(queries), keys) * 0.125
    out = []
    for h in range(4):
        part = jnp.where(allowed, scores[CAP * h : CAP * (h + 1)], -1e30)
        expo = jnp.exp(part - jnp.max(part, axis=1, keepdims=True))
        out.append(expo / jnp.sum(expo, axis=1, keepdims=True))
    return out


def attend_kernel(*refs):
    parts, table, w_hbm, o_hbm = refs[:8], refs[8], refs[9], refs[10]
    queries, key_values, mixed, far, near = refs[11:16]
    x, ids, w, o, x_sems, i_sems, w_sems = refs[16:]
    step = pl.program_id(0)

    @pl.when(step == 0)
    def _():
        copies = block_copies(parts, x, x_sems) + id_copies(parts, ids, i_sems)
        copies.append(pltpu.make_async_copy(w_hbm, w, w_sems.at[0]))
        copies.append(pltpu.make_async_copy(o_hbm, o, w_sems.at[1]))
        for copy in copies:
            copy.start()
        for copy in copies:
            copy.wait()

    half = 1 - step
    rows = pl.ds(pl.multiple_of(half * 512, 512), 512)
    qkv = dot_nn(x[rows, :], w[...])
    to_key, to_value = spreads()
    for k in range(4):
        allowed, factors = block_tables(ids[half * 4 + k], table)
        block = turned(qkv[CAP * k : CAP * (k + 1)], factors, 1.0).astype(BF16)
        here = slice(CAP * k, CAP * (k + 1))
        queries[here, :] = block[:, :256]
        key_values[here, :] = block[:, 256:]
        keys = dot_nn(block[:, 256:], to_key).astype(BF16)
        values = dot_nn(block[:, 256:], to_value).astype(BF16)
        probs = softmax_heads(block[:, :256], keys, allowed)
        probs = jnp.concatenate([item.astype(BF16) for item in probs], axis=1)
        mixed[here, :] = dot_nn(probs, stack_heads(values)).astype(BF16)
    total = dot_nn(mixed[...], o[...])

    @pl.when(step == 0)
    def _():
        far[...] = total.astype(BF16)

    @pl.when(step == 1)
    def _():
        near[...] = total


def attend(parts, table, qkv_full, out_full):
    row = lambda i: (1 - i, 0)
    still = lambda i: (0, 0)
    return pl.pallas_call(
        attend_kernel,
        grid=(2,),
        in_specs=[HBM] * 8 + [pl.BlockSpec((2, CAP, 1152), lambda i: (0, 0, 0))] + [HBM] * 2,
        out_specs=[
            pl.BlockSpec((512, 256), row),
            pl.BlockSpec((512, CAP), row),
            pl.BlockSpec((512, 256), row),
            pl.BlockSpec((512, D), still),
            pl.BlockSpec((512, D), still),
        ],
        out_shape=[
            jax.ShapeDtypeStruct((1024, 256), BF16),
            jax.ShapeDtypeStruct((1024, CAP), BF16),
            jax.ShapeDtypeStruct((1024, 256), BF16),
            jax.ShapeDtypeStruct((512, D), BF16),
            jax.ShapeDtypeStruct((512, D), F32),
        ],
        scratch_shapes=[
            pltpu.VMEM((1024, D), BF16),
            pltpu.VMEM((8, 16, CAP), BF16),
            pltpu.VMEM((D, 384), BF16),
            pltpu.VMEM((256, D), BF16),
            pltpu.SemaphoreType.DMA((8,)),
            pltpu.SemaphoreType.DMA((8,)),
            pltpu.SemaphoreType.DMA((2,)),
        ],
        compiler_params=pltpu.CompilerParams(vmem_limit_bytes=26 * 1024 * 1024),
        cost_estimate=pl.CostEstimate(
            flops=2 * 1024 * D * 640 * 2, bytes_accessed=15 * 2**20, transcendentals=2**19
        ),
    )(*parts, table, qkv_full, out_full)


def attend_back_kernel(*refs):
    parts, id_parts, table = refs[:8], refs[8:16], refs[16]
    w_hbm, o_hbm, queries, key_values = refs[17:21]
    grads, far, near = refs[21:24]
    g, ids, w, o, g_sems, i_sems, w_sems = refs[24:]
    step = pl.program_id(0)
    loads = [
        pltpu.make_async_copy(w_hbm, w, w_sems.at[0]),
        pltpu.make_async_copy(o_hbm, o, w_sems.at[1]),
    ]

    @pl.when(step == 0)
    def _():
        copies = block_copies(parts, g, g_sems) + id_copies(id_parts, ids, i_sems) + loads
        for copy in copies:
            copy.start()
        for copy in copies:
            copy.wait()

    half = 1 - step
    rows = pl.ds(pl.multiple_of(half * 512, 512), 512)
    grad_mixed = dot_nt(g[rows, :], o[...]).astype(BF16)
    to_key, to_value = spreads()
    for k in range(4):
        allowed, factors = block_tables(ids[half * 4 + k], table)
        here = slice(CAP * k, CAP * (k + 1))
        query, both = queries[here, :], key_values[here, :]
        keys = dot_nn(both, to_key).astype(BF16)
        values = dot_nn(both, to_value).astype(BF16)
        probs = softmax_heads(query, keys, allowed)
        grad_heads = stack_heads(grad_mixed[here])
        grad_probs = dot_nt(grad_heads, values)
        scores = []
        for h in range(4):
            part = grad_probs[CAP * h : CAP * (h + 1)]
            delta = jnp.sum(probs[h] * part, axis=1, keepdims=True)
            scores.append((probs[h] * (part - delta)).astype(BF16))
        grad_query = dot_nn(jnp.concatenate(scores, axis=1), stack_heads(keys)) * 0.125
        folded = dot_nt(stack_heads(query), to_key).astype(BF16)
        grad_folded = dot_nt(grad_heads, to_value).astype(BF16)
        low = jnp.concatenate([item.astype(BF16) for item in probs], axis=0)
        grad_both = dot_tn(jnp.concatenate(scores, axis=0), folded) * 0.125 + dot_tn(low, grad_folded)
        item = jnp.concatenate([grad_query, grad_both], axis=1)
        grads[here, :] = turned(item, factors, -1.0).astype(BF16)
    total = dot_nt(grads[...], w[...])

    @pl.when(step == 0)
    def _():
        far[...] = total.astype(BF16)

    @pl.when(step == 1)
    def _():
        near[...] = total


def attend_back(parts, id_parts, table, qkv_full, out_full, queries, key_values):
    row = lambda i: (1 - i, 0)
    return pl.pallas_call(
        attend_back_kernel,
        grid=(2,),
        in_specs=[HBM] * 16
        + [pl.BlockSpec((2, CAP, 1152), lambda i: (0, 0, 0))]
        + [HBM] * 2
        + [pl.BlockSpec((512, 256), row), pl.BlockSpec((512, CAP), row)],
        out_specs=[
            pl.BlockSpec((512, 384), row),
            pl.BlockSpec((512, D), lambda i: (0, 0)),
            pl.BlockSpec((512, D), lambda i: (0, 0)),
        ],
        out_shape=[
            jax.ShapeDtypeStruct((1024, 384), BF16),
            jax.ShapeDtypeStruct((512, D), BF16),
            jax.ShapeDtypeStruct((512, D), F32),
        ],
        scratch_shapes=[
            pltpu.VMEM((1024, D), BF16),
            pltpu.VMEM((8, 16, CAP), BF16),
            pltpu.VMEM((D, 384), BF16),
            pltpu.VMEM((256, D), BF16),
            pltpu.SemaphoreType.DMA((8,)),
            pltpu.SemaphoreType.DMA((8,)),
            pltpu.SemaphoreType.DMA((2,)),
        ],
        compiler_params=pltpu.CompilerParams(vmem_limit_bytes=28 * 1024 * 1024),
        cost_estimate=pl.CostEstimate(
            flops=2 * 1024 * D * 640 * 2, bytes_accessed=15 * 2**20, transcendentals=2**19
        ),
    )(*parts, *id_parts, table, qkv_full, out_full, queries, key_values)


def small_grads_kernel(*refs):
    x_parts, g_parts, mixed_hbm, grads_hbm = refs[:8], refs[8:16], refs[16], refs[17]
    pack, x, g, mixed, grads, x_sems, g_sems, in_sems = refs[18:]
    first = block_copies(x_parts, x, x_sems)
    second = block_copies(g_parts, g, g_sems)
    loads = [
        pltpu.make_async_copy(grads_hbm, grads, in_sems.at[0]),
        pltpu.make_async_copy(mixed_hbm, mixed, in_sems.at[1]),
    ]
    for copy in first + loads + second:
        copy.start()
    for copy in first + loads[:1]:
        copy.wait()
    for k in range(8):
        tile = dot_tn(x[:, 256 * k : 256 * (k + 1)], grads[...]).astype(BF16)
        row = 128 * (k % 4) + 64 * (k // 4)
        for j in range(4):
            pack[j, row : row + 64, :384] = tile[64 * j : 64 * (j + 1)]
    for copy in second + loads[1:]:
        copy.wait()
    for k in range(8):
        tile = dot_tn(mixed[...], g[:, 256 * k : 256 * (k + 1)]).astype(BF16)
        for j in range(4):
            pack[j, 64 * k : 64 * (k + 1), 384:] = tile[64 * j : 64 * (j + 1)]


def small_grads(x_parts, g_parts, mixed, grads):
    return pl.pallas_call(
        small_grads_kernel,
        in_specs=[HBM] * 18,
        out_specs=pl.BlockSpec(memory_space=pltpu.VMEM),
        out_shape=jax.ShapeDtypeStruct((4, 512, 640), BF16),
        scratch_shapes=[
            pltpu.VMEM((1024, D), BF16),
            pltpu.VMEM((1024, D), BF16),
            pltpu.VMEM((1024, 256), BF16),
            pltpu.VMEM((1024, 384), BF16),
            pltpu.SemaphoreType.DMA((8,)),
            pltpu.SemaphoreType.DMA((8,)),
            pltpu.SemaphoreType.DMA((2,)),
        ],
        compiler_params=pltpu.CompilerParams(vmem_limit_bytes=60 * 1024 * 1024),
        cost_estimate=pl.CostEstimate(
            flops=2 * 1024 * D * 640, bytes_accessed=12 * 2**20, transcendentals=0
        ),
    )(*x_parts, *g_parts, mixed, grads)


def times(left, right):
    return jnp.dot(left, right, preferred_element_type=F32)


def times_t(left, right):
    return lax.dot_general(left, right, (((1,), (1,)), ((), ())), preferred_element_type=F32)


def t_times(left, right):
    return lax.dot_general(left, right, (((0,), (0,)), ((), ())), preferred_element_type=F32)


def rms_scale(rows):
    return lax.rsqrt(jnp.mean(rows * rows, axis=-1, keepdims=True) + norm_eps)


def norm_back(rows, scale, inner):
    return scale * inner - rows * (scale * scale * scale) * jnp.mean(
        inner * rows, axis=-1, keepdims=True
    )


def from_ring(item, step):
    return lax.ppermute(item, RING, [(i, (i - step) % 4) for i in range(4)])


def to_ring(item, step):
    return lax.ppermute(item, RING, [(i, (i + step) % 4) for i in range(4)])


def swap(item, axis):
    return lax.ppermute(item, axis, SWAP)


def share_parts(item, *first):
    own = swap(item, "c")
    ring = after(tuple(from_ring(item, step) for step in STEPS[1:]), *first)
    return [item, *ring, own] + [swap(part, "c") for part in ring]


def pair_blocks(near, far, *first):
    far = after(swap(far, "c"), *first)

    def block(spot):
        here = slice(spot * CAP, (spot + 1) * CAP)
        return near[here] + far[here].astype(F32)

    return (block(0),) + tuple(block(spot).astype(BF16) for spot in (1, 2, 3))


def ring_sum(blocks, *first):
    came = tuple(to_ring(blocks[spot], STEPS[spot]) for spot in (1, 2, 3))
    return blocks[0] + sum(item.astype(F32) for item in after(came, *first))


def spread_columns(chunks, xl, c):
    mine = [jnp.where(c == 0, pair[0], pair[1]) for pair in chunks]
    away = [jnp.where(c == 0, pair[1], pair[0]) for pair in chunks]
    came = swap(jnp.concatenate(away, axis=0), "c")
    rows = mine[0].shape[0]
    both = []
    for k in range(2):
        other = came[k * rows : (k + 1) * rows]
        both.append(
            jnp.concatenate(
                [jnp.where(c == 0, mine[k], other), jnp.where(c == 0, other, mine[k])], axis=0
            )
        )
    kept = jnp.where(xl == 0, both[0], both[1])
    came = swap(jnp.where(xl == 0, both[1], both[0]), "xl")
    return jnp.stack([jnp.where(xl == 0, kept, came), jnp.where(xl == 0, came, kept)])


def gather_four(item, axis, spot, dim):
    parts = [item]
    for step in (1, 2, 3):
        parts.append(lax.ppermute(item, axis, [(i, (i - step) % 4) for i in range(4)]))
    return jnp.stack([pick(parts, (q - spot) % 4) for q in range(4)], axis=dim)


def pick(parts, which):
    out = parts[0]
    for k in range(1, len(parts)):
        out = jnp.where(which == k, parts[k], out)
    return out


def four_pieces(item, spot, dim):
    return [
        lax.dynamic_index_in_dim(item, (spot + step) % 4, dim, keepdims=False) for step in range(4)
    ]


def exchange(pieces, axis):
    return tuple(
        lax.ppermute(pieces[step], axis, [(i, (i + step) % 4) for i in range(4)])
        for step in (1, 2, 3)
    )


def four_sum(pieces, came):
    return pieces[0].astype(F32) + sum(item.astype(F32) for item in came)


def row_pairs(step, back):
    pairs = []
    for h in range(2):
        for e in range(2):
            first = 2 * h + e
            one = (h * 4 + first) * 2 + e
            other = (h * 4 + (first + step) % 4) * 2 + e
            pairs.append((other, one) if back else (one, other))
    return pairs


def after(item, *others):
    return lax.optimization_barrier((item,) + others)[0] if others else item


def order_of_columns(xh):
    place = jnp.arange(768)
    core, owner, row = place // 384, (place % 384) // 48, place % 48
    origin = jnp.where(row < 44, 176 * owner + 88 * core + 44 * xh + row, -1)
    return (jnp.arange(1408)[:, None] == origin[None, :]).astype(BF16)


def column_part(item, width, xh):
    out = []
    for k in range(2):
        start = 2 * width * k
        out.append(
            jnp.where(
                xh == 0, item[:, start : start + width], item[:, start + width : start + 2 * width]
            )
        )
    return out


def on_device(
    tokens,
    doc_ids,
    first_gain,
    query_weight,
    key_weight,
    value_weight,
    out_weight,
    second_gain,
    gate_weight,
    up_weight,
    down_weight,
    cotangent,
):
    xh, xl, y, z, c = (lax.axis_index(name) for name in ("xh", "xl", "y", "z", "c"))
    first_col = first_gain.astype(F32)[:, None]
    second_col = second_gain.astype(F32)[:, None]

    def scaled(item, gain):
        return (item.astype(F32) * gain).astype(BF16)

    q_parts = column_part(scaled(query_weight, first_col), 512, xh)
    k_parts = column_part(scaled(key_weight, first_col), 64, xh)
    v_parts = column_part(scaled(value_weight, first_col), 64, xh)
    chunks = [
        [
            jnp.concatenate([q_parts[k][:, 256 * j : 256 * (j + 1)], k_parts[k], v_parts[k]], axis=1)
            for j in range(2)
        ]
        for k in range(2)
    ]
    spread = spread_columns(chunks, xl, c)

    source = 2 * xh + c
    came = swap(out_weight, "c")
    head = jnp.concatenate(
        [jnp.where(c == 0, out_weight, came), jnp.where(c == 0, came, out_weight)], axis=0
    )
    lines = [head]
    for step in (1, 2, 3):
        lines.append(lax.ppermute(head, ("xh", "y", "c"), row_pairs(step, False)))
    head = pick(lines, (y - source) % 4)
    out_full = gather_four(head, "z", z, 0).reshape(256, D)
    qkv_full = lax.all_gather(spread, ("y", "z"), axis=1, tiled=True).reshape(D, 384)

    wide = jnp.stack([scaled(gate_weight, second_col), scaled(up_weight, second_col)])
    blocks = jnp.concatenate([wide[:, :, 1408 * k : 1408 * (k + 1)] for k in range(4)], axis=0)
    sorted_columns = times(blocks.reshape(256, 1408), order_of_columns(xh)).astype(BF16)
    sorted_columns = sorted_columns.reshape(2, 2, 2, 32, 768)
    chunks = [
        [
            jnp.concatenate(
                [
                    sorted_columns[k, h, item, :, 384 * j : 384 * (j + 1)]
                    for item in range(2)
                    for h in range(2)
                ],
                axis=1,
            )
            for j in range(2)
        ]
        for k in range(2)
    ]
    down_half = jnp.where(xh == 0, down_weight[:44], down_weight[44:])
    down_half = jnp.pad(down_half, ((0, 4), (0, 0)))
    corner = jnp.concatenate(
        [down_half[16 * k : 16 * (k + 1), 2 * WIDE :] for k in range(3)], axis=1
    )
    feed_spread = spread_columns(chunks, xl, c).reshape(128, 2 * WIDE)
    packed = jnp.concatenate([feed_spread, down_half[:, : 2 * WIDE], corner], axis=0)

    table = rotary_table()
    rows = tokens.astype(F32)
    first_scale = rms_scale(rows)
    id_rows = jnp.pad(doc_ids.astype(BF16)[None], ((0, 15), (0, D - CAP)))
    payload = jnp.concatenate([(rows * first_scale).astype(BF16), id_rows], axis=0)
    first = share_parts(after(payload, spread, feed_spread))
    packed = after(packed, qkv_full, out_full, *first[1:4])
    packed = lax.all_gather(packed, ("y", "z"), axis=0, tiled=True)

    queries, key_values, mixed, far, near = attend(first, table, qkv_full, out_full)
    shuffle = jnp.concatenate([order_of_columns(0), order_of_columns(1)], axis=1)
    upstream = share_parts(after(cotangent, *first[1:4]), mixed)
    far = after(far, upstream[1])
    midway = rows + ring_sum(pair_blocks(near, far), shuffle)

    second_scale = rms_scale(midway)
    second = share_parts((midway * second_scale).astype(BF16))
    hidden, grad_feed, far, near = feed_forward(second, upstream, packed)
    blocks = pair_blocks(near, far)
    pack = feed_grads(second, upstream, after(hidden, *blocks), grad_feed)
    inner_two = ring_sum(blocks, pack)
    grad_mid = cotangent.astype(F32) + norm_back(midway, second_scale, inner_two)
    out_far, out_near = output_product(after(hidden, pack), packed)
    third = share_parts(grad_mid.astype(BF16), out_far)
    pack = lax.psum_scatter(after(pack, inner_two), ("y", "z"), scatter_dimension=0, tiled=True)

    out_blocks = pair_blocks(out_near, out_far)
    grad_qkv, far, near = attend_back(
        third, first, table, qkv_full, out_full, after(queries, *out_blocks), key_values
    )
    product = ring_sum(out_blocks, grad_qkv)
    output = (midway + product).astype(BF16)

    terms = small_grads(first, third, mixed, grad_qkv)
    blocks = pair_blocks(near, after(far, product), terms)
    sent = four_pieces(after(terms, *blocks), z, 0)
    came = exchange(sent, "z")
    ring_came = (to_ring(blocks[1], STEPS[1]), to_ring(blocks[2], STEPS[2]))
    came, ring_came = lax.optimization_barrier((came, ring_came))
    terms = four_sum(sent, came).astype(BF16)
    head = jnp.concatenate(
        [
            jnp.concatenate([terms[64 * k : 64 * (k + 1), 384:] for k in range(h, h + 4)], axis=1)
            for h in (0, 4)
        ],
        axis=0,
    )
    lines = terms[:, :384].reshape(4, 128, 384)
    sent = [jnp.concatenate([item, head], axis=1) for item in four_pieces(lines, y, 0)]
    came = exchange(sent, "y")
    last_came = to_ring(after(blocks[3], *ring_came), STEPS[3])
    corner = jnp.concatenate([pack[176:, 512 * k : 512 * (k + 1)] for k in range(3)], axis=0)
    down_part = jnp.concatenate([pack[128:176], corner], axis=1)
    down_other = swap(after(down_part, *ring_came), "xh")
    came, last_came, down_other = lax.optimization_barrier((came, last_came, down_other))
    total = four_sum(sent, came).astype(BF16)
    qkv_part = total[:, :384].reshape(2, 64, 384)
    out_part = jnp.concatenate([total[:64, 384:], total[64:, 384:]], axis=1)
    inner_one = blocks[0] + sum(item.astype(F32) for item in ring_came + (last_came,))
    tokens_grad = grad_mid + norm_back(rows, first_scale, inner_one)
    down_grad = jnp.concatenate(
        [
            jnp.where(xh == 0, down_part, down_other)[:44],
            jnp.where(xh == 0, down_other, down_part)[:44],
        ],
        axis=0,
    ).astype(F32)

    wide = jnp.concatenate([pack[:128].reshape(2, 64, 2 * WIDE), qkv_part], axis=2)
    low, high = wide[:, :32], wide[:, 32:]
    away = jnp.where(c == 0, out_part[32:], out_part[:32])
    sent = jnp.concatenate(
        [
            jnp.where(c == 0, high, low).reshape(64, 1920),
            jnp.concatenate([away[:, :1024], away[:, 1024:]], axis=0),
        ],
        axis=1,
    )
    came = swap(sent, "c")
    mine, other = jnp.where(c == 0, low, high), came[:, :1920].reshape(2, 32, 1920)
    zero, one = jnp.where(c == 0, mine, other), jnp.where(c == 0, other, mine)
    pair = zero[:, :, 1792:].astype(F32) + one[:, :, 1792:].astype(F32)
    both = jnp.concatenate(
        [
            zero[:, :, :1536],
            one[:, :, :1536],
            zero[:, :, 1536:1792],
            one[:, :, 1536:1792],
            pair.astype(BF16),
        ],
        axis=2,
    )
    out_half = jnp.where(
        y % 2 == c,
        jnp.where(c == 0, out_part[:32], out_part[32:]),
        jnp.concatenate([came[:32, 1920:], came[32:, 1920:]], axis=1),
    )
    here = jnp.where(xl == 0, both[0], both[1])
    there = jnp.where(xl == 0, both[1], both[0])
    across = to_ring(jnp.concatenate([here, out_half], axis=1), 2)
    came = after((to_ring(there, 1), across, to_ring(there, 3)))
    stacked = [here, came[0], came[1][:, :3712], came[2]]
    spot = 2 * xh + xl
    parts = [[pick(stacked, (spot - (2 * h + k)) % 4) for h in range(2)] for k in range(2)]
    out_grad = jnp.where(y // 2 == xh, out_half, came[1][:, 3712:]).astype(F32)

    def joined(start, end):
        return jnp.concatenate(
            [parts[k][h][:, start:end] for k in range(2) for h in range(2)], axis=1
        ).astype(F32)

    query_raw, key_raw, value_raw = joined(3072, 3584), joined(3584, 3648), joined(3648, 3712)
    first_grad = (
        jnp.sum(query_raw * query_weight.astype(F32), axis=1)
        + jnp.sum(key_raw * key_weight.astype(F32), axis=1)
        + jnp.sum(value_raw * value_weight.astype(F32), axis=1)
    )

    rows_of = []
    for item in range(2):
        for k in range(2):
            for half in range(2):
                start = item * WIDE + half * 384
                rows_of.append(
                    jnp.concatenate(
                        [
                            parts[k][h][:, e * 2 * WIDE + start : e * 2 * WIDE + start + 384]
                            for h in range(2)
                            for e in range(2)
                        ],
                        axis=1,
                    )
                )
    unsorted = times_t(jnp.concatenate(rows_of, axis=0), shuffle).reshape(2, 4, 32, 1408)
    gate_raw = jnp.concatenate([unsorted[0, k] for k in range(4)], axis=1)
    up_raw = jnp.concatenate([unsorted[1, k] for k in range(4)], axis=1)
    second_grad = jnp.sum(gate_raw * gate_weight.astype(F32), axis=1) + jnp.sum(
        up_raw * up_weight.astype(F32), axis=1
    )

    return (
        output,
        tokens_grad,
        first_grad,
        query_raw * first_col,
        key_raw * first_col,
        value_raw * first_col,
        out_grad,
        second_grad,
        gate_raw * second_col,
        up_raw * second_col,
        down_grad,
    )


def solution(mesh):
    fine = Mesh(mesh.devices.reshape(2, 2, 4, 4, 2), ("xh", "xl", "y", "z", "c"))
    everyone = ("xh", "xl", "y", "z", "c")
    group = ("xl", "y", "z", "c")
    in_specs = (
        P(everyone, None),
        P(everyone),
        P(group),
        P(group, None),
        P(group, None),
        P(group, None),
        P(group, None),
        P(group),
        P(group, None),
        P(group, None),
        P(group, None),
        P(everyone, None),
    )
    out_specs = (
        P(everyone, None),
        P(everyone, None),
        P(group),
        P(group, None),
        P(group, None),
        P(group, None),
        P(group, None),
        P(group),
        P(group, None),
        P(group, None),
        P(group, None),
    )
    return jax.shard_map(
        on_device, mesh=fine, in_specs=in_specs, out_specs=out_specs, check_vma=False
    )
```

```python
import jax
import jax.numpy as jnp
import ml_dtypes
import numpy as np
from jax import lax
from jax.experimental import pallas as pl
from jax.experimental.pallas import tpu as pltpu
from jax.sharding import Mesh, PartitionSpec as P

D = 2048
HDIM = 64
CAP = 128
WIDE = 768
BF16 = jnp.bfloat16
F32 = jnp.float32

norm_eps = 1e-05

RING = ("xh", "xl")
SWAP = [(0, 1), (1, 0)]
STEPS = (0, 1, 3, 2)


def dot_nn(left, right):
    return lax.dot_general(left, right, (((1,), (0,)), ((), ())), preferred_element_type=F32)


def dot_nt(left, right):
    return lax.dot_general(left, right, (((1,), (1,)), ((), ())), preferred_element_type=F32)


def dot_tn(left, right):
    return lax.dot_general(left, right, (((0,), (0,)), ((), ())), preferred_element_type=F32)


HBM = pl.BlockSpec(memory_space=pltpu.HBM)


def in_hbm(*items):
    return [pltpu.with_memory_space_constraint(item, pltpu.HBM) for item in items]


def block_copies(parts, whole, sems):
    return [
        pltpu.make_async_copy(
            part.at[pl.ds(0, CAP)], whole.at[pl.ds(CAP * spot, CAP)], sems.at[spot]
        )
        for spot, part in enumerate(parts)
    ]


def id_copies(parts, ids, sems):
    return [
        pltpu.make_async_copy(part.at[pl.ds(CAP, 16), pl.ds(0, CAP)], ids.at[spot], sems.at[spot])
        for spot, part in enumerate(parts)
    ]


def feed_copies(packed, feed, sems):
    copies = []
    for k in range(16):
        for h in range(2):
            copies.append(
                pltpu.make_async_copy(
                    packed.at[pl.ds(192 * k + 64 * h, 64)],
                    feed.at[pl.ds(1024 * h + 64 * k, 64)],
                    sems.at[2 * k + h],
                )
            )
    return copies


def down_copies(packed, down, sems):
    copies = []
    for k in range(16):
        copies.append(
            pltpu.make_async_copy(
                packed.at[pl.ds(192 * k + 128, 48)],
                down.at[pl.ds(48 * k, 48), pl.ds(0, 1536)],
                sems.at[4 * k],
            )
        )
        for h in range(3):
            copies.append(
                pltpu.make_async_copy(
                    packed.at[pl.ds(192 * k + 176, 16), pl.ds(512 * h, 512)],
                    down.at[pl.ds(48 * k + 16 * h, 16), pl.ds(1536, 512)],
                    sems.at[4 * k + 1 + h],
                )
            )
    return copies


def feed_kernel(*refs):
    x_parts, c_parts, packed = refs[:8], refs[8:16], refs[16]
    hidden, grads, far, near = refs[17:21]
    x, c, feed, down, x_sems, c_sems, f_sems, d_sems = refs[21:]
    step = pl.program_id(0)

    first, third = block_copies(x_parts, x, x_sems), block_copies(c_parts, c, c_sems)

    @pl.when(step == 0)
    def _():
        second, fourth = feed_copies(packed, feed, f_sems), down_copies(packed, down, d_sems)
        for group in (first[4:6], second, third[4:6], fourth, first[6:], third[6:], first[:4], third[:4]):
            for copy in group:
                copy.start()
        for copy in first[4:6] + second:
            copy.wait()

    for k in range(1, 4):

        @pl.when(step == k)
        def _(k=k):
            spot = (2 * k + 4) % 8
            for copy in first[spot : spot + 2] + third[spot : spot + 2]:
                copy.wait()

    rows = pl.ds(pl.multiple_of(((step + 2) % 4) * 256, 256), 256)
    block = x[rows, :]
    gate = dot_nn(block, feed[:, :WIDE])
    up = dot_nn(block, feed[:, WIDE:])

    @pl.when(step == 0)
    def _():
        for copy in third[4:6] + down_copies(packed, down, d_sems):
            copy.wait()

    back = dot_nt(c[rows, :], down[...])
    sig = jax.nn.sigmoid(gate)
    silu = gate * sig
    hidden[...] = (silu * up).astype(BF16)
    grad_gate = (back * up * (sig * (1.0 + gate * (1.0 - sig)))).astype(BF16)
    grad_up = (back * silu).astype(BF16)
    grads[:, :WIDE] = grad_gate
    grads[:, WIDE:] = grad_up
    inner = dot_nt(grads[...], feed[...])

    @pl.when(step < 2)
    def _():
        far[...] = inner.astype(BF16)

    @pl.when(step >= 2)
    def _():
        near[...] = inner.astype(BF16)


def feed_forward(x_parts, c_parts, packed):
    row = lambda i: ((i + 2) % 4, 0)
    return pl.pallas_call(
        feed_kernel,
        grid=(4,),
        in_specs=[HBM] * 17,
        out_specs=[
            pl.BlockSpec((256, WIDE), row),
            pl.BlockSpec((256, 2 * WIDE), row),
            pl.BlockSpec((256, D), lambda i: (jnp.minimum(i, 1), 0)),
            pl.BlockSpec((256, D), lambda i: (jnp.maximum(i - 2, 0), 0)),
        ],
        out_shape=[
            jax.ShapeDtypeStruct((1024, WIDE), BF16),
            jax.ShapeDtypeStruct((1024, 2 * WIDE), BF16),
            jax.ShapeDtypeStruct((512, D), BF16),
            jax.ShapeDtypeStruct((512, D), BF16),
        ],
        scratch_shapes=[
            pltpu.VMEM((1024, D), BF16),
            pltpu.VMEM((1024, D), BF16),
            pltpu.VMEM((D, 2 * WIDE), BF16),
            pltpu.VMEM((WIDE, D), BF16),
            pltpu.SemaphoreType.DMA((8,)),
            pltpu.SemaphoreType.DMA((8,)),
            pltpu.SemaphoreType.DMA((32,)),
            pltpu.SemaphoreType.DMA((64,)),
        ],
        compiler_params=pltpu.CompilerParams(vmem_limit_bytes=40 * 1024 * 1024),
        cost_estimate=pl.CostEstimate(
            flops=2 * 1024 * D * WIDE * 5, bytes_accessed=28 * 2**20, transcendentals=1024 * WIDE
        ),
    )(*in_hbm(*x_parts, *c_parts, packed))


def grads_kernel(*refs):
    x_parts, c_parts, hidden_hbm, grads_hbm = refs[:8], refs[8:16], refs[16], refs[17]
    out = refs[18]
    x, c, hidden, grads, pack, x_sems, c_sems, in_sems, sems = refs[19:]
    first = block_copies(x_parts, x, x_sems)
    second = block_copies(c_parts, c, c_sems)
    loads = [
        pltpu.make_async_copy(grads_hbm, grads, in_sems.at[0]),
        pltpu.make_async_copy(hidden_hbm, hidden, in_sems.at[1]),
    ]
    for copy in first + loads + second:
        copy.start()
    for copy in first + loads[:1]:
        copy.wait()
    stores = []

    def store(row, rows):
        copy = pltpu.make_async_copy(
            pack.at[pl.ds(row, rows)], out.at[pl.ds(row, rows)], sems.at[len(stores)]
        )
        copy.start()
        stores.append(copy)

    for k in range(8):
        tile = dot_tn(x[:, 256 * k : 256 * (k + 1)], grads[...]).astype(BF16)
        half, spot = k // 4, (k % 4) * 4
        for j in range(4):
            row = 192 * (spot + j) + 64 * half
            pack[row : row + 64, :] = tile[64 * j : 64 * (j + 1)]
            store(row, 64)
    for copy in second + loads[1:]:
        copy.wait()
    for k in range(2):
        tile = dot_tn(hidden[:, 384 * k : 384 * (k + 1)], c[...]).astype(BF16)
        for j in range(8):
            row = 192 * (8 * k + j) + 128
            piece = tile[48 * j : 48 * (j + 1)]
            pack[row : row + 48, :] = piece[:, :1536]
            for h in range(3):
                pack[row + 48 : row + 64, 512 * h : 512 * (h + 1)] = piece[
                    16 * h : 16 * (h + 1), 1536:
                ]
            store(row, 64)
    for copy in stores:
        copy.wait()


def feed_grads(x_parts, c_parts, hidden, grads):
    return pl.pallas_call(
        grads_kernel,
        in_specs=[HBM] * 18,
        out_specs=HBM,
        out_shape=jax.ShapeDtypeStruct((3072, 1536), BF16),
        scratch_shapes=[
            pltpu.VMEM((1024, D), BF16),
            pltpu.VMEM((1024, D), BF16),
            pltpu.VMEM((1024, WIDE), BF16),
            pltpu.VMEM((1024, 2 * WIDE), BF16),
            pltpu.VMEM((3072, 2 * WIDE), BF16),
            pltpu.SemaphoreType.DMA((8,)),
            pltpu.SemaphoreType.DMA((8,)),
            pltpu.SemaphoreType.DMA((2,)),
            pltpu.SemaphoreType.DMA((48,)),
        ],
        compiler_params=pltpu.CompilerParams(vmem_limit_bytes=60 * 1024 * 1024),
        cost_estimate=pl.CostEstimate(
            flops=2 * 1024 * D * WIDE * 3, bytes_accessed=22 * 2**20, transcendentals=0
        ),
    )(*in_hbm(*x_parts, *c_parts, hidden, grads))


def output_kernel(hidden, packed, far, near, down, sems):
    copies = down_copies(packed, down, sems)
    for copy in copies:
        copy.start()
    for copy in copies:
        copy.wait()
    far[...] = dot_nn(hidden[512:], down[...]).astype(BF16)
    near[...] = dot_nn(hidden[:512], down[...]).astype(BF16)


def output_product(hidden, packed):
    whole = pl.BlockSpec(memory_space=pltpu.VMEM)
    return pl.pallas_call(
        output_kernel,
        in_specs=[whole, HBM],
        out_specs=[whole, whole],
        out_shape=[jax.ShapeDtypeStruct((512, D), BF16), jax.ShapeDtypeStruct((512, D), BF16)],
        scratch_shapes=[pltpu.VMEM((WIDE, D), BF16), pltpu.SemaphoreType.DMA((64,))],
        compiler_params=pltpu.CompilerParams(vmem_limit_bytes=24 * 1024 * 1024),
        cost_estimate=pl.CostEstimate(
            flops=2 * 1024 * D * WIDE, bytes_accessed=11 * 2**20, transcendentals=0
        ),
    )(hidden, *in_hbm(packed))


def rotary_table():
    place = np.arange(CAP, dtype=np.float32)[:, None]
    inverse = np.float32(10000.0) ** (np.arange(32, dtype=np.float32) * np.float32(-2.0 / HDIM))
    angle = (place * inverse).astype(np.float32)
    cosine, sine = np.cos(angle), np.sin(angle)
    zero, one = np.zeros((CAP, 64), np.float32), np.ones((CAP, 64), np.float32)
    straight = np.concatenate([cosine, cosine] * 5 + [one], axis=1)
    down = np.concatenate([-sine, zero[:, :32]] * 5 + [zero], axis=1)
    up = np.concatenate([zero[:, :32], sine] * 5 + [zero], axis=1)
    table = np.concatenate([straight, down, up], axis=1)
    high = table.astype(ml_dtypes.bfloat16)
    rest = (table - high.astype(np.float32)).astype(ml_dtypes.bfloat16)
    return jnp.asarray(np.stack([high, rest]))


def lane_of(shape, dim):
    return lax.broadcasted_iota(jnp.int32, shape, dim)


def block_tables(ids, table):
    row = jnp.broadcast_to(ids.astype(F32)[:1], (CAP, CAP))
    same = row == row.T
    to, frm = lane_of((CAP, CAP), 0), lane_of((CAP, CAP), 1)
    place = jnp.sum(jnp.where(same & (frm < to), 1.0, 0.0), axis=1, keepdims=True)
    chosen = (frm.astype(F32) == place).astype(BF16)
    factors = dot_nn(chosen, table[0]) + dot_nn(chosen, table[1])
    return same & (frm <= to), factors


def turned(item, factors, sign):
    other = (
        pltpu.roll(item, 352, 1) * factors[:, 384:768] + pltpu.roll(item, 32, 1) * factors[:, 768:]
    )
    return item * factors[:, :384] + sign * other


def stack_heads(item):
    head = lane_of((CAP, 256), 1) // 64
    return jnp.concatenate([jnp.where(head == h, item, 0).astype(BF16) for h in range(4)], axis=0)


def spreads():
    lane, own = lane_of((CAP, 256), 1) % 64, lane_of((CAP, 256), 0)
    return (lane == own).astype(BF16), (lane + 64 == own).astype(BF16)


def softmax_heads(queries, keys, allowed):
    scores = dot_nt(stack_heads(queries), keys) * 0.125
    out = []
    for h in range(4):
        part = jnp.where(allowed, scores[CAP * h : CAP * (h + 1)], -1e30)
        expo = jnp.exp(part - jnp.max(part, axis=1, keepdims=True))
        out.append(expo / jnp.sum(expo, axis=1, keepdims=True))
    return out


def attend_kernel(*refs):
    parts, table, w_hbm, o_hbm = refs[:8], refs[8], refs[9], refs[10]
    queries, key_values, mixed, far, near = refs[11:16]
    x, ids, w, o, x_sems, i_sems, w_sems = refs[16:]
    step = pl.program_id(0)
    blocks, numbers = block_copies(parts, x, x_sems), id_copies(parts, ids, i_sems)
    loads = [
        pltpu.make_async_copy(w_hbm, w, w_sems.at[0]),
        pltpu.make_async_copy(o_hbm, o, w_sems.at[1]),
    ]

    @pl.when(step == 0)
    def _():
        for copy in loads[:1] + blocks[4:] + numbers[4:] + loads[1:] + blocks[:4] + numbers[:4]:
            copy.start()
        for copy in loads[:1] + blocks[4:] + numbers[4:]:
            copy.wait()

    @pl.when(step == 1)
    def _():
        for copy in blocks[:4] + numbers[:4]:
            copy.wait()

    half = 1 - step
    rows = pl.ds(pl.multiple_of(half * 512, 512), 512)
    qkv = dot_nn(x[rows, :], w[...])
    to_key, to_value = spreads()
    for k in range(4):
        allowed, factors = block_tables(ids[half * 4 + k], table)
        block = turned(qkv[CAP * k : CAP * (k + 1)], factors, 1.0).astype(BF16)
        here = slice(CAP * k, CAP * (k + 1))
        queries[here, :] = block[:, :256]
        key_values[here, :] = block[:, 256:]
        keys = dot_nn(block[:, 256:], to_key).astype(BF16)
        values = dot_nn(block[:, 256:], to_value).astype(BF16)
        probs = softmax_heads(block[:, :256], keys, allowed)
        probs = jnp.concatenate([item.astype(BF16) for item in probs], axis=1)
        mixed[here, :] = dot_nn(probs, stack_heads(values)).astype(BF16)

    @pl.when(step == 0)
    def _():
        loads[1].wait()

    total = dot_nn(mixed[...], o[...])

    @pl.when(step == 0)
    def _():
        far[...] = total.astype(BF16)

    @pl.when(step == 1)
    def _():
        near[...] = total.astype(BF16)


def attend(parts, table, qkv_full, out_full):
    row = lambda i: (1 - i, 0)
    still = lambda i: (0, 0)
    return pl.pallas_call(
        attend_kernel,
        grid=(2,),
        in_specs=[HBM] * 8 + [pl.BlockSpec((2, CAP, 1152), lambda i: (0, 0, 0))] + [HBM] * 2,
        out_specs=[
            pl.BlockSpec((512, 256), row),
            pl.BlockSpec((512, CAP), row),
            pl.BlockSpec((512, 256), row),
            pl.BlockSpec((512, D), still),
            pl.BlockSpec((512, D), still),
        ],
        out_shape=[
            jax.ShapeDtypeStruct((1024, 256), BF16),
            jax.ShapeDtypeStruct((1024, CAP), BF16),
            jax.ShapeDtypeStruct((1024, 256), BF16),
            jax.ShapeDtypeStruct((512, D), BF16),
            jax.ShapeDtypeStruct((512, D), BF16),
        ],
        scratch_shapes=[
            pltpu.VMEM((1024, D), BF16),
            pltpu.VMEM((8, 16, CAP), BF16),
            pltpu.VMEM((D, 384), BF16),
            pltpu.VMEM((256, D), BF16),
            pltpu.SemaphoreType.DMA((8,)),
            pltpu.SemaphoreType.DMA((8,)),
            pltpu.SemaphoreType.DMA((2,)),
        ],
        compiler_params=pltpu.CompilerParams(vmem_limit_bytes=32 * 1024 * 1024),
        cost_estimate=pl.CostEstimate(
            flops=2 * 1024 * D * 640 * 2, bytes_accessed=15 * 2**20, transcendentals=2**19
        ),
    )(*in_hbm(*parts), table, *in_hbm(qkv_full, out_full))


def attend_back_kernel(*refs):
    parts, id_parts, table = refs[:8], refs[8:16], refs[16]
    w_hbm, o_hbm, queries, key_values = refs[17:21]
    grads, far, near = refs[21:24]
    g, ids, w, o, g_sems, i_sems, w_sems = refs[24:]
    step = pl.program_id(0)
    blocks, numbers = block_copies(parts, g, g_sems), id_copies(id_parts, ids, i_sems)
    loads = [
        pltpu.make_async_copy(o_hbm, o, w_sems.at[1]),
        pltpu.make_async_copy(w_hbm, w, w_sems.at[0]),
    ]

    @pl.when(step == 0)
    def _():
        for copy in loads[:1] + blocks[4:] + numbers[4:] + loads[1:] + blocks[:4] + numbers[:4]:
            copy.start()
        for copy in loads[:1] + blocks[4:] + numbers[4:]:
            copy.wait()

    @pl.when(step == 1)
    def _():
        for copy in blocks[:4] + numbers[:4]:
            copy.wait()

    half = 1 - step
    rows = pl.ds(pl.multiple_of(half * 512, 512), 512)
    grad_mixed = dot_nt(g[rows, :], o[...]).astype(BF16)
    to_key, to_value = spreads()
    for k in range(4):
        allowed, factors = block_tables(ids[half * 4 + k], table)
        here = slice(CAP * k, CAP * (k + 1))
        query, both = queries[here, :], key_values[here, :]
        keys = dot_nn(both, to_key).astype(BF16)
        values = dot_nn(both, to_value).astype(BF16)
        probs = softmax_heads(query, keys, allowed)
        grad_heads = stack_heads(grad_mixed[here])
        grad_probs = dot_nt(grad_heads, values)
        scores = []
        for h in range(4):
            part = grad_probs[CAP * h : CAP * (h + 1)]
            delta = jnp.sum(probs[h] * part, axis=1, keepdims=True)
            scores.append((probs[h] * (part - delta)).astype(BF16))
        grad_query = dot_nn(jnp.concatenate(scores, axis=1), stack_heads(keys)) * 0.125
        folded = dot_nt(stack_heads(query), to_key).astype(BF16)
        grad_folded = dot_nt(grad_heads, to_value).astype(BF16)
        low = jnp.concatenate([item.astype(BF16) for item in probs], axis=0)
        grad_both = dot_tn(jnp.concatenate(scores, axis=0), folded) * 0.125 + dot_tn(low, grad_folded)
        item = jnp.concatenate([grad_query, grad_both], axis=1)
        grads[here, :] = turned(item, factors, -1.0).astype(BF16)

    @pl.when(step == 0)
    def _():
        loads[1].wait()

    total = dot_nt(grads[...], w[...])

    @pl.when(step == 0)
    def _():
        far[...] = total.astype(BF16)

    @pl.when(step == 1)
    def _():
        near[...] = total.astype(BF16)


def attend_back(parts, id_parts, table, qkv_full, out_full, queries, key_values):
    row = lambda i: (1 - i, 0)
    return pl.pallas_call(
        attend_back_kernel,
        grid=(2,),
        in_specs=[HBM] * 16
        + [pl.BlockSpec((2, CAP, 1152), lambda i: (0, 0, 0))]
        + [HBM] * 2
        + [pl.BlockSpec((512, 256), row), pl.BlockSpec((512, CAP), row)],
        out_specs=[
            pl.BlockSpec((512, 384), row),
            pl.BlockSpec((512, D), lambda i: (0, 0)),
            pl.BlockSpec((512, D), lambda i: (0, 0)),
        ],
        out_shape=[
            jax.ShapeDtypeStruct((1024, 384), BF16),
            jax.ShapeDtypeStruct((512, D), BF16),
            jax.ShapeDtypeStruct((512, D), BF16),
        ],
        scratch_shapes=[
            pltpu.VMEM((1024, D), BF16),
            pltpu.VMEM((8, 16, CAP), BF16),
            pltpu.VMEM((D, 384), BF16),
            pltpu.VMEM((256, D), BF16),
            pltpu.SemaphoreType.DMA((8,)),
            pltpu.SemaphoreType.DMA((8,)),
            pltpu.SemaphoreType.DMA((2,)),
        ],
        compiler_params=pltpu.CompilerParams(vmem_limit_bytes=32 * 1024 * 1024),
        cost_estimate=pl.CostEstimate(
            flops=2 * 1024 * D * 640 * 2, bytes_accessed=15 * 2**20, transcendentals=2**19
        ),
    )(*in_hbm(*parts, *id_parts), table, *in_hbm(qkv_full, out_full), queries, key_values)


def out_grads_kernel(*refs):
    parts, mixed_hbm, out, g, mixed, sems, in_sems = refs[:8], *refs[8:]
    copies = block_copies(parts, g, sems)
    copies.append(pltpu.make_async_copy(mixed_hbm, mixed, in_sems.at[0]))
    for copy in copies:
        copy.start()
    for copy in copies:
        copy.wait()
    out[...] = dot_tn(mixed[...], g[...]).astype(BF16)


def out_grads(parts, mixed):
    return pl.pallas_call(
        out_grads_kernel,
        in_specs=[HBM] * 9,
        out_specs=pl.BlockSpec(memory_space=pltpu.VMEM),
        out_shape=jax.ShapeDtypeStruct((256, D), BF16),
        scratch_shapes=[
            pltpu.VMEM((1024, D), BF16),
            pltpu.VMEM((1024, 256), BF16),
            pltpu.SemaphoreType.DMA((8,)),
            pltpu.SemaphoreType.DMA((1,)),
        ],
        compiler_params=pltpu.CompilerParams(vmem_limit_bytes=24 * 1024 * 1024),
        cost_estimate=pl.CostEstimate(
            flops=2 * 1024 * D * 256, bytes_accessed=6 * 2**20, transcendentals=0
        ),
    )(*in_hbm(*parts, mixed))


def qkv_grads_kernel(*refs):
    parts, grads_hbm, out, x, grads, sems, in_sems = refs[:8], *refs[8:]
    copies = block_copies(parts, x, sems)
    copies.append(pltpu.make_async_copy(grads_hbm, grads, in_sems.at[0]))
    for copy in copies:
        copy.start()
    for copy in copies:
        copy.wait()
    for k in range(8):
        out[k // 4, k % 4] = dot_tn(x[:, 256 * k : 256 * (k + 1)], grads[...]).astype(BF16)


def qkv_grads(parts, grads):
    return pl.pallas_call(
        qkv_grads_kernel,
        in_specs=[HBM] * 9,
        out_specs=pl.BlockSpec(memory_space=pltpu.VMEM),
        out_shape=jax.ShapeDtypeStruct((2, 4, 256, 384), BF16),
        scratch_shapes=[
            pltpu.VMEM((1024, D), BF16),
            pltpu.VMEM((1024, 384), BF16),
            pltpu.SemaphoreType.DMA((8,)),
            pltpu.SemaphoreType.DMA((1,)),
        ],
        compiler_params=pltpu.CompilerParams(vmem_limit_bytes=24 * 1024 * 1024),
        cost_estimate=pl.CostEstimate(
            flops=2 * 1024 * D * 384, bytes_accessed=6 * 2**20, transcendentals=0
        ),
    )(*in_hbm(*parts, grads))


def norm_back_kernel(own, one, two, three, rows, upstream, grad, low):
    x = rows[...]
    inner = own[...] + one[...].astype(F32) + two[...].astype(F32) + three[...].astype(F32)
    scale = lax.rsqrt(jnp.mean(x * x, axis=1, keepdims=True) + norm_eps)
    slope = jnp.mean(inner * x, axis=1, keepdims=True)
    total = upstream[...].astype(F32) + scale * inner - x * (scale * scale * scale * slope)
    grad[...] = total
    low[...] = total.astype(BF16)


def norm_back_sum(own, came, rows, upstream):
    spec = pl.BlockSpec((32, D), lambda i: (i, 0))
    return pl.pallas_call(
        norm_back_kernel,
        grid=(CAP // 32,),
        in_specs=[spec] * 6,
        out_specs=[spec] * 2,
        out_shape=[jax.ShapeDtypeStruct((CAP, D), F32), jax.ShapeDtypeStruct((CAP, D), BF16)],
        compiler_params=pltpu.CompilerParams(vmem_limit_bytes=16 * 1024 * 1024),
        cost_estimate=pl.CostEstimate(
            flops=20 * CAP * D, bytes_accessed=6 * 2**20, transcendentals=CAP
        ),
    )(own, *came, rows, upstream)


def times(left, right):
    return jnp.dot(left, right, preferred_element_type=F32)


def times_t(left, right):
    return lax.dot_general(left, right, (((1,), (1,)), ((), ())), preferred_element_type=F32)


def t_times(left, right):
    return lax.dot_general(left, right, (((0,), (0,)), ((), ())), preferred_element_type=F32)


def rms_scale(rows):
    return lax.rsqrt(jnp.mean(rows * rows, axis=-1, keepdims=True) + norm_eps)


def norm_back(rows, scale, inner):
    return scale * inner - rows * (scale * scale * scale) * jnp.mean(
        inner * rows, axis=-1, keepdims=True
    )


def from_ring(item, step):
    return lax.ppermute(item, RING, [(i, (i - step) % 4) for i in range(4)])


def to_ring(item, step):
    return lax.ppermute(item, RING, [(i, (i + step) % 4) for i in range(4)])


def swap(item, axis):
    return lax.ppermute(item, axis, SWAP)


def share_parts(item, *first):
    own = swap(item, "c")
    ring = after(tuple(from_ring(item, step) for step in STEPS[1:]), *first)
    return [item, *ring, own] + [swap(part, "c") for part in ring]


def pair_blocks(near, far, *first):
    far = after(swap(far, "c"), *first)

    def block(spot):
        here = slice(spot * CAP, (spot + 1) * CAP)
        return near[here].astype(F32) + far[here].astype(F32)

    return (block(0),) + tuple(block(spot).astype(BF16) for spot in (1, 2, 3))


def ring_sum(blocks, *first):
    came = tuple(to_ring(blocks[spot], STEPS[spot]) for spot in (1, 2, 3))
    return blocks[0] + sum(item.astype(F32) for item in after(came, *first))


def spread_columns(chunks, xl, c):
    mine = [jnp.where(c == 0, pair[0], pair[1]) for pair in chunks]
    away = [jnp.where(c == 0, pair[1], pair[0]) for pair in chunks]
    came = swap(jnp.concatenate(away, axis=0), "c")
    rows = mine[0].shape[0]
    both = []
    for k in range(2):
        other = came[k * rows : (k + 1) * rows]
        both.append(
            jnp.concatenate(
                [jnp.where(c == 0, mine[k], other), jnp.where(c == 0, other, mine[k])], axis=0
            )
        )
    kept = jnp.where(xl == 0, both[0], both[1])
    came = swap(jnp.where(xl == 0, both[1], both[0]), "xl")
    return jnp.stack([jnp.where(xl == 0, kept, came), jnp.where(xl == 0, came, kept)])


def gather_four(item, axis, spot, dim):
    parts = [item]
    for step in (1, 2, 3):
        parts.append(lax.ppermute(item, axis, [(i, (i - step) % 4) for i in range(4)]))
    return jnp.stack([pick(parts, (q - spot) % 4) for q in range(4)], axis=dim)


def pick(parts, which):
    out = parts[0]
    for k in range(1, len(parts)):
        out = jnp.where(which == k, parts[k], out)
    return out


def four_pieces(item, spot, dim):
    return [
        lax.dynamic_index_in_dim(item, (spot + step) % 4, dim, keepdims=False) for step in range(4)
    ]


def exchange(pieces, axis):
    return tuple(
        lax.ppermute(pieces[step], axis, [(i, (i + step) % 4) for i in range(4)])
        for step in (1, 2, 3)
    )


def four_sum(pieces, came):
    return pieces[0].astype(F32) + sum(item.astype(F32) for item in came)


def row_pairs(step, back):
    pairs = []
    for h in range(2):
        for e in range(2):
            first = 2 * h + e
            one = (h * 4 + first) * 2 + e
            other = (h * 4 + (first + step) % 4) * 2 + e
            pairs.append((other, one) if back else (one, other))
    return pairs


def after(item, *others):
    return lax.optimization_barrier((item,) + others)[0] if others else item


def order_of_columns(xh):
    place = jnp.arange(768)
    core, owner, row = place // 384, (place % 384) // 48, place % 48
    origin = jnp.where(row < 44, 176 * owner + 88 * core + 44 * xh + row, -1)
    return (jnp.arange(1408)[:, None] == origin[None, :]).astype(BF16)


def column_part(item, width, xh):
    out = []
    for k in range(2):
        start = 2 * width * k
        out.append(
            jnp.where(
                xh == 0, item[:, start : start + width], item[:, start + width : start + 2 * width]
            )
        )
    return out


def on_device(
    tokens,
    doc_ids,
    first_gain,
    query_weight,
    key_weight,
    value_weight,
    out_weight,
    second_gain,
    gate_weight,
    up_weight,
    down_weight,
    cotangent,
):
    xh, xl, y, z, c = (lax.axis_index(name) for name in ("xh", "xl", "y", "z", "c"))
    first_col = first_gain.astype(F32)[:, None]
    second_col = second_gain.astype(F32)[:, None]

    def scaled(item, gain):
        return (item.astype(F32) * gain).astype(BF16)

    q_parts = column_part(scaled(query_weight, first_col), 512, xh)
    k_parts = column_part(scaled(key_weight, first_col), 64, xh)
    v_parts = column_part(scaled(value_weight, first_col), 64, xh)
    chunks = [
        [
            jnp.concatenate([q_parts[k][:, 256 * j : 256 * (j + 1)], k_parts[k], v_parts[k]], axis=1)
            for j in range(2)
        ]
        for k in range(2)
    ]
    spread = spread_columns(chunks, xl, c)

    qkv_full = lax.all_gather(spread, ("y", "z"), axis=1, tiled=True).reshape(D, 384)

    wide = jnp.stack([scaled(gate_weight, second_col), scaled(up_weight, second_col)])
    blocks = jnp.concatenate([wide[:, :, 1408 * k : 1408 * (k + 1)] for k in range(4)], axis=0)
    sorted_columns = times(blocks.reshape(256, 1408), order_of_columns(xh)).astype(BF16)
    sorted_columns = sorted_columns.reshape(2, 2, 2, 32, 768)
    chunks = [
        [
            jnp.concatenate(
                [
                    sorted_columns[k, h, item, :, 384 * j : 384 * (j + 1)]
                    for item in range(2)
                    for h in range(2)
                ],
                axis=1,
            )
            for j in range(2)
        ]
        for k in range(2)
    ]
    down_half = jnp.where(xh == 0, down_weight[:44], down_weight[44:])
    down_half = jnp.pad(down_half, ((0, 4), (0, 0)))
    corner = jnp.concatenate(
        [down_half[16 * k : 16 * (k + 1), 2 * WIDE :] for k in range(3)], axis=1
    )
    feed_spread = spread_columns(chunks, xl, c).reshape(128, 2 * WIDE)
    packed = jnp.concatenate([feed_spread, down_half[:, : 2 * WIDE], corner], axis=0)

    source = 2 * xh + c
    came = swap(out_weight, "c")
    head = jnp.concatenate(
        [jnp.where(c == 0, out_weight, came), jnp.where(c == 0, came, out_weight)], axis=0
    )
    lines = [head]
    for step in (1, 2, 3):
        lines.append(lax.ppermute(head, ("xh", "y", "c"), row_pairs(step, False)))
    head = pick(lines, (y - source) % 4)
    out_full = gather_four(head, "z", z, 0).reshape(256, D)

    table = rotary_table()
    rows = tokens.astype(F32)
    first_scale = rms_scale(rows)
    id_rows = jnp.pad(doc_ids.astype(BF16)[None], ((0, 15), (0, D - CAP)))
    payload = jnp.concatenate([(rows * first_scale).astype(BF16), id_rows], axis=0)
    first = share_parts(after(payload, spread, feed_spread))
    packed = after(packed, qkv_full, out_full, *first[1:4])
    packed = lax.all_gather(packed, ("y", "z"), axis=0, tiled=True)

    queries, key_values, mixed, far, near = attend(first, table, qkv_full, out_full)
    upstream = share_parts(after(cotangent, *first[1:4]), mixed)
    far = after(far, upstream[1])
    shuffle = after(jnp.concatenate([order_of_columns(0), order_of_columns(1)], axis=1), mixed)
    midway = rows + ring_sum(pair_blocks(near, far), shuffle)

    second_scale = rms_scale(midway)
    second = share_parts((midway * second_scale).astype(BF16))
    hidden, grad_feed, far, near = feed_forward(second, upstream, packed)
    blocks = pair_blocks(near, far)
    pack = feed_grads(second, upstream, after(hidden, *blocks), grad_feed)
    came = tuple(to_ring(blocks[spot], STEPS[spot]) for spot in (1, 2, 3))
    grad_mid, grad_low = norm_back_sum(blocks[0], after(came, pack), midway, cotangent)
    out_far, out_near = output_product(after(hidden, pack), packed)
    third = share_parts(grad_low, out_far)
    pack = lax.psum_scatter(after(pack, grad_low), ("y", "z"), scatter_dimension=0, tiled=True)

    out_blocks = pair_blocks(out_near, after(out_far, *third[1:4]))
    out_term = out_grads(third, mixed).reshape(4, 64, D)
    out_sent = four_pieces(out_term, z, 0)
    out_came = exchange(out_sent, "z")
    grad_qkv, far, near = attend_back(
        third,
        first,
        table,
        qkv_full,
        out_full,
        after(queries, *out_sent, *out_blocks),
        key_values,
    )
    product = ring_sum(out_blocks, grad_qkv)
    output = (midway + product).astype(BF16)
    out_part = four_sum(out_sent, after(out_came, product))
    far = after(far, out_part)
    sent = out_part.astype(BF16)
    out_came = tuple(
        lax.ppermute(sent, ("xh", "y", "c"), row_pairs(step, True)) for step in (1, 2, 3)
    )
    qkv_term = qkv_grads(first, after(grad_qkv, sent))
    blocks = pair_blocks(near, far, qkv_term)
    out_came = after(out_came, *blocks)
    out_part = (out_part + sum(item.astype(F32) for item in out_came)).astype(BF16)

    def halves(item):
        low, high = item[:, :32], item[:, 32:]
        return jnp.where(c == 0, low, high), jnp.where(c == 0, high, low)

    sent = four_pieces(after(qkv_term, out_part, *blocks), y, 1)
    came = exchange(sent, "y")
    ring_came = (to_ring(blocks[1], STEPS[1]), to_ring(blocks[2], STEPS[2]))
    corner = jnp.concatenate([pack[176:, 512 * k : 512 * (k + 1)] for k in range(3)], axis=0)
    down_part = jnp.concatenate([pack[128:176], corner], axis=1)
    feed_part = pack[:128].reshape(2, 64, 2 * WIDE)
    feed_mine, feed_away = halves(feed_part)
    came, ring_came, feed_mine, feed_away, down_part = lax.optimization_barrier(
        (came, ring_came, feed_mine, feed_away, down_part)
    )
    sent = four_pieces(four_sum(sent, came).astype(BF16).reshape(2, 4, 64, 384), z, 1)
    came = exchange(sent, "z")
    last_came = to_ring(blocks[3], STEPS[3])
    feed_came = swap(feed_away, "c")
    came, last_came, feed_came = lax.optimization_barrier((came, last_came, feed_came))

    def in_order(mine, came):
        return jnp.where(c == 0, mine, came), jnp.where(c == 0, came, mine)

    def along_ring(both, more):
        here = jnp.where(xl == 0, both[0], both[1])
        there = jnp.where(xl == 0, both[1], both[0])
        across = jnp.concatenate([here, more], axis=1)
        return here, (to_ring(there, 1), to_ring(across, 2), to_ring(there, 3))

    def by_chip(here, came):
        width, spot = here.shape[1], 2 * xh + xl
        stacked = [here, came[0], came[1][:, :width], came[2]]
        return [[pick(stacked, (spot - (2 * h + k)) % 4) for h in range(2)] for k in range(2)]

    down_wide = jnp.concatenate(
        [down_part[:32], jnp.concatenate([down_part[32:, :1024], down_part[32:, 1024:]], axis=0)],
        axis=1,
    )
    feed_here, feed_came = along_ring(
        jnp.concatenate(in_order(feed_mine, feed_came), axis=2), down_wide
    )

    qkv_part = four_sum(sent, came).astype(BF16)
    qkv_mine, qkv_away = halves(qkv_part)
    away = jnp.where(c == 0, out_part[32:], out_part[:32])
    sent = jnp.concatenate(
        [
            qkv_away.reshape(64, 384),
            jnp.concatenate([away[:, :1024], away[:, 1024:]], axis=0),
        ],
        axis=1,
    )
    came = swap(sent, "c")
    zero, one = in_order(qkv_mine, came[:, :384].reshape(2, 32, 384))
    pair = zero[:, :, 256:].astype(F32) + one[:, :, 256:].astype(F32)
    both = jnp.concatenate([zero[:, :, :256], one[:, :, :256], pair.astype(BF16)], axis=2)
    out_half = jnp.where(
        y % 2 == c,
        jnp.where(c == 0, out_part[:32], out_part[32:]),
        jnp.concatenate([came[:32, 384:], came[32:, 384:]], axis=1),
    )
    both, out_half = lax.optimization_barrier((both, out_half))
    qkv_here, came = along_ring(both, out_half)
    feed_came = after(feed_came, both)

    inner_one = blocks[0] + sum(item.astype(F32) for item in ring_came + (last_came,))
    tokens_grad = grad_mid + norm_back(rows, first_scale, inner_one)
    parts = by_chip(feed_here, feed_came)
    down_other = feed_came[1][:, 3072:]
    down_other = jnp.concatenate(
        [
            down_other[:, :2048],
            jnp.concatenate([down_other[:16, 2048:], down_other[16:, 2048:]], axis=1),
        ],
        axis=0,
    )
    down_grad = jnp.concatenate(
        [
            jnp.where(xh == 0, down_part, down_other)[:44],
            jnp.where(xh == 0, down_other, down_part)[:44],
        ],
        axis=0,
    ).astype(F32)
    rows_of = []
    for item in range(2):
        for k in range(2):
            for half in range(2):
                start = item * WIDE + half * 384
                rows_of.append(
                    jnp.concatenate(
                        [
                            parts[k][h][:, e * 2 * WIDE + start : e * 2 * WIDE + start + 384]
                            for h in range(2)
                            for e in range(2)
                        ],
                        axis=1,
                    )
                )
    unsorted = times_t(jnp.concatenate(rows_of, axis=0), shuffle).reshape(2, 4, 32, 1408)
    gate_raw = jnp.concatenate([unsorted[0, k] for k in range(4)], axis=1)
    up_raw = jnp.concatenate([unsorted[1, k] for k in range(4)], axis=1)
    second_grad = jnp.sum(gate_raw * gate_weight.astype(F32), axis=1) + jnp.sum(
        up_raw * up_weight.astype(F32), axis=1
    )

    parts = by_chip(qkv_here, came)
    out_grad = jnp.where(y // 2 == xh, out_half, came[1][:, 640:]).astype(F32)

    def joined(start, end):
        return jnp.concatenate(
            [parts[k][h][:, start:end] for k in range(2) for h in range(2)], axis=1
        ).astype(F32)

    query_raw, key_raw, value_raw = joined(0, 512), joined(512, 576), joined(576, 640)
    first_grad = (
        jnp.sum(query_raw * query_weight.astype(F32), axis=1)
        + jnp.sum(key_raw * key_weight.astype(F32), axis=1)
        + jnp.sum(value_raw * value_weight.astype(F32), axis=1)
    )

    return (
        output,
        tokens_grad,
        first_grad,
        query_raw * first_col,
        key_raw * first_col,
        value_raw * first_col,
        out_grad,
        second_grad,
        gate_raw * second_col,
        up_raw * second_col,
        down_grad,
    )


def solution(mesh):
    fine = Mesh(mesh.devices.reshape(2, 2, 4, 4, 2), ("xh", "xl", "y", "z", "c"))
    everyone = ("xh", "xl", "y", "z", "c")
    group = ("xl", "y", "z", "c")
    in_specs = (
        P(everyone, None),
        P(everyone),
        P(group),
        P(group, None),
        P(group, None),
        P(group, None),
        P(group, None),
        P(group),
        P(group, None),
        P(group, None),
        P(group, None),
        P(everyone, None),
    )
    out_specs = (
        P(everyone, None),
        P(everyone, None),
        P(group),
        P(group, None),
        P(group, None),
        P(group, None),
        P(group, None),
        P(group),
        P(group, None),
        P(group, None),
        P(group, None),
    )
    return jax.shard_map(
        on_device, mesh=fine, in_specs=in_specs, out_specs=out_specs, check_vma=False
    )
```

```python
import jax
import jax.numpy as jnp
import ml_dtypes
import numpy as np
from jax import lax
from jax.experimental import pallas as pl
from jax.experimental.pallas import tpu as pltpu
from jax.sharding import Mesh, PartitionSpec as P

D = 2048
HDIM = 64
CAP = 128
WIDE = 768
BF16 = jnp.bfloat16
F32 = jnp.float32

norm_eps = 1e-05

RING = ("xh", "xl")
SWAP = [(0, 1), (1, 0)]
STEPS = (0, 1, 3, 2)


def dot_nn(left, right):
    return lax.dot_general(left, right, (((1,), (0,)), ((), ())), preferred_element_type=F32)


def dot_nt(left, right):
    return lax.dot_general(left, right, (((1,), (1,)), ((), ())), preferred_element_type=F32)


def dot_tn(left, right):
    return lax.dot_general(left, right, (((0,), (0,)), ((), ())), preferred_element_type=F32)


HBM = pl.BlockSpec(memory_space=pltpu.HBM)


def in_hbm(*items):
    return [pltpu.with_memory_space_constraint(item, pltpu.HBM) for item in items]


def block_copies(parts, whole, sems):
    return [
        pltpu.make_async_copy(
            part.at[pl.ds(0, CAP)], whole.at[pl.ds(CAP * spot, CAP)], sems.at[spot]
        )
        for spot, part in enumerate(parts)
    ]


def id_copies(parts, ids, sems):
    return [
        pltpu.make_async_copy(part.at[pl.ds(CAP, 16), pl.ds(0, CAP)], ids.at[spot], sems.at[spot])
        for spot, part in enumerate(parts)
    ]


def feed_copies(packed, feed, sems):
    copies = []
    for k in range(16):
        for h in range(2):
            copies.append(
                pltpu.make_async_copy(
                    packed.at[pl.ds(192 * k + 64 * h, 64)],
                    feed.at[pl.ds(1024 * h + 64 * k, 64)],
                    sems.at[2 * k + h],
                )
            )
    return copies


def down_copies(packed, down, sems):
    copies = []
    for k in range(16):
        copies.append(
            pltpu.make_async_copy(
                packed.at[pl.ds(192 * k + 128, 48)],
                down.at[pl.ds(48 * k, 48), pl.ds(0, 1536)],
                sems.at[4 * k],
            )
        )
        for h in range(3):
            copies.append(
                pltpu.make_async_copy(
                    packed.at[pl.ds(192 * k + 176, 16), pl.ds(512 * h, 512)],
                    down.at[pl.ds(48 * k + 16 * h, 16), pl.ds(1536, 512)],
                    sems.at[4 * k + 1 + h],
                )
            )
    return copies


def back_kernel(*refs):
    parts, packed, out, c, down, c_sems, d_sems = refs[:8], *refs[8:]
    step = pl.program_id(0)
    loads = block_copies(parts, c, c_sems)

    @pl.when(step == 0)
    def _():
        rows = down_copies(packed, down, d_sems)
        for copy in loads[:4] + rows + loads[4:]:
            copy.start()
        for copy in loads[:4] + rows:
            copy.wait()

    @pl.when(step == 1)
    def _():
        for copy in loads[4:]:
            copy.wait()

    rows = pl.ds(pl.multiple_of(step * 512, 512), 512)
    out[...] = dot_nt(c[rows, :], down[...])


def feed_back(c_parts, packed):
    return pl.pallas_call(
        back_kernel,
        grid=(2,),
        in_specs=[HBM] * 9,
        out_specs=pl.BlockSpec((512, WIDE), lambda i: (i, 0)),
        out_shape=jax.ShapeDtypeStruct((1024, WIDE), F32),
        scratch_shapes=[
            pltpu.VMEM((1024, D), BF16),
            pltpu.VMEM((WIDE, D), BF16),
            pltpu.SemaphoreType.DMA((8,)),
            pltpu.SemaphoreType.DMA((64,)),
        ],
        compiler_params=pltpu.CompilerParams(vmem_limit_bytes=24 * 1024 * 1024),
        cost_estimate=pl.CostEstimate(
            flops=2 * 1024 * D * WIDE, bytes_accessed=10 * 2**20, transcendentals=0
        ),
    )(*in_hbm(*c_parts, packed))


def feed_kernel(*refs):
    x_parts, packed, back = refs[:8], refs[8], refs[9]
    hidden, grads, far, near, x, feed, x_sems, f_sems = refs[10:]
    step = pl.program_id(0)
    first = block_copies(x_parts, x, x_sems)

    @pl.when(step == 0)
    def _():
        second = feed_copies(packed, feed, f_sems)
        for copy in first[4:6] + second + first[6:] + first[:4]:
            copy.start()
        for copy in first[4:6] + second:
            copy.wait()

    for k in range(1, 4):

        @pl.when(step == k)
        def _(k=k):
            spot = (2 * k + 4) % 8
            for copy in first[spot : spot + 2]:
                copy.wait()

    rows = pl.ds(pl.multiple_of(((step + 2) % 4) * 256, 256), 256)
    block = x[rows, :]
    for k in range(0, WIDE, 256):
        here, beside = slice(k, k + 256), slice(WIDE + k, WIDE + k + 256)
        gate = dot_nn(block, feed[:, here])
        up = dot_nn(block, feed[:, beside])
        slope = back[:, here]
        sig = jax.nn.sigmoid(gate)
        silu = gate * sig
        hidden[:, here] = (silu * up).astype(BF16)
        grads[:, here] = (slope * up * (sig * (1.0 + gate * (1.0 - sig)))).astype(BF16)
        grads[:, beside] = (slope * silu).astype(BF16)
    inner = dot_nt(grads[...], feed[...])

    @pl.when(step < 2)
    def _():
        far[...] = inner.astype(BF16)

    @pl.when(step >= 2)
    def _():
        near[...] = inner.astype(BF16)


def feed_forward(x_parts, packed, back):
    row = lambda i: ((i + 2) % 4, 0)
    return pl.pallas_call(
        feed_kernel,
        grid=(4,),
        in_specs=[HBM] * 9 + [pl.BlockSpec((256, WIDE), row)],
        out_specs=[
            pl.BlockSpec((256, WIDE), row),
            pl.BlockSpec((256, 2 * WIDE), row),
            pl.BlockSpec((256, D), lambda i: (jnp.minimum(i, 1), 0)),
            pl.BlockSpec((256, D), lambda i: (jnp.maximum(i - 2, 0), 0)),
        ],
        out_shape=[
            jax.ShapeDtypeStruct((1024, WIDE), BF16),
            jax.ShapeDtypeStruct((1024, 2 * WIDE), BF16),
            jax.ShapeDtypeStruct((512, D), BF16),
            jax.ShapeDtypeStruct((512, D), BF16),
        ],
        scratch_shapes=[
            pltpu.VMEM((1024, D), BF16),
            pltpu.VMEM((D, 2 * WIDE), BF16),
            pltpu.SemaphoreType.DMA((8,)),
            pltpu.SemaphoreType.DMA((32,)),
        ],
        compiler_params=pltpu.CompilerParams(vmem_limit_bytes=36 * 1024 * 1024),
        cost_estimate=pl.CostEstimate(
            flops=2 * 1024 * D * WIDE * 4, bytes_accessed=24 * 2**20, transcendentals=1024 * WIDE
        ),
    )(*in_hbm(*x_parts, packed), back)


def grads_kernel(*refs):
    x_parts, c_parts, hidden_hbm, grads_hbm = refs[:8], refs[8:16], refs[16], refs[17]
    out = refs[18]
    x, c, hidden, grads, pack, x_sems, c_sems, in_sems, sems = refs[19:]
    first = block_copies(x_parts, x, x_sems)
    second = block_copies(c_parts, c, c_sems)
    loads = [
        pltpu.make_async_copy(grads_hbm, grads, in_sems.at[0]),
        pltpu.make_async_copy(hidden_hbm, hidden, in_sems.at[1]),
    ]
    for copy in first + loads + second:
        copy.start()
    for copy in first + loads[:1]:
        copy.wait()
    stores = []

    def store(row, rows):
        copy = pltpu.make_async_copy(
            pack.at[pl.ds(row, rows)], out.at[pl.ds(row, rows)], sems.at[len(stores)]
        )
        copy.start()
        stores.append(copy)

    for k in range(8):
        tile = dot_tn(x[:, 256 * k : 256 * (k + 1)], grads[...]).astype(BF16)
        half, spot = k // 4, (k % 4) * 4
        for j in range(4):
            row = 192 * (spot + j) + 64 * half
            pack[row : row + 64, :] = tile[64 * j : 64 * (j + 1)]
            store(row, 64)
    for copy in second + loads[1:]:
        copy.wait()
    for k in range(2):
        tile = dot_tn(hidden[:, 384 * k : 384 * (k + 1)], c[...]).astype(BF16)
        for j in range(8):
            row = 192 * (8 * k + j) + 128
            piece = tile[48 * j : 48 * (j + 1)]
            pack[row : row + 48, :] = piece[:, :1536]
            for h in range(3):
                pack[row + 48 : row + 64, 512 * h : 512 * (h + 1)] = piece[
                    16 * h : 16 * (h + 1), 1536:
                ]
            store(row, 64)
    for copy in stores:
        copy.wait()


def feed_grads(x_parts, c_parts, hidden, grads):
    return pl.pallas_call(
        grads_kernel,
        in_specs=[HBM] * 18,
        out_specs=HBM,
        out_shape=jax.ShapeDtypeStruct((3072, 1536), BF16),
        scratch_shapes=[
            pltpu.VMEM((1024, D), BF16),
            pltpu.VMEM((1024, D), BF16),
            pltpu.VMEM((1024, WIDE), BF16),
            pltpu.VMEM((1024, 2 * WIDE), BF16),
            pltpu.VMEM((3072, 2 * WIDE), BF16),
            pltpu.SemaphoreType.DMA((8,)),
            pltpu.SemaphoreType.DMA((8,)),
            pltpu.SemaphoreType.DMA((2,)),
            pltpu.SemaphoreType.DMA((48,)),
        ],
        compiler_params=pltpu.CompilerParams(vmem_limit_bytes=60 * 1024 * 1024),
        cost_estimate=pl.CostEstimate(
            flops=2 * 1024 * D * WIDE * 3, bytes_accessed=22 * 2**20, transcendentals=0
        ),
    )(*in_hbm(*x_parts, *c_parts, hidden, grads))


def output_kernel(hidden_hbm, packed, far, near, hidden, down, total, sems, out_sems):
    copies = down_copies(packed, down, sems)
    copies.append(pltpu.make_async_copy(hidden_hbm, hidden, sems.at[64]))
    for copy in copies:
        copy.start()
    for copy in copies:
        copy.wait()
    stores = []
    for k, out in ((1, far), (0, near)):
        total[k] = dot_nn(hidden[512 * k : 512 * (k + 1)], down[...]).astype(BF16)
        stores.append(pltpu.make_async_copy(total.at[k], out, out_sems.at[k]))
        stores[-1].start()
    for copy in stores:
        copy.wait()


def output_product(hidden, packed):
    return pl.pallas_call(
        output_kernel,
        in_specs=[HBM, HBM],
        out_specs=[HBM, HBM],
        out_shape=[pltpu.HBM((512, D), BF16), pltpu.HBM((512, D), BF16)],
        scratch_shapes=[
            pltpu.VMEM((1024, WIDE), BF16),
            pltpu.VMEM((WIDE, D), BF16),
            pltpu.VMEM((2, 512, D), BF16),
            pltpu.SemaphoreType.DMA((65,)),
            pltpu.SemaphoreType.DMA((2,)),
        ],
        compiler_params=pltpu.CompilerParams(vmem_limit_bytes=24 * 1024 * 1024),
        cost_estimate=pl.CostEstimate(
            flops=2 * 1024 * D * WIDE, bytes_accessed=11 * 2**20, transcendentals=0
        ),
    )(*in_hbm(hidden, packed))


def rotary_table():
    place = np.arange(CAP, dtype=np.float32)[:, None]
    inverse = np.float32(10000.0) ** (np.arange(32, dtype=np.float32) * np.float32(-2.0 / HDIM))
    angle = (place * inverse).astype(np.float32)
    cosine, sine = np.cos(angle), np.sin(angle)
    zero, one = np.zeros((CAP, 64), np.float32), np.ones((CAP, 64), np.float32)
    ahead = np.concatenate([-sine, zero[:, :32]], axis=1)
    behind = np.concatenate([zero[:, :32], sine], axis=1)
    cosine = np.concatenate([cosine, cosine], axis=1)
    table = np.concatenate(
        [cosine, cosine, ahead, ahead, behind, behind, cosine, one, ahead, zero, behind, zero], axis=1
    )
    high = table.astype(ml_dtypes.bfloat16)
    rest = (table - high.astype(np.float32)).astype(ml_dtypes.bfloat16)
    return jnp.asarray(np.stack([high, rest]))


def lane_of(shape, dim):
    return lax.broadcasted_iota(jnp.int32, shape, dim)


def block_tables(ids, table):
    row = jnp.broadcast_to(ids.astype(F32)[:1], (CAP, CAP))
    same = row == row.T
    to, frm = lane_of((CAP, CAP), 0), lane_of((CAP, CAP), 1)
    place = jnp.sum(jnp.where(same & (frm < to), 1.0, 0.0), axis=1, keepdims=True)
    chosen = (frm.astype(F32) == place).astype(BF16)
    factors = dot_nn(chosen, table[0]) + dot_nn(chosen, table[1])
    return same & (frm <= to), factors


def turned(item, factors, sign):
    def three(k):
        pair = factors[:, CAP * k : CAP * (k + 1)]
        return jnp.concatenate([pair, pair, factors[:, CAP * (k + 3) : CAP * (k + 4)]], axis=1)

    other = pltpu.roll(item, 352, 1) * three(1) + pltpu.roll(item, 32, 1) * three(2)
    return item * three(0) + sign * other


def stack_heads(item):
    head = lane_of((CAP, 256), 1) // 64
    return jnp.concatenate([jnp.where(head == h, item, 0).astype(BF16) for h in range(4)], axis=0)


def spreads():
    lane, own = lane_of((CAP, 256), 1) % 64, lane_of((CAP, 256), 0)
    return (lane == own).astype(BF16), (lane + 64 == own).astype(BF16)


def softmax_heads(queries, keys, allowed):
    scores = dot_nt(stack_heads(queries), keys) * 0.125
    out = []
    for h in range(4):
        part = jnp.where(allowed, scores[CAP * h : CAP * (h + 1)], -1e30)
        expo = jnp.exp(part - jnp.max(part, axis=1, keepdims=True))
        out.append(expo / jnp.sum(expo, axis=1, keepdims=True))
    return out


def attend_kernel(*refs):
    parts, table, w_hbm, o_hbm = refs[:8], refs[8], refs[9], refs[10]
    queries, key_values, mixed, far, near = refs[11:16]
    x, ids, w, o, x_sems, i_sems, w_sems = refs[16:]
    step = pl.program_id(0)
    blocks, numbers = block_copies(parts, x, x_sems), id_copies(parts, ids, i_sems)
    loads = [
        pltpu.make_async_copy(w_hbm, w, w_sems.at[0]),
        pltpu.make_async_copy(o_hbm, o, w_sems.at[1]),
    ]

    @pl.when(step == 0)
    def _():
        for copy in loads[:1] + blocks[4:] + numbers[4:] + loads[1:] + blocks[:4] + numbers[:4]:
            copy.start()
        for copy in loads[:1] + blocks[4:] + numbers[4:]:
            copy.wait()

    @pl.when(step == 1)
    def _():
        for copy in blocks[:4] + numbers[:4]:
            copy.wait()

    half = 1 - step
    rows = pl.ds(pl.multiple_of(half * 512, 512), 512)
    qkv = dot_nn(x[rows, :], w[...])
    to_key, to_value = spreads()
    for k in range(4):
        allowed, factors = block_tables(ids[half * 4 + k], table)
        block = turned(qkv[CAP * k : CAP * (k + 1)], factors, 1.0).astype(BF16)
        here = slice(CAP * k, CAP * (k + 1))
        queries[here, :] = block[:, :256]
        key_values[here, :] = block[:, 256:]
        keys = dot_nn(block[:, 256:], to_key).astype(BF16)
        values = dot_nn(block[:, 256:], to_value).astype(BF16)
        probs = softmax_heads(block[:, :256], keys, allowed)
        probs = jnp.concatenate([item.astype(BF16) for item in probs], axis=1)
        mixed[here, :] = dot_nn(probs, stack_heads(values)).astype(BF16)

    @pl.when(step == 0)
    def _():
        loads[1].wait()

    total = dot_nn(mixed[...], o[...])

    @pl.when(step == 0)
    def _():
        far[...] = total.astype(BF16)

    @pl.when(step == 1)
    def _():
        near[...] = total.astype(BF16)


def attend(parts, table, qkv_full, out_full):
    row = lambda i: (1 - i, 0)
    still = lambda i: (0, 0)
    return pl.pallas_call(
        attend_kernel,
        grid=(2,),
        in_specs=[HBM] * 8 + [pl.BlockSpec((2, CAP, 768), lambda i: (0, 0, 0))] + [HBM] * 2,
        out_specs=[
            pl.BlockSpec((512, 256), row),
            pl.BlockSpec((512, CAP), row),
            pl.BlockSpec((512, 256), row),
            pl.BlockSpec((512, D), still),
            pl.BlockSpec((512, D), still),
        ],
        out_shape=[
            jax.ShapeDtypeStruct((1024, 256), BF16),
            jax.ShapeDtypeStruct((1024, CAP), BF16),
            jax.ShapeDtypeStruct((1024, 256), BF16),
            jax.ShapeDtypeStruct((512, D), BF16),
            jax.ShapeDtypeStruct((512, D), BF16),
        ],
        scratch_shapes=[
            pltpu.VMEM((1024, D), BF16),
            pltpu.VMEM((8, 16, CAP), BF16),
            pltpu.VMEM((D, 384), BF16),
            pltpu.VMEM((256, D), BF16),
            pltpu.SemaphoreType.DMA((8,)),
            pltpu.SemaphoreType.DMA((8,)),
            pltpu.SemaphoreType.DMA((2,)),
        ],
        compiler_params=pltpu.CompilerParams(vmem_limit_bytes=32 * 1024 * 1024),
        cost_estimate=pl.CostEstimate(
            flops=2 * 1024 * D * 640 * 2, bytes_accessed=15 * 2**20, transcendentals=2**19
        ),
    )(*in_hbm(*parts), table, *in_hbm(qkv_full, out_full))


def prepare_kernel(*refs):
    parts, table, queries, key_values = refs[:8], *refs[8:11]
    probs, keys, values, folded, factors, ids, i_sems = refs[11:]
    step = pl.program_id(0)

    @pl.when(step == 0)
    def _():
        copies = id_copies(parts, ids, i_sems)
        for copy in copies:
            copy.start()
        for copy in copies:
            copy.wait()

    to_key, to_value = spreads()
    allowed, around = block_tables(ids[step], table)
    factors[...] = around
    both = key_values[...]
    keys[...] = dot_nn(both, to_key).astype(BF16)
    values[...] = dot_nn(both, to_value).astype(BF16)
    folded[...] = dot_nt(stack_heads(queries[...]), to_key).astype(BF16)
    for h, item in enumerate(softmax_heads(queries[...], keys[...], allowed)):
        probs[CAP * h : CAP * (h + 1), :] = item


def prepare_back(id_parts, table, queries, key_values):
    row = lambda i: (i, 0)
    sizes = ((512, CAP, F32), (CAP, 256, BF16), (CAP, 256, BF16), (512, CAP, BF16), (CAP, 768, F32))
    return pl.pallas_call(
        prepare_kernel,
        grid=(8,),
        in_specs=[HBM] * 8
        + [pl.BlockSpec((2, CAP, 768), lambda i: (0, 0, 0))]
        + [pl.BlockSpec((CAP, 256), row), pl.BlockSpec((CAP, CAP), row)],
        out_specs=[pl.BlockSpec((rows, lanes), row) for rows, lanes, _ in sizes],
        out_shape=[jax.ShapeDtypeStruct((8 * rows, lanes), kind) for rows, lanes, kind in sizes],
        scratch_shapes=[pltpu.VMEM((8, 16, CAP), BF16), pltpu.SemaphoreType.DMA((8,))],
        compiler_params=pltpu.CompilerParams(vmem_limit_bytes=20 * 1024 * 1024),
        cost_estimate=pl.CostEstimate(
            flops=2**30, bytes_accessed=9 * 2**20, transcendentals=2**19
        ),
    )(*in_hbm(*id_parts), table, queries, key_values)


def attend_back_kernel(*refs):
    parts, w_hbm, o_hbm = refs[:8], refs[8], refs[9]
    probs, keys, values, folded, factors = refs[10:15]
    grads, far, near, g, w, o, g_sems, w_sems = refs[15:]
    step = pl.program_id(0)
    blocks = block_copies(parts, g, g_sems)
    loads = [
        pltpu.make_async_copy(o_hbm, o, w_sems.at[0]),
        pltpu.make_async_copy(w_hbm, w, w_sems.at[1]),
    ]

    @pl.when(step == 0)
    def _():
        for copy in loads[:1] + blocks[4:] + loads[1:] + blocks[:4]:
            copy.start()
        for copy in loads[:1] + blocks[4:]:
            copy.wait()

    @pl.when(step == 1)
    def _():
        for copy in blocks[:4]:
            copy.wait()

    rows = pl.ds(pl.multiple_of((1 - step) * 512, 512), 512)
    grad_mixed = dot_nt(g[rows, :], o[...]).astype(BF16)
    to_value = spreads()[1]
    for k in range(4):
        here, heads = slice(CAP * k, CAP * (k + 1)), slice(512 * k, 512 * (k + 1))
        grad_heads = stack_heads(grad_mixed[here])
        part = dot_nt(grad_heads, values[here, :])
        prob = probs[heads, :]
        scores = (prob * (part - jnp.sum(prob * part, axis=1, keepdims=True))).astype(BF16)
        beside = jnp.concatenate([scores[CAP * h : CAP * (h + 1)] for h in range(4)], axis=1)
        grad_query = dot_nn(beside, stack_heads(keys[here, :])) * 0.125
        grad_folded = dot_nt(grad_heads, to_value).astype(BF16)
        grad_both = dot_tn(scores, folded[heads, :]) * 0.125 + dot_tn(prob.astype(BF16), grad_folded)
        item = jnp.concatenate([grad_query, grad_both], axis=1)
        grads[here, :] = turned(item, factors[here, :], -1.0).astype(BF16)

    @pl.when(step == 0)
    def _():
        loads[1].wait()

    total = dot_nt(grads[...], w[...]).astype(BF16)

    @pl.when(step == 0)
    def _():
        far[...] = total

    @pl.when(step == 1)
    def _():
        near[...] = total


def attend_back(parts, qkv_full, out_full, prepared):
    row = lambda i: (1 - i, 0)
    return pl.pallas_call(
        attend_back_kernel,
        grid=(2,),
        in_specs=[HBM] * 10
        + [
            pl.BlockSpec((2048, CAP), row),
            pl.BlockSpec((512, 256), row),
            pl.BlockSpec((512, 256), row),
            pl.BlockSpec((2048, CAP), row),
            pl.BlockSpec((512, 768), row),
        ],
        out_specs=[
            pl.BlockSpec((512, 384), row),
            pl.BlockSpec((512, D), lambda i: (0, 0)),
            pl.BlockSpec((512, D), lambda i: (0, 0)),
        ],
        out_shape=[
            jax.ShapeDtypeStruct((1024, 384), BF16),
            jax.ShapeDtypeStruct((512, D), BF16),
            jax.ShapeDtypeStruct((512, D), BF16),
        ],
        scratch_shapes=[
            pltpu.VMEM((1024, D), BF16),
            pltpu.VMEM((D, 384), BF16),
            pltpu.VMEM((256, D), BF16),
            pltpu.SemaphoreType.DMA((8,)),
            pltpu.SemaphoreType.DMA((2,)),
        ],
        compiler_params=pltpu.CompilerParams(vmem_limit_bytes=36 * 1024 * 1024),
        cost_estimate=pl.CostEstimate(
            flops=2 * 1024 * D * 640 * 2, bytes_accessed=15 * 2**20, transcendentals=0
        ),
    )(*in_hbm(*parts, qkv_full, out_full), *prepared)


def out_grads_kernel(*refs):
    parts, mixed_hbm, out, g, mixed, sems, in_sems = refs[:8], *refs[8:]
    copies = block_copies(parts, g, sems)
    copies.append(pltpu.make_async_copy(mixed_hbm, mixed, in_sems.at[0]))
    for copy in copies:
        copy.start()
    for copy in copies:
        copy.wait()
    out[...] = dot_tn(mixed[...], g[...]).astype(BF16)


def out_grads(parts, mixed):
    return pl.pallas_call(
        out_grads_kernel,
        in_specs=[HBM] * 9,
        out_specs=pl.BlockSpec(memory_space=pltpu.VMEM),
        out_shape=jax.ShapeDtypeStruct((256, D), BF16),
        scratch_shapes=[
            pltpu.VMEM((1024, D), BF16),
            pltpu.VMEM((1024, 256), BF16),
            pltpu.SemaphoreType.DMA((8,)),
            pltpu.SemaphoreType.DMA((1,)),
        ],
        compiler_params=pltpu.CompilerParams(vmem_limit_bytes=24 * 1024 * 1024),
        cost_estimate=pl.CostEstimate(
            flops=2 * 1024 * D * 256, bytes_accessed=6 * 2**20, transcendentals=0
        ),
    )(*in_hbm(*parts, mixed))


def qkv_grads_kernel(*refs):
    parts, grads_hbm, out, x, grads, sems, in_sems = refs[:8], *refs[8:]
    copies = block_copies(parts, x, sems)
    copies.append(pltpu.make_async_copy(grads_hbm, grads, in_sems.at[0]))
    for copy in copies:
        copy.start()
    for copy in copies:
        copy.wait()
    for k in range(8):
        out[k // 4, k % 4] = dot_tn(x[:, 256 * k : 256 * (k + 1)], grads[...]).astype(BF16)


def qkv_grads(parts, grads):
    return pl.pallas_call(
        qkv_grads_kernel,
        in_specs=[HBM] * 9,
        out_specs=pl.BlockSpec(memory_space=pltpu.VMEM),
        out_shape=jax.ShapeDtypeStruct((2, 4, 256, 384), BF16),
        scratch_shapes=[
            pltpu.VMEM((1024, D), BF16),
            pltpu.VMEM((1024, 384), BF16),
            pltpu.SemaphoreType.DMA((8,)),
            pltpu.SemaphoreType.DMA((1,)),
        ],
        compiler_params=pltpu.CompilerParams(vmem_limit_bytes=24 * 1024 * 1024),
        cost_estimate=pl.CostEstimate(
            flops=2 * 1024 * D * 384, bytes_accessed=6 * 2**20, transcendentals=0
        ),
    )(*in_hbm(*parts, grads))


def norm_back_kernel(own, one, two, three, rows, upstream, grad, low):
    x = rows[...]
    inner = own[...] + one[...].astype(F32) + two[...].astype(F32) + three[...].astype(F32)
    scale = lax.rsqrt(jnp.mean(x * x, axis=1, keepdims=True) + norm_eps)
    slope = jnp.mean(inner * x, axis=1, keepdims=True)
    total = upstream[...].astype(F32) + scale * inner - x * (scale * scale * scale * slope)
    grad[...] = total
    low[...] = total.astype(BF16)


def norm_back_sum(own, came, rows, upstream):
    spec = pl.BlockSpec((32, D), lambda i: (i, 0))
    return pl.pallas_call(
        norm_back_kernel,
        grid=(CAP // 32,),
        in_specs=[spec] * 6,
        out_specs=[spec] * 2,
        out_shape=[pltpu.HBM((CAP, D), F32), pltpu.HBM((CAP, D), BF16)],
        compiler_params=pltpu.CompilerParams(vmem_limit_bytes=16 * 1024 * 1024),
        cost_estimate=pl.CostEstimate(
            flops=20 * CAP * D, bytes_accessed=6 * 2**20, transcendentals=CAP
        ),
    )(*in_hbm(own, *came, rows, upstream))


def times(left, right):
    return jnp.dot(left, right, preferred_element_type=F32)


def times_t(left, right):
    return lax.dot_general(left, right, (((1,), (1,)), ((), ())), preferred_element_type=F32)


def t_times(left, right):
    return lax.dot_general(left, right, (((0,), (0,)), ((), ())), preferred_element_type=F32)


def rms_scale(rows):
    return lax.rsqrt(jnp.mean(rows * rows, axis=-1, keepdims=True) + norm_eps)


def norm_back(rows, scale, inner):
    return scale * inner - rows * (scale * scale * scale) * jnp.mean(
        inner * rows, axis=-1, keepdims=True
    )


def from_ring(item, step):
    return lax.ppermute(item, RING, [(i, (i - step) % 4) for i in range(4)])


def to_ring(item, step):
    return lax.ppermute(item, RING, [(i, (i + step) % 4) for i in range(4)])


def swap(item, axis):
    return lax.ppermute(item, axis, SWAP)


def share_parts(item, *first):
    own = swap(item, "c")
    ring = after(tuple(from_ring(item, step) for step in STEPS[1:]), *first)
    return [item, *ring, own] + [swap(part, "c") for part in ring]


def pair_blocks(near, far, *first):
    far = after(swap(far, "c"), *first)

    def block(spot):
        here = slice(spot * CAP, (spot + 1) * CAP)
        return near[here].astype(F32) + far[here].astype(F32)

    return (block(0),) + tuple(block(spot).astype(BF16) for spot in (1, 2, 3))


def ring_sum(blocks, *first):
    came = tuple(to_ring(blocks[spot], STEPS[spot]) for spot in (1, 2, 3))
    return blocks[0] + sum(item.astype(F32) for item in after(came, *first))


def spread_columns(chunks, xl, c):
    mine = [jnp.where(c == 0, pair[0], pair[1]) for pair in chunks]
    away = [jnp.where(c == 0, pair[1], pair[0]) for pair in chunks]
    came = swap(jnp.concatenate(away, axis=0), "c")
    rows = mine[0].shape[0]
    both = []
    for k in range(2):
        other = came[k * rows : (k + 1) * rows]
        both.append(
            jnp.concatenate(
                [jnp.where(c == 0, mine[k], other), jnp.where(c == 0, other, mine[k])], axis=0
            )
        )
    kept = jnp.where(xl == 0, both[0], both[1])
    came = swap(jnp.where(xl == 0, both[1], both[0]), "xl")
    return jnp.stack([jnp.where(xl == 0, kept, came), jnp.where(xl == 0, came, kept)])


def gather_four(item, axis, spot, dim):
    parts = [item]
    for step in (1, 2, 3):
        parts.append(lax.ppermute(item, axis, [(i, (i - step) % 4) for i in range(4)]))
    return jnp.stack([pick(parts, (q - spot) % 4) for q in range(4)], axis=dim)


def pick(parts, which):
    out = parts[0]
    for k in range(1, len(parts)):
        out = jnp.where(which == k, parts[k], out)
    return out


def four_pieces(item, spot, dim):
    return [
        lax.dynamic_index_in_dim(item, (spot + step) % 4, dim, keepdims=False) for step in range(4)
    ]


def shifted(item, axis, step):
    return lax.ppermute(item, axis, [(i, (i + step) % 4) for i in range(4)])


def exchange(pieces, axis):
    return tuple(shifted(pieces[step], axis, step) for step in (1, 2, 3))


def four_sum(pieces, came):
    return pieces[0].astype(F32) + sum(item.astype(F32) for item in came)


def row_pairs(step, back):
    pairs = []
    for h in range(2):
        for e in range(2):
            first = 2 * h + e
            one = (h * 4 + first) * 2 + e
            other = (h * 4 + (first + step) % 4) * 2 + e
            pairs.append((other, one) if back else (one, other))
    return pairs


def after(item, *others):
    return lax.optimization_barrier((item,) + others)[0] if others else item


def order_of_columns(xh):
    place = jnp.arange(768)
    core, owner, row = place // 384, (place % 384) // 48, place % 48
    origin = jnp.where(row < 44, 176 * owner + 88 * core + 44 * xh + row, -1)
    return (jnp.arange(1408)[:, None] == origin[None, :]).astype(BF16)


def column_part(item, width, xh):
    out = []
    for k in range(2):
        start = 2 * width * k
        out.append(
            jnp.where(
                xh == 0, item[:, start : start + width], item[:, start + width : start + 2 * width]
            )
        )
    return out


def on_device(
    tokens,
    doc_ids,
    first_gain,
    query_weight,
    key_weight,
    value_weight,
    out_weight,
    second_gain,
    gate_weight,
    up_weight,
    down_weight,
    cotangent,
):
    xh, xl, y, z, c = (lax.axis_index(name) for name in ("xh", "xl", "y", "z", "c"))
    first_col = first_gain.astype(F32)[:, None]
    second_col = second_gain.astype(F32)[:, None]

    def scaled(item, gain):
        return (item.astype(F32) * gain).astype(BF16)

    q_parts = column_part(scaled(query_weight, first_col), 512, xh)
    k_parts = column_part(scaled(key_weight, first_col), 64, xh)
    v_parts = column_part(scaled(value_weight, first_col), 64, xh)
    chunks = [
        [
            jnp.concatenate([q_parts[k][:, 256 * j : 256 * (j + 1)], k_parts[k], v_parts[k]], axis=1)
            for j in range(2)
        ]
        for k in range(2)
    ]
    spread = spread_columns(chunks, xl, c)

    qkv_full = lax.all_gather(spread, ("y", "z"), axis=1, tiled=True).reshape(D, 384)

    wide = jnp.stack([scaled(gate_weight, second_col), scaled(up_weight, second_col)])
    blocks = jnp.concatenate([wide[:, :, 1408 * k : 1408 * (k + 1)] for k in range(4)], axis=0)
    sorted_columns = times(blocks.reshape(256, 1408), order_of_columns(xh)).astype(BF16)
    sorted_columns = sorted_columns.reshape(2, 2, 2, 32, 768)
    chunks = [
        [
            jnp.concatenate(
                [
                    sorted_columns[k, h, item, :, 384 * j : 384 * (j + 1)]
                    for item in range(2)
                    for h in range(2)
                ],
                axis=1,
            )
            for j in range(2)
        ]
        for k in range(2)
    ]
    down_half = jnp.where(xh == 0, down_weight[:44], down_weight[44:])
    down_half = jnp.pad(down_half, ((0, 4), (0, 0)))
    corner = jnp.concatenate(
        [down_half[16 * k : 16 * (k + 1), 2 * WIDE :] for k in range(3)], axis=1
    )
    feed_spread = spread_columns(chunks, xl, c).reshape(128, 2 * WIDE)
    packed = jnp.concatenate([feed_spread, down_half[:, : 2 * WIDE], corner], axis=0)

    source = 2 * xh + c
    came = swap(out_weight, "c")
    head = jnp.concatenate(
        [jnp.where(c == 0, out_weight, came), jnp.where(c == 0, came, out_weight)], axis=0
    )
    lines = [head]
    for step in (1, 2, 3):
        lines.append(lax.ppermute(head, ("xh", "y", "c"), row_pairs(step, False)))
    head = pick(lines, (y - source) % 4)
    out_full = gather_four(head, "z", z, 0).reshape(256, D)

    table = rotary_table()
    rows = tokens.astype(F32)
    first_scale = rms_scale(rows)
    id_rows = jnp.pad(doc_ids.astype(BF16)[None], ((0, 15), (0, D - CAP)))
    payload = jnp.concatenate([(rows * first_scale).astype(BF16), id_rows], axis=0)
    first = share_parts(after(payload, spread, feed_spread))
    packed = after(packed, qkv_full, out_full, *first[1:4])
    packed = lax.all_gather(packed, ("y", "z"), axis=0, tiled=True)

    queries, key_values, mixed, far, near = attend(first, table, qkv_full, out_full)
    upstream = share_parts(after(cotangent, *first[1:4]), mixed)
    far = after(far, upstream[1])
    shuffle = after(jnp.concatenate([order_of_columns(0), order_of_columns(1)], axis=1), mixed)
    blocks = pair_blocks(near, far)
    prepared = prepare_back(first, table, after(queries, *blocks), key_values)
    midway = rows + ring_sum(blocks, shuffle, *prepared)

    second_scale = rms_scale(midway)
    back = feed_back(upstream, packed)
    second = share_parts((midway * second_scale).astype(BF16), back)
    hidden, grad_feed, far, near = feed_forward(second, packed, back)
    blocks = pair_blocks(near, far)
    pack = feed_grads(second, upstream, after(hidden, *blocks), grad_feed)
    came = tuple(to_ring(blocks[spot], STEPS[spot]) for spot in (1, 2, 3))
    out_far, out_near = output_product(after(hidden, pack), packed)
    grad_mid, grad_low = norm_back_sum(blocks[0], after(came, pack, out_far), midway, cotangent)
    out_blocks = pair_blocks(out_near, after(out_far, grad_low))
    third = share_parts(grad_low, *out_blocks)
    pack = lax.psum_scatter(after(pack, *came, out_far), ("y", "z"), scatter_dimension=0, tiled=True)

    out_term = out_grads(third, mixed).reshape(4, 64, D)
    out_sent = four_pieces(out_term, z, 0)
    out_came = tuple(shifted(out_sent[step], "z", step) for step in (1, 2))
    grad_qkv, far, near = attend_back(
        third, qkv_full, after(out_full, *out_sent, *out_blocks), prepared
    )
    product = ring_sum(out_blocks, grad_qkv)
    output = (midway + product).astype(BF16)
    out_came += (shifted(after(out_sent[3], grad_qkv), "z", 3),)
    out_part = four_sum(out_sent, after(out_came, product))
    far = after(far, out_part)
    sent = out_part.astype(BF16)
    out_came = tuple(
        lax.ppermute(sent, ("xh", "y", "c"), row_pairs(step, True)) for step in (1, 2, 3)
    )
    qkv_term = qkv_grads(first, after(grad_qkv, sent))
    blocks = pair_blocks(near, far, qkv_term)
    out_came = after(out_came, *blocks)
    out_part = (out_part + sum(item.astype(F32) for item in out_came)).astype(BF16)

    def halves(item):
        low, high = item[:, :32], item[:, 32:]
        return jnp.where(c == 0, low, high), jnp.where(c == 0, high, low)

    sent = four_pieces(after(qkv_term, out_part, *blocks), y, 1)
    came = exchange(sent, "y")
    ring_came = (to_ring(blocks[1], STEPS[1]), to_ring(blocks[2], STEPS[2]))
    corner = jnp.concatenate([pack[176:, 512 * k : 512 * (k + 1)] for k in range(3)], axis=0)
    down_part = jnp.concatenate([pack[128:176], corner], axis=1)
    feed_part = pack[:128].reshape(2, 64, 2 * WIDE)
    feed_mine, feed_away = halves(feed_part)
    came, ring_came, feed_mine, feed_away, down_part = lax.optimization_barrier(
        (came, ring_came, feed_mine, feed_away, down_part)
    )
    sent = four_pieces(four_sum(sent, came).astype(BF16).reshape(2, 4, 64, 384), z, 1)
    came = exchange(sent, "z")
    last_came = to_ring(blocks[3], STEPS[3])
    feed_came = swap(feed_away, "c")
    came, last_came, feed_came = lax.optimization_barrier((came, last_came, feed_came))

    def in_order(mine, came):
        return jnp.where(c == 0, mine, came), jnp.where(c == 0, came, mine)

    def along_ring(both, more):
        here = jnp.where(xl == 0, both[0], both[1])
        there = jnp.where(xl == 0, both[1], both[0])
        across = jnp.concatenate([here, more], axis=1)
        return here, (to_ring(there, 1), to_ring(across, 2), to_ring(there, 3))

    def by_chip(here, came):
        width, spot = here.shape[1], 2 * xh + xl
        stacked = [here, came[0], came[1][:, :width], came[2]]
        return [[pick(stacked, (spot - (2 * h + k)) % 4) for h in range(2)] for k in range(2)]

    down_wide = jnp.concatenate(
        [down_part[:32], jnp.concatenate([down_part[32:, :1024], down_part[32:, 1024:]], axis=0)],
        axis=1,
    )
    feed_here, feed_came = along_ring(
        jnp.concatenate(in_order(feed_mine, feed_came), axis=2), down_wide
    )

    qkv_part = four_sum(sent, came).astype(BF16)
    qkv_mine, qkv_away = halves(qkv_part)
    away = jnp.where(c == 0, out_part[32:], out_part[:32])
    sent = jnp.concatenate(
        [
            qkv_away.reshape(64, 384),
            jnp.concatenate([away[:, :1024], away[:, 1024:]], axis=0),
        ],
        axis=1,
    )
    came = swap(sent, "c")
    zero, one = in_order(qkv_mine, came[:, :384].reshape(2, 32, 384))
    pair = zero[:, :, 256:].astype(F32) + one[:, :, 256:].astype(F32)
    both = jnp.concatenate([zero[:, :, :256], one[:, :, :256], pair.astype(BF16)], axis=2)
    out_half = jnp.where(
        y % 2 == c,
        jnp.where(c == 0, out_part[:32], out_part[32:]),
        jnp.concatenate([came[:32, 384:], came[32:, 384:]], axis=1),
    )
    both, out_half = lax.optimization_barrier((both, out_half))
    qkv_here, came = along_ring(both, out_half)
    feed_came = after(feed_came, both)

    inner_one = blocks[0] + sum(item.astype(F32) for item in ring_came + (last_came,))
    tokens_grad = grad_mid + norm_back(rows, first_scale, inner_one)
    parts = by_chip(feed_here, feed_came)
    down_other = feed_came[1][:, 3072:]
    down_other = jnp.concatenate(
        [
            down_other[:, :2048],
            jnp.concatenate([down_other[:16, 2048:], down_other[16:, 2048:]], axis=1),
        ],
        axis=0,
    )
    down_grad = jnp.concatenate(
        [
            jnp.where(xh == 0, down_part, down_other)[:44],
            jnp.where(xh == 0, down_other, down_part)[:44],
        ],
        axis=0,
    ).astype(F32)
    rows_of = []
    for item in range(2):
        for k in range(2):
            for half in range(2):
                start = item * WIDE + half * 384
                rows_of.append(
                    jnp.concatenate(
                        [
                            parts[k][h][:, e * 2 * WIDE + start : e * 2 * WIDE + start + 384]
                            for h in range(2)
                            for e in range(2)
                        ],
                        axis=1,
                    )
                )
    unsorted = times_t(jnp.concatenate(rows_of, axis=0), shuffle).reshape(2, 4, 32, 1408)
    gate_raw = jnp.concatenate([unsorted[0, k] for k in range(4)], axis=1)
    up_raw = jnp.concatenate([unsorted[1, k] for k in range(4)], axis=1)
    second_grad = jnp.sum(gate_raw * gate_weight.astype(F32), axis=1) + jnp.sum(
        up_raw * up_weight.astype(F32), axis=1
    )

    parts = by_chip(qkv_here, came)
    out_grad = jnp.where(y // 2 == xh, out_half, came[1][:, 640:]).astype(F32)

    def joined(start, end):
        return jnp.concatenate(
            [parts[k][h][:, start:end] for k in range(2) for h in range(2)], axis=1
        ).astype(F32)

    query_raw, key_raw, value_raw = joined(0, 512), joined(512, 576), joined(576, 640)
    first_grad = (
        jnp.sum(query_raw * query_weight.astype(F32), axis=1)
        + jnp.sum(key_raw * key_weight.astype(F32), axis=1)
        + jnp.sum(value_raw * value_weight.astype(F32), axis=1)
    )

    return (
        output,
        tokens_grad,
        first_grad,
        query_raw * first_col,
        key_raw * first_col,
        value_raw * first_col,
        out_grad,
        second_grad,
        gate_raw * second_col,
        up_raw * second_col,
        down_grad,
    )


def solution(mesh):
    fine = Mesh(mesh.devices.reshape(2, 2, 4, 4, 2), ("xh", "xl", "y", "z", "c"))
    everyone = ("xh", "xl", "y", "z", "c")
    group = ("xl", "y", "z", "c")
    in_specs = (
        P(everyone, None),
        P(everyone),
        P(group),
        P(group, None),
        P(group, None),
        P(group, None),
        P(group, None),
        P(group),
        P(group, None),
        P(group, None),
        P(group, None),
        P(everyone, None),
    )
    out_specs = (
        P(everyone, None),
        P(everyone, None),
        P(group),
        P(group, None),
        P(group, None),
        P(group, None),
        P(group, None),
        P(group),
        P(group, None),
        P(group, None),
        P(group, None),
    )
    return jax.shard_map(
        on_device, mesh=fine, in_specs=in_specs, out_specs=out_specs, check_vma=False
    )
```

```python
import jax
import jax.numpy as jnp
import ml_dtypes
import numpy as np
from jax import lax
from jax.experimental import pallas as pl
from jax.experimental.pallas import tpu as pltpu
from jax.sharding import Mesh, PartitionSpec as P

D = 2048
HDIM = 64
CAP = 128
WIDE = 768
BF16 = jnp.bfloat16
F32 = jnp.float32

norm_eps = 1e-05

RING = ("xh", "xl")
SWAP = [(0, 1), (1, 0)]
STEPS = (0, 1, 3, 2)


def dot_nn(left, right):
    return lax.dot_general(left, right, (((1,), (0,)), ((), ())), preferred_element_type=F32)


def dot_nt(left, right):
    return lax.dot_general(left, right, (((1,), (1,)), ((), ())), preferred_element_type=F32)


def dot_tn(left, right):
    return lax.dot_general(left, right, (((0,), (0,)), ((), ())), preferred_element_type=F32)


HBM = pl.BlockSpec(memory_space=pltpu.HBM)


def in_hbm(*items):
    return [pltpu.with_memory_space_constraint(item, pltpu.HBM) for item in items]


def block_copies(parts, whole, sems):
    return [
        pltpu.make_async_copy(
            part.at[pl.ds(0, CAP)], whole.at[pl.ds(CAP * spot, CAP)], sems.at[spot]
        )
        for spot, part in enumerate(parts)
    ]


def id_copies(parts, ids, sems):
    return [
        pltpu.make_async_copy(part.at[pl.ds(CAP, 16), pl.ds(0, CAP)], ids.at[spot], sems.at[spot])
        for spot, part in enumerate(parts)
    ]


def feed_copies(packed, feed, sems):
    copies = []
    for k in range(16):
        for h in range(2):
            copies.append(
                pltpu.make_async_copy(
                    packed.at[pl.ds(192 * k + 64 * h, 64)],
                    feed.at[pl.ds(1024 * h + 64 * k, 64)],
                    sems.at[2 * k + h],
                )
            )
    return copies


def down_copies(packed, down, sems):
    copies = []
    for k in range(16):
        copies.append(
            pltpu.make_async_copy(
                packed.at[pl.ds(192 * k + 128, 48)],
                down.at[pl.ds(48 * k, 48), pl.ds(0, 1536)],
                sems.at[4 * k],
            )
        )
        for h in range(3):
            copies.append(
                pltpu.make_async_copy(
                    packed.at[pl.ds(192 * k + 176, 16), pl.ds(512 * h, 512)],
                    down.at[pl.ds(48 * k + 16 * h, 16), pl.ds(1536, 512)],
                    sems.at[4 * k + 1 + h],
                )
            )
    return copies


def back_kernel(*refs):
    parts, packed, out, down_out, c, down, c_sems, d_sems, out_sems = refs[:8], *refs[8:]
    step = pl.program_id(0)
    loads = block_copies(parts, c, c_sems)
    keep = pltpu.make_async_copy(down, down_out, out_sems.at[0])

    @pl.when(step == 0)
    def _():
        rows = down_copies(packed, down, d_sems)
        for copy in loads[:4] + rows + loads[4:]:
            copy.start()
        for copy in loads[:4] + rows:
            copy.wait()
        keep.start()

    @pl.when(step == 1)
    def _():
        for copy in loads[4:]:
            copy.wait()

    rows = pl.ds(pl.multiple_of(step * 512, 512), 512)
    out[...] = dot_nt(c[rows, :], down[...])

    @pl.when(step == 1)
    def _():
        keep.wait()


def feed_back(c_parts, packed):
    return pl.pallas_call(
        back_kernel,
        grid=(2,),
        in_specs=[HBM] * 9,
        out_specs=[pl.BlockSpec((512, WIDE), lambda i: (i, 0)), HBM],
        out_shape=[jax.ShapeDtypeStruct((1024, WIDE), F32), pltpu.HBM((WIDE, D), BF16)],
        scratch_shapes=[
            pltpu.VMEM((1024, D), BF16),
            pltpu.VMEM((WIDE, D), BF16),
            pltpu.SemaphoreType.DMA((8,)),
            pltpu.SemaphoreType.DMA((64,)),
            pltpu.SemaphoreType.DMA((1,)),
        ],
        compiler_params=pltpu.CompilerParams(vmem_limit_bytes=24 * 1024 * 1024),
        cost_estimate=pl.CostEstimate(
            flops=2 * 1024 * D * WIDE, bytes_accessed=10 * 2**20, transcendentals=0
        ),
    )(*in_hbm(*c_parts, packed))


def feed_kernel(*refs):
    x_parts, packed, back = refs[:8], refs[8], refs[9]
    hidden, grads, far, near, x, feed, x_sems, f_sems = refs[10:]
    step = pl.program_id(0)
    first = block_copies(x_parts, x, x_sems)

    @pl.when(step == 0)
    def _():
        second = feed_copies(packed, feed, f_sems)
        for copy in first[4:6] + second + first[6:] + first[:4]:
            copy.start()
        for copy in first[4:6] + second:
            copy.wait()

    for k in range(1, 4):

        @pl.when(step == k)
        def _(k=k):
            spot = (2 * k + 4) % 8
            for copy in first[spot : spot + 2]:
                copy.wait()

    rows = pl.ds(pl.multiple_of(((step + 2) % 4) * 256, 256), 256)
    block = x[rows, :]
    for k in range(0, WIDE, 256):
        here, beside = slice(k, k + 256), slice(WIDE + k, WIDE + k + 256)
        gate = dot_nn(block, feed[:, here])
        up = dot_nn(block, feed[:, beside])
        slope = back[:, here]
        sig = jax.nn.sigmoid(gate)
        silu = gate * sig
        hidden[:, here] = (silu * up).astype(BF16)
        grads[:, here] = (slope * up * (sig * (1.0 + gate * (1.0 - sig)))).astype(BF16)
        grads[:, beside] = (slope * silu).astype(BF16)
    inner = dot_nt(grads[...], feed[...])

    @pl.when(step < 2)
    def _():
        far[...] = inner.astype(BF16)

    @pl.when(step >= 2)
    def _():
        near[...] = inner.astype(BF16)


def feed_forward(x_parts, packed, back):
    row = lambda i: ((i + 2) % 4, 0)
    return pl.pallas_call(
        feed_kernel,
        grid=(4,),
        in_specs=[HBM] * 9 + [pl.BlockSpec((256, WIDE), row)],
        out_specs=[
            pl.BlockSpec((256, WIDE), row),
            pl.BlockSpec((256, 2 * WIDE), row),
            pl.BlockSpec((256, D), lambda i: (jnp.minimum(i, 1), 0)),
            pl.BlockSpec((256, D), lambda i: (jnp.maximum(i - 2, 0), 0)),
        ],
        out_shape=[
            jax.ShapeDtypeStruct((1024, WIDE), BF16),
            jax.ShapeDtypeStruct((1024, 2 * WIDE), BF16),
            jax.ShapeDtypeStruct((512, D), BF16),
            jax.ShapeDtypeStruct((512, D), BF16),
        ],
        scratch_shapes=[
            pltpu.VMEM((1024, D), BF16),
            pltpu.VMEM((D, 2 * WIDE), BF16),
            pltpu.SemaphoreType.DMA((8,)),
            pltpu.SemaphoreType.DMA((32,)),
        ],
        compiler_params=pltpu.CompilerParams(vmem_limit_bytes=36 * 1024 * 1024),
        cost_estimate=pl.CostEstimate(
            flops=2 * 1024 * D * WIDE * 4, bytes_accessed=24 * 2**20, transcendentals=1024 * WIDE
        ),
    )(*in_hbm(*x_parts, packed), back)


def grads_kernel(*refs):
    x_parts, c_parts, hidden_hbm, grads_hbm = refs[:8], refs[8:16], refs[16], refs[17]
    out = refs[18]
    x, c, hidden, grads, pack, x_sems, c_sems, in_sems, sems = refs[19:]
    first = block_copies(x_parts, x, x_sems)
    second = block_copies(c_parts, c, c_sems)
    loads = [
        pltpu.make_async_copy(grads_hbm, grads, in_sems.at[0]),
        pltpu.make_async_copy(hidden_hbm, hidden, in_sems.at[1]),
    ]
    for copy in first + loads + second:
        copy.start()
    for copy in first + loads[:1]:
        copy.wait()
    stores = []

    def store(row, rows):
        copy = pltpu.make_async_copy(
            pack.at[pl.ds(row, rows)], out.at[pl.ds(row, rows)], sems.at[len(stores)]
        )
        copy.start()
        stores.append(copy)

    for k in range(8):
        tile = dot_tn(x[:, 256 * k : 256 * (k + 1)], grads[...]).astype(BF16)
        half, spot = k // 4, (k % 4) * 4
        for j in range(4):
            row = 192 * (spot + j) + 64 * half
            pack[row : row + 64, :] = tile[64 * j : 64 * (j + 1)]
            store(row, 64)
    for copy in second + loads[1:]:
        copy.wait()
    for k in range(2):
        tile = dot_tn(hidden[:, 384 * k : 384 * (k + 1)], c[...]).astype(BF16)
        for j in range(8):
            row = 192 * (8 * k + j) + 128
            piece = tile[48 * j : 48 * (j + 1)]
            pack[row : row + 48, :] = piece[:, :1536]
            for h in range(3):
                pack[row + 48 : row + 64, 512 * h : 512 * (h + 1)] = piece[
                    16 * h : 16 * (h + 1), 1536:
                ]
            store(row, 64)
    for copy in stores:
        copy.wait()


def feed_grads(x_parts, c_parts, hidden, grads):
    return pl.pallas_call(
        grads_kernel,
        in_specs=[HBM] * 18,
        out_specs=HBM,
        out_shape=jax.ShapeDtypeStruct((3072, 1536), BF16),
        scratch_shapes=[
            pltpu.VMEM((1024, D), BF16),
            pltpu.VMEM((1024, D), BF16),
            pltpu.VMEM((1024, WIDE), BF16),
            pltpu.VMEM((1024, 2 * WIDE), BF16),
            pltpu.VMEM((3072, 2 * WIDE), BF16),
            pltpu.SemaphoreType.DMA((8,)),
            pltpu.SemaphoreType.DMA((8,)),
            pltpu.SemaphoreType.DMA((2,)),
            pltpu.SemaphoreType.DMA((48,)),
        ],
        compiler_params=pltpu.CompilerParams(vmem_limit_bytes=60 * 1024 * 1024),
        cost_estimate=pl.CostEstimate(
            flops=2 * 1024 * D * WIDE * 3, bytes_accessed=22 * 2**20, transcendentals=0
        ),
    )(*in_hbm(*x_parts, *c_parts, hidden, grads))


def output_kernel(hidden_hbm, down_hbm, far, near, hidden, down, total, sems, out_sems):
    copies = [
        pltpu.make_async_copy(down_hbm, down, sems.at[0]),
        pltpu.make_async_copy(hidden_hbm, hidden, sems.at[1]),
    ]
    for copy in copies:
        copy.start()
    for copy in copies:
        copy.wait()
    stores = []
    for k, out in ((1, far), (0, near)):
        total[k] = dot_nn(hidden[512 * k : 512 * (k + 1)], down[...]).astype(BF16)
        stores.append(pltpu.make_async_copy(total.at[k], out, out_sems.at[k]))
        stores[-1].start()
    for copy in stores:
        copy.wait()


def output_product(hidden, down_full):
    return pl.pallas_call(
        output_kernel,
        in_specs=[HBM, HBM],
        out_specs=[HBM, HBM],
        out_shape=[pltpu.HBM((512, D), BF16), pltpu.HBM((512, D), BF16)],
        scratch_shapes=[
            pltpu.VMEM((1024, WIDE), BF16),
            pltpu.VMEM((WIDE, D), BF16),
            pltpu.VMEM((2, 512, D), BF16),
            pltpu.SemaphoreType.DMA((2,)),
            pltpu.SemaphoreType.DMA((2,)),
        ],
        compiler_params=pltpu.CompilerParams(vmem_limit_bytes=24 * 1024 * 1024),
        cost_estimate=pl.CostEstimate(
            flops=2 * 1024 * D * WIDE, bytes_accessed=11 * 2**20, transcendentals=0
        ),
    )(*in_hbm(hidden, down_full))


def rotary_table():
    place = np.arange(CAP, dtype=np.float32)[:, None]
    inverse = np.float32(10000.0) ** (np.arange(32, dtype=np.float32) * np.float32(-2.0 / HDIM))
    angle = (place * inverse).astype(np.float32)
    cosine, sine = np.cos(angle), np.sin(angle)
    zero, one = np.zeros((CAP, 64), np.float32), np.ones((CAP, 64), np.float32)
    ahead = np.concatenate([-sine, zero[:, :32]], axis=1)
    behind = np.concatenate([zero[:, :32], sine], axis=1)
    cosine = np.concatenate([cosine, cosine], axis=1)
    table = np.concatenate(
        [cosine, cosine, ahead, ahead, behind, behind, cosine, one, ahead, zero, behind, zero], axis=1
    )
    high = table.astype(ml_dtypes.bfloat16)
    rest = (table - high.astype(np.float32)).astype(ml_dtypes.bfloat16)
    return jnp.asarray(np.stack([high, rest]))


def lane_of(shape, dim):
    return lax.broadcasted_iota(jnp.int32, shape, dim)


def block_tables(ids, table):
    row = jnp.broadcast_to(ids.astype(F32)[:1], (CAP, CAP))
    same = row == row.T
    to, frm = lane_of((CAP, CAP), 0), lane_of((CAP, CAP), 1)
    place = jnp.sum(jnp.where(same & (frm < to), 1.0, 0.0), axis=1, keepdims=True)
    chosen = (frm.astype(F32) == place).astype(BF16)
    factors = dot_nn(chosen, table[0]) + dot_nn(chosen, table[1])
    return same & (frm <= to), factors


def turned(item, factors, sign):
    def three(k):
        pair = factors[:, CAP * k : CAP * (k + 1)]
        return jnp.concatenate([pair, pair, factors[:, CAP * (k + 3) : CAP * (k + 4)]], axis=1)

    other = pltpu.roll(item, 352, 1) * three(1) + pltpu.roll(item, 32, 1) * three(2)
    return item * three(0) + sign * other


def stack_heads(item):
    head = lane_of((CAP, 256), 1) // 64
    return jnp.concatenate([jnp.where(head == h, item, 0).astype(BF16) for h in range(4)], axis=0)


def spreads():
    lane, own = lane_of((CAP, 256), 1) % 64, lane_of((CAP, 256), 0)
    return (lane == own).astype(BF16), (lane + 64 == own).astype(BF16)


def softmax_heads(queries, keys, allowed):
    scores = dot_nt(stack_heads(queries), keys) * 0.125
    out = []
    for h in range(4):
        part = jnp.where(allowed, scores[CAP * h : CAP * (h + 1)], -1e30)
        expo = jnp.exp(part - jnp.max(part, axis=1, keepdims=True))
        out.append(expo / jnp.sum(expo, axis=1, keepdims=True))
    return out


def attend_kernel(*refs):
    parts, table, w_hbm, o_hbm = refs[:8], refs[8], refs[9], refs[10]
    queries, key_values, mixed, far, near = refs[11:16]
    x, ids, w, o, x_sems, i_sems, w_sems = refs[16:]
    step = pl.program_id(0)
    blocks, numbers = block_copies(parts, x, x_sems), id_copies(parts, ids, i_sems)
    loads = [
        pltpu.make_async_copy(w_hbm, w, w_sems.at[0]),
        pltpu.make_async_copy(o_hbm, o, w_sems.at[1]),
    ]

    @pl.when(step == 0)
    def _():
        for copy in loads[:1] + blocks[4:] + numbers[4:] + loads[1:] + blocks[:4] + numbers[:4]:
            copy.start()
        for copy in loads[:1] + blocks[4:] + numbers[4:]:
            copy.wait()

    @pl.when(step == 1)
    def _():
        for copy in blocks[:4] + numbers[:4]:
            copy.wait()

    half = 1 - step
    rows = pl.ds(pl.multiple_of(half * 512, 512), 512)
    qkv = dot_nn(x[rows, :], w[...])
    to_key, to_value = spreads()
    for k in range(4):
        allowed, factors = block_tables(ids[half * 4 + k], table)
        block = turned(qkv[CAP * k : CAP * (k + 1)], factors, 1.0).astype(BF16)
        here = slice(CAP * k, CAP * (k + 1))
        queries[here, :] = block[:, :256]
        key_values[here, :] = block[:, 256:]
        keys = dot_nn(block[:, 256:], to_key).astype(BF16)
        values = dot_nn(block[:, 256:], to_value).astype(BF16)
        probs = softmax_heads(block[:, :256], keys, allowed)
        probs = jnp.concatenate([item.astype(BF16) for item in probs], axis=1)
        mixed[here, :] = dot_nn(probs, stack_heads(values)).astype(BF16)

    @pl.when(step == 0)
    def _():
        loads[1].wait()

    total = dot_nn(mixed[...], o[...])

    @pl.when(step == 0)
    def _():
        far[...] = total.astype(BF16)

    @pl.when(step == 1)
    def _():
        near[...] = total.astype(BF16)


def attend(parts, table, qkv_full, out_full):
    row = lambda i: (1 - i, 0)
    still = lambda i: (0, 0)
    return pl.pallas_call(
        attend_kernel,
        grid=(2,),
        in_specs=[HBM] * 8 + [pl.BlockSpec((2, CAP, 768), lambda i: (0, 0, 0))] + [HBM] * 2,
        out_specs=[
            pl.BlockSpec((512, 256), row),
            pl.BlockSpec((512, CAP), row),
            pl.BlockSpec((512, 256), row),
            pl.BlockSpec((512, D), still),
            pl.BlockSpec((512, D), still),
        ],
        out_shape=[
            jax.ShapeDtypeStruct((1024, 256), BF16),
            jax.ShapeDtypeStruct((1024, CAP), BF16),
            jax.ShapeDtypeStruct((1024, 256), BF16),
            jax.ShapeDtypeStruct((512, D), BF16),
            jax.ShapeDtypeStruct((512, D), BF16),
        ],
        scratch_shapes=[
            pltpu.VMEM((1024, D), BF16),
            pltpu.VMEM((8, 16, CAP), BF16),
            pltpu.VMEM((D, 384), BF16),
            pltpu.VMEM((256, D), BF16),
            pltpu.SemaphoreType.DMA((8,)),
            pltpu.SemaphoreType.DMA((8,)),
            pltpu.SemaphoreType.DMA((2,)),
        ],
        compiler_params=pltpu.CompilerParams(vmem_limit_bytes=32 * 1024 * 1024),
        cost_estimate=pl.CostEstimate(
            flops=2 * 1024 * D * 640 * 2, bytes_accessed=15 * 2**20, transcendentals=2**19
        ),
    )(*in_hbm(*parts), table, *in_hbm(qkv_full, out_full))


def prepare_kernel(*refs):
    parts, table, queries, key_values = refs[:8], *refs[8:11]
    probs, keys, values, folded, factors, ids, i_sems = refs[11:]
    step = pl.program_id(0)

    @pl.when(step == 0)
    def _():
        copies = id_copies(parts, ids, i_sems)
        for copy in copies:
            copy.start()
        for copy in copies:
            copy.wait()

    to_key, to_value = spreads()
    allowed, around = block_tables(ids[step], table)
    factors[...] = around
    both = key_values[...]
    keys[...] = dot_nn(both, to_key).astype(BF16)
    values[...] = dot_nn(both, to_value).astype(BF16)
    folded[...] = dot_nt(stack_heads(queries[...]), to_key).astype(BF16)
    for h, item in enumerate(softmax_heads(queries[...], keys[...], allowed)):
        probs[CAP * h : CAP * (h + 1), :] = item


def prepare_back(id_parts, table, queries, key_values):
    row = lambda i: (i, 0)
    sizes = ((512, CAP, F32), (CAP, 256, BF16), (CAP, 256, BF16), (512, CAP, BF16), (CAP, 768, F32))
    return pl.pallas_call(
        prepare_kernel,
        grid=(8,),
        in_specs=[HBM] * 8
        + [pl.BlockSpec((2, CAP, 768), lambda i: (0, 0, 0))]
        + [pl.BlockSpec((CAP, 256), row), pl.BlockSpec((CAP, CAP), row)],
        out_specs=[pl.BlockSpec((rows, lanes), row) for rows, lanes, _ in sizes],
        out_shape=[jax.ShapeDtypeStruct((8 * rows, lanes), kind) for rows, lanes, kind in sizes],
        scratch_shapes=[pltpu.VMEM((8, 16, CAP), BF16), pltpu.SemaphoreType.DMA((8,))],
        compiler_params=pltpu.CompilerParams(vmem_limit_bytes=20 * 1024 * 1024),
        cost_estimate=pl.CostEstimate(
            flops=2**30, bytes_accessed=9 * 2**20, transcendentals=2**19
        ),
    )(*in_hbm(*id_parts), table, queries, key_values)


def attend_back_kernel(*refs):
    parts, w_hbm, o_hbm = refs[:8], refs[8], refs[9]
    probs, keys, values, folded, factors = refs[10:15]
    grads, far, near, g, w, o, g_sems, w_sems = refs[15:]
    step = pl.program_id(0)
    blocks = block_copies(parts, g, g_sems)
    loads = [
        pltpu.make_async_copy(o_hbm, o, w_sems.at[0]),
        pltpu.make_async_copy(w_hbm, w, w_sems.at[1]),
    ]

    @pl.when(step == 0)
    def _():
        for copy in loads[:1] + blocks[4:] + loads[1:] + blocks[:4]:
            copy.start()
        for copy in loads[:1] + blocks[4:]:
            copy.wait()

    @pl.when(step == 1)
    def _():
        for copy in blocks[:4]:
            copy.wait()

    rows = pl.ds(pl.multiple_of((1 - step) * 512, 512), 512)
    grad_mixed = dot_nt(g[rows, :], o[...]).astype(BF16)
    to_value = spreads()[1]
    for k in range(4):
        here, heads = slice(CAP * k, CAP * (k + 1)), slice(512 * k, 512 * (k + 1))
        grad_heads = stack_heads(grad_mixed[here])
        part = dot_nt(grad_heads, values[here, :])
        prob = probs[heads, :]
        scores = (prob * (part - jnp.sum(prob * part, axis=1, keepdims=True))).astype(BF16)
        beside = jnp.concatenate([scores[CAP * h : CAP * (h + 1)] for h in range(4)], axis=1)
        grad_query = dot_nn(beside, stack_heads(keys[here, :])) * 0.125
        grad_folded = dot_nt(grad_heads, to_value).astype(BF16)
        grad_both = dot_tn(scores, folded[heads, :]) * 0.125 + dot_tn(prob.astype(BF16), grad_folded)
        item = jnp.concatenate([grad_query, grad_both], axis=1)
        grads[here, :] = turned(item, factors[here, :], -1.0).astype(BF16)

    @pl.when(step == 0)
    def _():
        loads[1].wait()

    total = dot_nt(grads[...], w[...]).astype(BF16)

    @pl.when(step == 0)
    def _():
        far[...] = total

    @pl.when(step == 1)
    def _():
        near[...] = total


def attend_back(parts, qkv_full, out_full, prepared):
    row = lambda i: (1 - i, 0)
    return pl.pallas_call(
        attend_back_kernel,
        grid=(2,),
        in_specs=[HBM] * 10
        + [
            pl.BlockSpec((2048, CAP), row),
            pl.BlockSpec((512, 256), row),
            pl.BlockSpec((512, 256), row),
            pl.BlockSpec((2048, CAP), row),
            pl.BlockSpec((512, 768), row),
        ],
        out_specs=[
            pl.BlockSpec((512, 384), row),
            pl.BlockSpec((512, D), lambda i: (0, 0)),
            pl.BlockSpec((512, D), lambda i: (0, 0)),
        ],
        out_shape=[
            jax.ShapeDtypeStruct((1024, 384), BF16),
            jax.ShapeDtypeStruct((512, D), BF16),
            jax.ShapeDtypeStruct((512, D), BF16),
        ],
        scratch_shapes=[
            pltpu.VMEM((1024, D), BF16),
            pltpu.VMEM((D, 384), BF16),
            pltpu.VMEM((256, D), BF16),
            pltpu.SemaphoreType.DMA((8,)),
            pltpu.SemaphoreType.DMA((2,)),
        ],
        compiler_params=pltpu.CompilerParams(vmem_limit_bytes=36 * 1024 * 1024),
        cost_estimate=pl.CostEstimate(
            flops=2 * 1024 * D * 640 * 2, bytes_accessed=15 * 2**20, transcendentals=0
        ),
    )(*in_hbm(*parts, qkv_full, out_full), *prepared)


def out_grads_kernel(*refs):
    parts, mixed_hbm, out, g, mixed, sems, in_sems = refs[:8], *refs[8:]
    copies = block_copies(parts, g, sems)
    copies.append(pltpu.make_async_copy(mixed_hbm, mixed, in_sems.at[0]))
    for copy in copies:
        copy.start()
    for copy in copies:
        copy.wait()
    out[...] = dot_tn(mixed[...], g[...]).astype(BF16)


def out_grads(parts, mixed):
    return pl.pallas_call(
        out_grads_kernel,
        in_specs=[HBM] * 9,
        out_specs=pl.BlockSpec(memory_space=pltpu.VMEM),
        out_shape=jax.ShapeDtypeStruct((256, D), BF16),
        scratch_shapes=[
            pltpu.VMEM((1024, D), BF16),
            pltpu.VMEM((1024, 256), BF16),
            pltpu.SemaphoreType.DMA((8,)),
            pltpu.SemaphoreType.DMA((1,)),
        ],
        compiler_params=pltpu.CompilerParams(vmem_limit_bytes=24 * 1024 * 1024),
        cost_estimate=pl.CostEstimate(
            flops=2 * 1024 * D * 256, bytes_accessed=6 * 2**20, transcendentals=0
        ),
    )(*in_hbm(*parts, mixed))


def qkv_grads_kernel(*refs):
    parts, grads_hbm, out, x, grads, sems, in_sems = refs[:8], *refs[8:]
    copies = block_copies(parts, x, sems)
    copies.append(pltpu.make_async_copy(grads_hbm, grads, in_sems.at[0]))
    for copy in copies:
        copy.start()
    for copy in copies:
        copy.wait()
    for k in range(8):
        out[k // 4, k % 4] = dot_tn(x[:, 256 * k : 256 * (k + 1)], grads[...]).astype(BF16)


def qkv_grads(parts, grads):
    return pl.pallas_call(
        qkv_grads_kernel,
        in_specs=[HBM] * 9,
        out_specs=pl.BlockSpec(memory_space=pltpu.VMEM),
        out_shape=jax.ShapeDtypeStruct((2, 4, 256, 384), BF16),
        scratch_shapes=[
            pltpu.VMEM((1024, D), BF16),
            pltpu.VMEM((1024, 384), BF16),
            pltpu.SemaphoreType.DMA((8,)),
            pltpu.SemaphoreType.DMA((1,)),
        ],
        compiler_params=pltpu.CompilerParams(vmem_limit_bytes=24 * 1024 * 1024),
        cost_estimate=pl.CostEstimate(
            flops=2 * 1024 * D * 384, bytes_accessed=6 * 2**20, transcendentals=0
        ),
    )(*in_hbm(*parts, grads))


def norm_back_kernel(own, one, two, three, rows, upstream, grad, low):
    x = rows[...]
    inner = own[...] + one[...].astype(F32) + two[...].astype(F32) + three[...].astype(F32)
    scale = lax.rsqrt(jnp.mean(x * x, axis=1, keepdims=True) + norm_eps)
    slope = jnp.mean(inner * x, axis=1, keepdims=True)
    total = upstream[...].astype(F32) + scale * inner - x * (scale * scale * scale * slope)
    grad[...] = total
    low[...] = total.astype(BF16)


def norm_back_sum(own, came, rows, upstream):
    spec = pl.BlockSpec((32, D), lambda i: (i, 0))
    return pl.pallas_call(
        norm_back_kernel,
        grid=(CAP // 32,),
        in_specs=[spec] * 6,
        out_specs=[spec] * 2,
        out_shape=[pltpu.HBM((CAP, D), F32), pltpu.HBM((CAP, D), BF16)],
        compiler_params=pltpu.CompilerParams(vmem_limit_bytes=16 * 1024 * 1024),
        cost_estimate=pl.CostEstimate(
            flops=20 * CAP * D, bytes_accessed=6 * 2**20, transcendentals=CAP
        ),
    )(*in_hbm(own, *came, rows, upstream))


def finish_kernel(place, here, one, two, three, gain, *refs):
    query_weight, key_weight, value_weight, half, query, key, value, gain_grad, out = refs
    stacked = [here[...], one[...], two[:, :640], three[...]]
    scale = gain[...]
    lane = lane_of((32, CAP), 1)
    parts = []
    for chip in (0, 2, 1, 3):
        which = lax.rem(place[0] - chip + 4, 4)
        item = stacked[0]
        for k in range(1, 4):
            item = jnp.where(which == k, stacked[k], item)
        parts.append(item.astype(F32))
    total = jnp.zeros((32, 1), F32)
    for k, item in enumerate(parts):
        side = slice(512 * k, 512 * (k + 1))
        raw = item[:, :512]
        query[:, side] = raw * scale
        total += jnp.sum(raw * query_weight[:, side].astype(F32), axis=1, keepdims=True)
    for k in range(2):
        side = slice(CAP * k, CAP * (k + 1))
        low, high = parts[2 * k][:, 512:], parts[2 * k + 1][:, 512:]
        raw = jnp.where(lane < HDIM, low, pltpu.roll(high, HDIM, 1))
        key[:, side] = raw * scale
        total += jnp.sum(raw * key_weight[:, side].astype(F32), axis=1, keepdims=True)
        raw = jnp.where(lane < HDIM, pltpu.roll(low, HDIM, 1), high)
        value[:, side] = raw * scale
        total += jnp.sum(raw * value_weight[:, side].astype(F32), axis=1, keepdims=True)
    gain_grad[...] = total
    out[...] = jnp.where(place[1] == 1, half[...], two[:, 640:]).astype(F32)


def finish(place, here, came, gain, weights, half):
    whole = pl.BlockSpec(memory_space=pltpu.VMEM)
    return pl.pallas_call(
        finish_kernel,
        in_specs=[pl.BlockSpec(memory_space=pltpu.SMEM)] + [whole] * 9,
        out_specs=[whole] * 5,
        out_shape=[
            jax.ShapeDtypeStruct((32, D), F32),
            jax.ShapeDtypeStruct((32, 256), F32),
            jax.ShapeDtypeStruct((32, 256), F32),
            jax.ShapeDtypeStruct((32, 1), F32),
            jax.ShapeDtypeStruct((32, D), F32),
        ],
        compiler_params=pltpu.CompilerParams(vmem_limit_bytes=16 * 1024 * 1024),
        cost_estimate=pl.CostEstimate(flops=2**19, bytes_accessed=2**20, transcendentals=0),
    )(place, here, *came, gain, *weights, half)


def times(left, right):
    return jnp.dot(left, right, preferred_element_type=F32)


def times_t(left, right):
    return lax.dot_general(left, right, (((1,), (1,)), ((), ())), preferred_element_type=F32)


def t_times(left, right):
    return lax.dot_general(left, right, (((0,), (0,)), ((), ())), preferred_element_type=F32)


def rms_scale(rows):
    return lax.rsqrt(jnp.mean(rows * rows, axis=-1, keepdims=True) + norm_eps)


def norm_back(rows, scale, inner):
    return scale * inner - rows * (scale * scale * scale) * jnp.mean(
        inner * rows, axis=-1, keepdims=True
    )


def from_ring(item, step):
    return lax.ppermute(item, RING, [(i, (i - step) % 4) for i in range(4)])


def to_ring(item, step):
    return lax.ppermute(item, RING, [(i, (i + step) % 4) for i in range(4)])


def swap(item, axis):
    return lax.ppermute(item, axis, SWAP)


def share_parts(item, *first):
    own = swap(item, "c")
    ring = after(tuple(from_ring(item, step) for step in STEPS[1:]), *first)
    return [item, *ring, own] + [swap(part, "c") for part in ring]


def pair_blocks(near, far, *first):
    far = after(swap(far, "c"), *first)

    def block(spot):
        here = slice(spot * CAP, (spot + 1) * CAP)
        return near[here].astype(F32) + far[here].astype(F32)

    return (block(0),) + tuple(block(spot).astype(BF16) for spot in (1, 2, 3))


def ring_sum(blocks, *first):
    came = tuple(to_ring(blocks[spot], STEPS[spot]) for spot in (1, 2, 3))
    return blocks[0] + sum(item.astype(F32) for item in after(came, *first))


def spread_columns(chunks, xl, c):
    mine = [jnp.where(c == 0, pair[0], pair[1]) for pair in chunks]
    away = [jnp.where(c == 0, pair[1], pair[0]) for pair in chunks]
    came = swap(jnp.concatenate(away, axis=0), "c")
    rows = mine[0].shape[0]
    both = []
    for k in range(2):
        other = came[k * rows : (k + 1) * rows]
        both.append(
            jnp.concatenate(
                [jnp.where(c == 0, mine[k], other), jnp.where(c == 0, other, mine[k])], axis=0
            )
        )
    kept = jnp.where(xl == 0, both[0], both[1])
    came = swap(jnp.where(xl == 0, both[1], both[0]), "xl")
    return jnp.stack([jnp.where(xl == 0, kept, came), jnp.where(xl == 0, came, kept)])


def gather_four(item, axis, spot, dim):
    parts = [item]
    for step in (1, 2, 3):
        parts.append(lax.ppermute(item, axis, [(i, (i - step) % 4) for i in range(4)]))
    return jnp.stack([pick(parts, (q - spot) % 4) for q in range(4)], axis=dim)


def pick(parts, which):
    out = parts[0]
    for k in range(1, len(parts)):
        out = jnp.where(which == k, parts[k], out)
    return out


def four_pieces(item, spot, dim):
    return [
        lax.dynamic_index_in_dim(item, (spot + step) % 4, dim, keepdims=False) for step in range(4)
    ]


def shifted(item, axis, step):
    return lax.ppermute(item, axis, [(i, (i + step) % 4) for i in range(4)])


def exchange(pieces, axis):
    return tuple(shifted(pieces[step], axis, step) for step in (1, 2, 3))


def four_sum(pieces, came):
    return pieces[0].astype(F32) + sum(item.astype(F32) for item in came)


def row_pairs(step, back):
    pairs = []
    for h in range(2):
        for e in range(2):
            first = 2 * h + e
            one = (h * 4 + first) * 2 + e
            other = (h * 4 + (first + step) % 4) * 2 + e
            pairs.append((other, one) if back else (one, other))
    return pairs


def after(item, *others):
    return lax.optimization_barrier((item,) + others)[0] if others else item


def order_of_columns(xh):
    place = jnp.arange(768)
    core, owner, row = place // 384, (place % 384) // 48, place % 48
    origin = jnp.where(row < 44, 176 * owner + 88 * core + 44 * xh + row, -1)
    return (jnp.arange(1408)[:, None] == origin[None, :]).astype(BF16)


def column_part(item, width, xh):
    out = []
    for k in range(2):
        start = 2 * width * k
        out.append(
            jnp.where(
                xh == 0, item[:, start : start + width], item[:, start + width : start + 2 * width]
            )
        )
    return out


def on_device(
    tokens,
    doc_ids,
    first_gain,
    query_weight,
    key_weight,
    value_weight,
    out_weight,
    second_gain,
    gate_weight,
    up_weight,
    down_weight,
    cotangent,
):
    xh, xl, y, z, c = (lax.axis_index(name) for name in ("xh", "xl", "y", "z", "c"))
    first_col = first_gain.astype(F32)[:, None]
    second_col = second_gain.astype(F32)[:, None]

    def scaled(item, gain):
        return (item.astype(F32) * gain).astype(BF16)

    q_parts = column_part(scaled(query_weight, first_col), 512, xh)
    k_parts = column_part(scaled(key_weight, first_col), 64, xh)
    v_parts = column_part(scaled(value_weight, first_col), 64, xh)
    chunks = [
        [
            jnp.concatenate([q_parts[k][:, 256 * j : 256 * (j + 1)], k_parts[k], v_parts[k]], axis=1)
            for j in range(2)
        ]
        for k in range(2)
    ]
    spread = spread_columns(chunks, xl, c)

    qkv_full = lax.all_gather(spread, ("y", "z"), axis=1, tiled=True).reshape(D, 384)

    wide = jnp.stack([scaled(gate_weight, second_col), scaled(up_weight, second_col)])
    blocks = jnp.concatenate([wide[:, :, 1408 * k : 1408 * (k + 1)] for k in range(4)], axis=0)
    sorted_columns = times(blocks.reshape(256, 1408), order_of_columns(xh)).astype(BF16)
    sorted_columns = sorted_columns.reshape(2, 2, 2, 32, 768)
    chunks = [
        [
            jnp.concatenate(
                [
                    sorted_columns[k, h, item, :, 384 * j : 384 * (j + 1)]
                    for item in range(2)
                    for h in range(2)
                ],
                axis=1,
            )
            for j in range(2)
        ]
        for k in range(2)
    ]
    down_half = jnp.where(xh == 0, down_weight[:44], down_weight[44:])
    down_half = jnp.pad(down_half, ((0, 4), (0, 0)))
    corner = jnp.concatenate(
        [down_half[16 * k : 16 * (k + 1), 2 * WIDE :] for k in range(3)], axis=1
    )
    feed_spread = spread_columns(chunks, xl, c).reshape(128, 2 * WIDE)
    packed = jnp.concatenate([feed_spread, down_half[:, : 2 * WIDE], corner], axis=0)

    source = 2 * xh + c
    came = swap(out_weight, "c")
    head = jnp.concatenate(
        [jnp.where(c == 0, out_weight, came), jnp.where(c == 0, came, out_weight)], axis=0
    )
    lines = [head]
    for step in (1, 2, 3):
        lines.append(lax.ppermute(head, ("xh", "y", "c"), row_pairs(step, False)))
    head = pick(lines, (y - source) % 4)
    out_full = gather_four(head, "z", z, 0).reshape(256, D)

    table = rotary_table()
    rows = tokens.astype(F32)
    first_scale = rms_scale(rows)
    id_rows = jnp.pad(doc_ids.astype(BF16)[None], ((0, 15), (0, D - CAP)))
    payload = jnp.concatenate([(rows * first_scale).astype(BF16), id_rows], axis=0)
    first = share_parts(after(payload, spread, feed_spread))
    packed = after(packed, qkv_full, out_full, *first[1:4])
    packed = lax.all_gather(packed, ("y", "z"), axis=0, tiled=True)

    queries, key_values, mixed, far, near = attend(first, table, qkv_full, out_full)
    upstream = share_parts(after(cotangent, *first[1:4]), mixed)
    far = after(far, upstream[1])
    shuffle = after(jnp.concatenate([order_of_columns(0), order_of_columns(1)], axis=1), mixed)
    blocks = pair_blocks(near, far)
    prepared = prepare_back(first, table, after(queries, *blocks), key_values)
    midway = rows + ring_sum(blocks, shuffle, *prepared)

    second_scale = rms_scale(midway)
    back, down_full = feed_back(upstream, packed)
    second = share_parts((midway * second_scale).astype(BF16), back)
    hidden, grad_feed, far, near = feed_forward(second, packed, back)
    blocks = pair_blocks(near, far)
    pack = feed_grads(second, upstream, after(hidden, *blocks), grad_feed)
    came = tuple(to_ring(blocks[spot], STEPS[spot]) for spot in (1, 2, 3))
    out_far, out_near = output_product(after(hidden, pack), down_full)
    grad_mid, grad_low = norm_back_sum(blocks[0], after(came, pack, out_far), midway, cotangent)
    out_blocks = pair_blocks(out_near, after(out_far, grad_low))
    third = share_parts(grad_low, *out_blocks)
    pack = lax.psum_scatter(after(pack, *came, out_far), ("y", "z"), scatter_dimension=0, tiled=True)

    out_term = out_grads(third, mixed).reshape(4, 64, D)
    out_sent = four_pieces(out_term, z, 0)
    out_came = tuple(shifted(out_sent[step], "z", step) for step in (1, 2))
    grad_qkv, far, near = attend_back(
        third, qkv_full, after(out_full, *out_sent, *out_blocks), prepared
    )
    product = ring_sum(out_blocks, grad_qkv)
    output = (midway + product).astype(BF16)
    out_came += (shifted(after(out_sent[3], grad_qkv), "z", 3),)
    out_part = four_sum(out_sent, after(out_came, product))
    far = after(far, out_part)
    sent = out_part.astype(BF16)
    out_came = tuple(
        lax.ppermute(sent, ("xh", "y", "c"), row_pairs(step, True)) for step in (1, 2, 3)
    )
    qkv_term = qkv_grads(first, after(grad_qkv, sent))
    blocks = pair_blocks(near, far, qkv_term)
    out_came = after(out_came, *blocks)
    out_part = (out_part + sum(item.astype(F32) for item in out_came)).astype(BF16)

    def halves(item):
        low, high = item[:, :32], item[:, 32:]
        return jnp.where(c == 0, low, high), jnp.where(c == 0, high, low)

    sent = four_pieces(after(qkv_term, out_part, *blocks), y, 1)
    came = exchange(sent, "y")
    ring_came = (to_ring(blocks[1], STEPS[1]), to_ring(blocks[2], STEPS[2]))
    corner = jnp.concatenate([pack[176:, 512 * k : 512 * (k + 1)] for k in range(3)], axis=0)
    down_part = jnp.concatenate([pack[128:176], corner], axis=1)
    feed_part = pack[:128].reshape(2, 64, 2 * WIDE)
    feed_mine, feed_away = halves(feed_part)
    came, ring_came, feed_mine, feed_away, down_part = lax.optimization_barrier(
        (came, ring_came, feed_mine, feed_away, down_part)
    )
    sent = four_pieces(four_sum(sent, came).astype(BF16).reshape(2, 4, 64, 384), z, 1)
    came = exchange(sent, "z")
    last_came = to_ring(blocks[3], STEPS[3])
    feed_came = swap(feed_away, "c")
    came, last_came, feed_came = lax.optimization_barrier((came, last_came, feed_came))

    def in_order(mine, came):
        return jnp.where(c == 0, mine, came), jnp.where(c == 0, came, mine)

    def along_ring(both, more):
        here = jnp.where(xl == 0, both[0], both[1])
        there = jnp.where(xl == 0, both[1], both[0])
        across = jnp.concatenate([here, more], axis=1)
        return here, (to_ring(there, 1), to_ring(across, 2), to_ring(there, 3))

    def by_chip(here, came):
        width, spot = here.shape[1], 2 * xh + xl
        stacked = [here, came[0], came[1][:, :width], came[2]]
        return [[pick(stacked, (spot - (2 * h + k)) % 4) for h in range(2)] for k in range(2)]

    down_wide = jnp.concatenate(
        [down_part[:32], jnp.concatenate([down_part[32:, :1024], down_part[32:, 1024:]], axis=0)],
        axis=1,
    )
    feed_here, feed_came = along_ring(
        jnp.concatenate(in_order(feed_mine, feed_came), axis=2), down_wide
    )

    qkv_part = four_sum(sent, came).astype(BF16)
    qkv_mine, qkv_away = halves(qkv_part)
    away = jnp.where(c == 0, out_part[32:], out_part[:32])
    sent = jnp.concatenate(
        [
            qkv_away.reshape(64, 384),
            jnp.concatenate([away[:, :1024], away[:, 1024:]], axis=0),
        ],
        axis=1,
    )
    came = swap(sent, "c")
    zero, one = in_order(qkv_mine, came[:, :384].reshape(2, 32, 384))
    pair = zero[:, :, 256:].astype(F32) + one[:, :, 256:].astype(F32)
    both = jnp.concatenate([zero[:, :, :256], one[:, :, :256], pair.astype(BF16)], axis=2)
    out_half = jnp.where(
        y % 2 == c,
        jnp.where(c == 0, out_part[:32], out_part[32:]),
        jnp.concatenate([came[:32, 384:], came[32:, 384:]], axis=1),
    )
    both, out_half = lax.optimization_barrier((both, out_half))
    qkv_here, came = along_ring(both, out_half)
    feed_came = after(feed_came, both)

    inner_one = blocks[0] + sum(item.astype(F32) for item in ring_came + (last_came,))
    tokens_grad = grad_mid + norm_back(rows, first_scale, inner_one)
    parts = by_chip(feed_here, feed_came)
    down_other = feed_came[1][:, 3072:]
    down_other = jnp.concatenate(
        [
            down_other[:, :2048],
            jnp.concatenate([down_other[:16, 2048:], down_other[16:, 2048:]], axis=1),
        ],
        axis=0,
    )
    down_grad = jnp.concatenate(
        [
            jnp.where(xh == 0, down_part, down_other)[:44],
            jnp.where(xh == 0, down_other, down_part)[:44],
        ],
        axis=0,
    ).astype(F32)
    rows_of = []
    for item in range(2):
        for k in range(2):
            for half in range(2):
                start = item * WIDE + half * 384
                rows_of.append(
                    jnp.concatenate(
                        [
                            parts[k][h][:, e * 2 * WIDE + start : e * 2 * WIDE + start + 384]
                            for h in range(2)
                            for e in range(2)
                        ],
                        axis=1,
                    )
                )
    unsorted = times_t(jnp.concatenate(rows_of, axis=0), shuffle).reshape(2, 4, 32, 1408)
    gate_raw = jnp.concatenate([unsorted[0, k] for k in range(4)], axis=1)
    up_raw = jnp.concatenate([unsorted[1, k] for k in range(4)], axis=1)
    second_grad = jnp.sum(gate_raw * gate_weight.astype(F32), axis=1) + jnp.sum(
        up_raw * up_weight.astype(F32), axis=1
    )

    place = jnp.stack([2 * xh + xl, (y // 2 == xh).astype(jnp.int32)]).astype(jnp.int32)
    weights = (query_weight, key_weight, value_weight)
    came = after(came, gate_raw, up_raw, second_grad, down_grad)
    query_grad, key_grad, value_grad, first_grad, out_grad = finish(
        place, qkv_here, came, first_col, weights, out_half
    )

    return (
        output,
        tokens_grad,
        first_grad[:, 0],
        query_grad,
        key_grad,
        value_grad,
        out_grad,
        second_grad,
        gate_raw * second_col,
        up_raw * second_col,
        down_grad,
    )


def solution(mesh):
    fine = Mesh(mesh.devices.reshape(2, 2, 4, 4, 2), ("xh", "xl", "y", "z", "c"))
    everyone = ("xh", "xl", "y", "z", "c")
    group = ("xl", "y", "z", "c")
    in_specs = (
        P(everyone, None),
        P(everyone),
        P(group),
        P(group, None),
        P(group, None),
        P(group, None),
        P(group, None),
        P(group),
        P(group, None),
        P(group, None),
        P(group, None),
        P(everyone, None),
    )
    out_specs = (
        P(everyone, None),
        P(everyone, None),
        P(group),
        P(group, None),
        P(group, None),
        P(group, None),
        P(group, None),
        P(group),
        P(group, None),
        P(group, None),
        P(group, None),
    )
    return jax.shard_map(
        on_device, mesh=fine, in_specs=in_specs, out_specs=out_specs, check_vma=False
    )
```

```python
import jax
import jax.numpy as jnp
import ml_dtypes
import numpy as np
from jax import lax
from jax.experimental import pallas as pl
from jax.experimental.pallas import tpu as pltpu
from jax.sharding import Mesh, PartitionSpec as P

D = 2048
HDIM = 64
CAP = 128
WIDE = 768
BF16 = jnp.bfloat16
F32 = jnp.float32

norm_eps = 1e-05

RING = ("xh", "xl")
SWAP = [(0, 1), (1, 0)]
STEPS = (0, 1, 3, 2)


def dot_nn(left, right):
    return lax.dot_general(left, right, (((1,), (0,)), ((), ())), preferred_element_type=F32)


def dot_nt(left, right):
    return lax.dot_general(left, right, (((1,), (1,)), ((), ())), preferred_element_type=F32)


def dot_tn(left, right):
    return lax.dot_general(left, right, (((0,), (0,)), ((), ())), preferred_element_type=F32)


HBM = pl.BlockSpec(memory_space=pltpu.HBM)


def in_hbm(*items):
    return [pltpu.with_memory_space_constraint(item, pltpu.HBM) for item in items]


def block_copies(parts, whole, sems):
    return [
        pltpu.make_async_copy(
            part.at[pl.ds(0, CAP)], whole.at[pl.ds(CAP * spot, CAP)], sems.at[spot]
        )
        for spot, part in enumerate(parts)
    ]


def id_copies(parts, ids, sems):
    return [
        pltpu.make_async_copy(part.at[pl.ds(CAP, 16), pl.ds(0, CAP)], ids.at[spot], sems.at[spot])
        for spot, part in enumerate(parts)
    ]


def feed_copies(packed, feed, sems):
    copies = []
    for k in range(16):
        for h in range(2):
            copies.append(
                pltpu.make_async_copy(
                    packed.at[pl.ds(192 * k + 64 * h, 64)],
                    feed.at[pl.ds(1024 * h + 64 * k, 64)],
                    sems.at[2 * k + h],
                )
            )
    return copies


def down_copies(packed, down, sems):
    copies = []
    for k in range(16):
        copies.append(
            pltpu.make_async_copy(
                packed.at[pl.ds(192 * k + 128, 48)],
                down.at[pl.ds(48 * k, 48), pl.ds(0, 1536)],
                sems.at[4 * k],
            )
        )
        for h in range(3):
            copies.append(
                pltpu.make_async_copy(
                    packed.at[pl.ds(192 * k + 176, 16), pl.ds(512 * h, 512)],
                    down.at[pl.ds(48 * k + 16 * h, 16), pl.ds(1536, 512)],
                    sems.at[4 * k + 1 + h],
                )
            )
    return copies


def back_kernel(*refs):
    parts, packed, out, down_out, c, down, c_sems, d_sems, out_sems = refs[:8], *refs[8:]
    step = pl.program_id(0)
    loads = block_copies(parts, c, c_sems)
    keep = pltpu.make_async_copy(down, down_out, out_sems.at[0])

    @pl.when(step == 0)
    def _():
        rows = down_copies(packed, down, d_sems)
        for copy in loads[:4] + rows + loads[4:]:
            copy.start()
        for copy in loads[:4] + rows:
            copy.wait()
        keep.start()

    @pl.when(step == 1)
    def _():
        for copy in loads[4:]:
            copy.wait()

    rows = pl.ds(pl.multiple_of(step * 512, 512), 512)
    out[...] = dot_nt(c[rows, :], down[...])

    @pl.when(step == 1)
    def _():
        keep.wait()


def feed_back(c_parts, packed):
    return pl.pallas_call(
        back_kernel,
        grid=(2,),
        in_specs=[HBM] * 9,
        out_specs=[pl.BlockSpec((512, WIDE), lambda i: (i, 0)), HBM],
        out_shape=[jax.ShapeDtypeStruct((1024, WIDE), F32), pltpu.HBM((WIDE, D), BF16)],
        scratch_shapes=[
            pltpu.VMEM((1024, D), BF16),
            pltpu.VMEM((WIDE, D), BF16),
            pltpu.SemaphoreType.DMA((8,)),
            pltpu.SemaphoreType.DMA((64,)),
            pltpu.SemaphoreType.DMA((1,)),
        ],
        compiler_params=pltpu.CompilerParams(vmem_limit_bytes=24 * 1024 * 1024),
        cost_estimate=pl.CostEstimate(
            flops=2 * 1024 * D * WIDE, bytes_accessed=10 * 2**20, transcendentals=0
        ),
    )(*in_hbm(*c_parts, packed))


def feed_kernel(*refs):
    x_parts, packed, back = refs[:8], refs[8], refs[9]
    hidden, grads, far, near, x, feed, x_sems, f_sems = refs[10:]
    step = pl.program_id(0)
    first = block_copies(x_parts, x, x_sems)

    @pl.when(step == 0)
    def _():
        second = feed_copies(packed, feed, f_sems)
        for copy in first[4:6] + second + first[6:] + first[:4]:
            copy.start()
        for copy in first[4:6] + second:
            copy.wait()

    for k in range(1, 4):

        @pl.when(step == k)
        def _(k=k):
            spot = (2 * k + 4) % 8
            for copy in first[spot : spot + 2]:
                copy.wait()

    rows = pl.ds(pl.multiple_of(((step + 2) % 4) * 256, 256), 256)
    block = x[rows, :]
    for k in range(0, WIDE, 256):
        here, beside = slice(k, k + 256), slice(WIDE + k, WIDE + k + 256)
        gate = dot_nn(block, feed[:, here])
        up = dot_nn(block, feed[:, beside])
        slope = back[:, here]
        sig = jax.nn.sigmoid(gate)
        silu = gate * sig
        hidden[:, here] = (silu * up).astype(BF16)
        grads[:, here] = (slope * up * (sig * (1.0 + gate * (1.0 - sig)))).astype(BF16)
        grads[:, beside] = (slope * silu).astype(BF16)
    inner = dot_nt(grads[...], feed[...])

    @pl.when(step < 2)
    def _():
        far[...] = inner.astype(BF16)

    @pl.when(step >= 2)
    def _():
        near[...] = inner.astype(BF16)


def feed_forward(x_parts, packed, back):
    row = lambda i: ((i + 2) % 4, 0)
    return pl.pallas_call(
        feed_kernel,
        grid=(4,),
        in_specs=[HBM] * 9 + [pl.BlockSpec((256, WIDE), row)],
        out_specs=[
            pl.BlockSpec((256, WIDE), row),
            pl.BlockSpec((256, 2 * WIDE), row),
            pl.BlockSpec((256, D), lambda i: (jnp.minimum(i, 1), 0)),
            pl.BlockSpec((256, D), lambda i: (jnp.maximum(i - 2, 0), 0)),
        ],
        out_shape=[
            jax.ShapeDtypeStruct((1024, WIDE), BF16),
            jax.ShapeDtypeStruct((1024, 2 * WIDE), BF16),
            jax.ShapeDtypeStruct((512, D), BF16),
            jax.ShapeDtypeStruct((512, D), BF16),
        ],
        scratch_shapes=[
            pltpu.VMEM((1024, D), BF16),
            pltpu.VMEM((D, 2 * WIDE), BF16),
            pltpu.SemaphoreType.DMA((8,)),
            pltpu.SemaphoreType.DMA((32,)),
        ],
        compiler_params=pltpu.CompilerParams(vmem_limit_bytes=36 * 1024 * 1024),
        cost_estimate=pl.CostEstimate(
            flops=2 * 1024 * D * WIDE * 4, bytes_accessed=24 * 2**20, transcendentals=1024 * WIDE
        ),
    )(*in_hbm(*x_parts, packed), back)


def grads_kernel(*refs):
    x_parts, c_parts, hidden_hbm, grads_hbm = refs[:8], refs[8:16], refs[16], refs[17]
    out = refs[18]
    x, c, hidden, grads, pack, x_sems, c_sems, in_sems, sems = refs[19:]
    first = block_copies(x_parts, x, x_sems)
    second = block_copies(c_parts, c, c_sems)
    loads = [
        pltpu.make_async_copy(grads_hbm, grads, in_sems.at[0]),
        pltpu.make_async_copy(hidden_hbm, hidden, in_sems.at[1]),
    ]
    for copy in first + loads + second:
        copy.start()
    for copy in first + loads[:1]:
        copy.wait()
    stores = []

    def store(row, rows):
        copy = pltpu.make_async_copy(
            pack.at[pl.ds(row, rows)], out.at[pl.ds(row, rows)], sems.at[len(stores)]
        )
        copy.start()
        stores.append(copy)

    for k in range(8):
        tile = dot_tn(x[:, 256 * k : 256 * (k + 1)], grads[...]).astype(BF16)
        half, spot = k // 4, (k % 4) * 4
        for j in range(4):
            row = 192 * (spot + j) + 64 * half
            pack[row : row + 64, :] = tile[64 * j : 64 * (j + 1)]
            store(row, 64)
    for copy in second + loads[1:]:
        copy.wait()
    for k in range(2):
        tile = dot_tn(hidden[:, 384 * k : 384 * (k + 1)], c[...]).astype(BF16)
        for j in range(8):
            row = 192 * (8 * k + j) + 128
            piece = tile[48 * j : 48 * (j + 1)]
            pack[row : row + 48, :] = piece[:, :1536]
            for h in range(3):
                pack[row + 48 : row + 64, 512 * h : 512 * (h + 1)] = piece[
                    16 * h : 16 * (h + 1), 1536:
                ]
            store(row, 64)
    for copy in stores:
        copy.wait()


def feed_grads(x_parts, c_parts, hidden, grads):
    return pl.pallas_call(
        grads_kernel,
        in_specs=[HBM] * 18,
        out_specs=HBM,
        out_shape=jax.ShapeDtypeStruct((3072, 1536), BF16),
        scratch_shapes=[
            pltpu.VMEM((1024, D), BF16),
            pltpu.VMEM((1024, D), BF16),
            pltpu.VMEM((1024, WIDE), BF16),
            pltpu.VMEM((1024, 2 * WIDE), BF16),
            pltpu.VMEM((3072, 2 * WIDE), BF16),
            pltpu.SemaphoreType.DMA((8,)),
            pltpu.SemaphoreType.DMA((8,)),
            pltpu.SemaphoreType.DMA((2,)),
            pltpu.SemaphoreType.DMA((48,)),
        ],
        compiler_params=pltpu.CompilerParams(vmem_limit_bytes=60 * 1024 * 1024),
        cost_estimate=pl.CostEstimate(
            flops=2 * 1024 * D * WIDE * 3, bytes_accessed=22 * 2**20, transcendentals=0
        ),
    )(*in_hbm(*x_parts, *c_parts, hidden, grads))


def output_kernel(hidden_hbm, down_hbm, far, near, hidden, down, total, sems, out_sems):
    copies = [
        pltpu.make_async_copy(down_hbm, down, sems.at[0]),
        pltpu.make_async_copy(hidden_hbm, hidden, sems.at[1]),
    ]
    for copy in copies:
        copy.start()
    for copy in copies:
        copy.wait()
    stores = []
    for k, out in ((1, far), (0, near)):
        total[k] = dot_nn(hidden[512 * k : 512 * (k + 1)], down[...]).astype(BF16)
        stores.append(pltpu.make_async_copy(total.at[k], out, out_sems.at[k]))
        stores[-1].start()
    for copy in stores:
        copy.wait()


def output_product(hidden, down_full):
    return pl.pallas_call(
        output_kernel,
        in_specs=[HBM, HBM],
        out_specs=[HBM, HBM],
        out_shape=[pltpu.HBM((512, D), BF16), pltpu.HBM((512, D), BF16)],
        scratch_shapes=[
            pltpu.VMEM((1024, WIDE), BF16),
            pltpu.VMEM((WIDE, D), BF16),
            pltpu.VMEM((2, 512, D), BF16),
            pltpu.SemaphoreType.DMA((2,)),
            pltpu.SemaphoreType.DMA((2,)),
        ],
        compiler_params=pltpu.CompilerParams(vmem_limit_bytes=24 * 1024 * 1024),
        cost_estimate=pl.CostEstimate(
            flops=2 * 1024 * D * WIDE, bytes_accessed=11 * 2**20, transcendentals=0
        ),
    )(*in_hbm(hidden, down_full))


def rotary_table():
    place = np.arange(CAP, dtype=np.float32)[:, None]
    inverse = np.float32(10000.0) ** (np.arange(32, dtype=np.float32) * np.float32(-2.0 / HDIM))
    angle = (place * inverse).astype(np.float32)
    cosine, sine = np.cos(angle), np.sin(angle)
    zero, one = np.zeros((CAP, 64), np.float32), np.ones((CAP, 64), np.float32)
    ahead = np.concatenate([-sine, zero[:, :32]], axis=1)
    behind = np.concatenate([zero[:, :32], sine], axis=1)
    cosine = np.concatenate([cosine, cosine], axis=1)
    table = np.concatenate(
        [cosine, cosine, ahead, ahead, behind, behind, cosine, one, ahead, zero, behind, zero], axis=1
    )
    high = table.astype(ml_dtypes.bfloat16)
    rest = (table - high.astype(np.float32)).astype(ml_dtypes.bfloat16)
    return jnp.asarray(np.stack([high, rest]))


def lane_of(shape, dim):
    return lax.broadcasted_iota(jnp.int32, shape, dim)


def block_tables(ids, table):
    row = jnp.broadcast_to(ids.astype(F32)[:1], (CAP, CAP))
    same = row == row.T
    to, frm = lane_of((CAP, CAP), 0), lane_of((CAP, CAP), 1)
    place = jnp.sum(jnp.where(same & (frm < to), 1.0, 0.0), axis=1, keepdims=True)
    chosen = (frm.astype(F32) == place).astype(BF16)
    factors = dot_nn(chosen, table[0]) + dot_nn(chosen, table[1])
    return same & (frm <= to), factors


def turned(item, factors, sign):
    def three(k):
        pair = factors[:, CAP * k : CAP * (k + 1)]
        return jnp.concatenate([pair, pair, factors[:, CAP * (k + 3) : CAP * (k + 4)]], axis=1)

    other = pltpu.roll(item, 352, 1) * three(1) + pltpu.roll(item, 32, 1) * three(2)
    return item * three(0) + sign * other


def stack_heads(item):
    head = lane_of((CAP, 256), 1) // 64
    return jnp.concatenate([jnp.where(head == h, item, 0).astype(BF16) for h in range(4)], axis=0)


def spreads():
    lane, own = lane_of((CAP, 256), 1) % 64, lane_of((CAP, 256), 0)
    return (lane == own).astype(BF16), (lane + 64 == own).astype(BF16)


def softmax_heads(queries, keys, allowed):
    scores = dot_nt(stack_heads(queries), keys) * 0.125
    out = []
    for h in range(4):
        part = jnp.where(allowed, scores[CAP * h : CAP * (h + 1)], -1e30)
        expo = jnp.exp(part - jnp.max(part, axis=1, keepdims=True))
        out.append(expo / jnp.sum(expo, axis=1, keepdims=True))
    return out


def attend_kernel(*refs):
    parts, table, w_hbm, o_hbm = refs[:8], refs[8], refs[9], refs[10]
    queries, key_values, mixed, far, near = refs[11:16]
    x, ids, w, o, x_sems, i_sems, w_sems = refs[16:]
    step = pl.program_id(0)
    blocks, numbers = block_copies(parts, x, x_sems), id_copies(parts, ids, i_sems)
    loads = [
        pltpu.make_async_copy(w_hbm, w, w_sems.at[0]),
        pltpu.make_async_copy(o_hbm, o, w_sems.at[1]),
    ]

    @pl.when(step == 0)
    def _():
        for copy in loads[:1] + blocks[4:] + numbers[4:] + loads[1:] + blocks[:4] + numbers[:4]:
            copy.start()
        for copy in loads[:1] + blocks[4:] + numbers[4:]:
            copy.wait()

    @pl.when(step == 1)
    def _():
        for copy in blocks[:4] + numbers[:4]:
            copy.wait()

    half = 1 - step
    rows = pl.ds(pl.multiple_of(half * 512, 512), 512)
    qkv = dot_nn(x[rows, :], w[...])
    to_key, to_value = spreads()
    for k in range(4):
        allowed, factors = block_tables(ids[half * 4 + k], table)
        block = turned(qkv[CAP * k : CAP * (k + 1)], factors, 1.0).astype(BF16)
        here = slice(CAP * k, CAP * (k + 1))
        queries[here, :] = block[:, :256]
        key_values[here, :] = block[:, 256:]
        keys = dot_nn(block[:, 256:], to_key).astype(BF16)
        values = dot_nn(block[:, 256:], to_value).astype(BF16)
        probs = softmax_heads(block[:, :256], keys, allowed)
        probs = jnp.concatenate([item.astype(BF16) for item in probs], axis=1)
        mixed[here, :] = dot_nn(probs, stack_heads(values)).astype(BF16)

    @pl.when(step == 0)
    def _():
        loads[1].wait()

    total = dot_nn(mixed[...], o[...])

    @pl.when(step == 0)
    def _():
        far[...] = total.astype(BF16)

    @pl.when(step == 1)
    def _():
        near[...] = total.astype(BF16)


def attend(parts, table, qkv_full, out_full):
    row = lambda i: (1 - i, 0)
    still = lambda i: (0, 0)
    return pl.pallas_call(
        attend_kernel,
        grid=(2,),
        in_specs=[HBM] * 8 + [pl.BlockSpec((2, CAP, 768), lambda i: (0, 0, 0))] + [HBM] * 2,
        out_specs=[
            pl.BlockSpec((512, 256), row),
            pl.BlockSpec((512, CAP), row),
            pl.BlockSpec((512, 256), row),
            pl.BlockSpec((512, D), still),
            pl.BlockSpec((512, D), still),
        ],
        out_shape=[
            jax.ShapeDtypeStruct((1024, 256), BF16),
            jax.ShapeDtypeStruct((1024, CAP), BF16),
            jax.ShapeDtypeStruct((1024, 256), BF16),
            jax.ShapeDtypeStruct((512, D), BF16),
            jax.ShapeDtypeStruct((512, D), BF16),
        ],
        scratch_shapes=[
            pltpu.VMEM((1024, D), BF16),
            pltpu.VMEM((8, 16, CAP), BF16),
            pltpu.VMEM((D, 384), BF16),
            pltpu.VMEM((256, D), BF16),
            pltpu.SemaphoreType.DMA((8,)),
            pltpu.SemaphoreType.DMA((8,)),
            pltpu.SemaphoreType.DMA((2,)),
        ],
        compiler_params=pltpu.CompilerParams(vmem_limit_bytes=32 * 1024 * 1024),
        cost_estimate=pl.CostEstimate(
            flops=2 * 1024 * D * 640 * 2, bytes_accessed=15 * 2**20, transcendentals=2**19
        ),
    )(*in_hbm(*parts), table, *in_hbm(qkv_full, out_full))


def prepare_kernel(*refs):
    parts, table, queries, key_values = refs[:8], *refs[8:11]
    probs, keys, values, folded, factors, ids, i_sems = refs[11:]
    step = pl.program_id(0)

    @pl.when(step == 0)
    def _():
        copies = id_copies(parts, ids, i_sems)
        for copy in copies:
            copy.start()
        for copy in copies:
            copy.wait()

    to_key, to_value = spreads()
    allowed, around = block_tables(ids[step], table)
    factors[...] = around
    both = key_values[...]
    keys[...] = dot_nn(both, to_key).astype(BF16)
    values[...] = dot_nn(both, to_value).astype(BF16)
    folded[...] = dot_nt(stack_heads(queries[...]), to_key).astype(BF16)
    for h, item in enumerate(softmax_heads(queries[...], keys[...], allowed)):
        probs[CAP * h : CAP * (h + 1), :] = item


def prepare_back(id_parts, table, queries, key_values):
    row = lambda i: (i, 0)
    sizes = ((512, CAP, F32), (CAP, 256, BF16), (CAP, 256, BF16), (512, CAP, BF16), (CAP, 768, F32))
    return pl.pallas_call(
        prepare_kernel,
        grid=(8,),
        in_specs=[HBM] * 8
        + [pl.BlockSpec((2, CAP, 768), lambda i: (0, 0, 0))]
        + [pl.BlockSpec((CAP, 256), row), pl.BlockSpec((CAP, CAP), row)],
        out_specs=[pl.BlockSpec((rows, lanes), row) for rows, lanes, _ in sizes],
        out_shape=[jax.ShapeDtypeStruct((8 * rows, lanes), kind) for rows, lanes, kind in sizes],
        scratch_shapes=[pltpu.VMEM((8, 16, CAP), BF16), pltpu.SemaphoreType.DMA((8,))],
        compiler_params=pltpu.CompilerParams(vmem_limit_bytes=20 * 1024 * 1024),
        cost_estimate=pl.CostEstimate(
            flops=2**30, bytes_accessed=9 * 2**20, transcendentals=2**19
        ),
    )(*in_hbm(*id_parts), table, queries, key_values)


def attend_back_kernel(*refs):
    parts, w_hbm, o_hbm = refs[:8], refs[8], refs[9]
    probs, keys, values, folded, factors = refs[10:15]
    grads, far, near, g, w, o, g_sems, w_sems = refs[15:]
    step = pl.program_id(0)
    blocks = block_copies(parts, g, g_sems)
    loads = [
        pltpu.make_async_copy(o_hbm, o, w_sems.at[0]),
        pltpu.make_async_copy(w_hbm, w, w_sems.at[1]),
    ]

    @pl.when(step == 0)
    def _():
        for copy in loads[:1] + blocks[4:] + loads[1:] + blocks[:4]:
            copy.start()
        for copy in loads[:1] + blocks[4:]:
            copy.wait()

    @pl.when(step == 1)
    def _():
        for copy in blocks[:4]:
            copy.wait()

    rows = pl.ds(pl.multiple_of((1 - step) * 512, 512), 512)
    grad_mixed = dot_nt(g[rows, :], o[...]).astype(BF16)
    to_value = spreads()[1]
    for k in range(4):
        here, heads = slice(CAP * k, CAP * (k + 1)), slice(512 * k, 512 * (k + 1))
        grad_heads = stack_heads(grad_mixed[here])
        part = dot_nt(grad_heads, values[here, :])
        prob = probs[heads, :]
        scores = (prob * (part - jnp.sum(prob * part, axis=1, keepdims=True))).astype(BF16)
        beside = jnp.concatenate([scores[CAP * h : CAP * (h + 1)] for h in range(4)], axis=1)
        grad_query = dot_nn(beside, stack_heads(keys[here, :])) * 0.125
        grad_folded = dot_nt(grad_heads, to_value).astype(BF16)
        grad_both = dot_tn(scores, folded[heads, :]) * 0.125 + dot_tn(prob.astype(BF16), grad_folded)
        item = jnp.concatenate([grad_query, grad_both], axis=1)
        grads[here, :] = turned(item, factors[here, :], -1.0).astype(BF16)

    @pl.when(step == 0)
    def _():
        loads[1].wait()

    total = dot_nt(grads[...], w[...]).astype(BF16)

    @pl.when(step == 0)
    def _():
        far[...] = total

    @pl.when(step == 1)
    def _():
        near[...] = total


def attend_back(parts, qkv_full, out_full, prepared):
    row = lambda i: (1 - i, 0)
    return pl.pallas_call(
        attend_back_kernel,
        grid=(2,),
        in_specs=[HBM] * 10
        + [
            pl.BlockSpec((2048, CAP), row),
            pl.BlockSpec((512, 256), row),
            pl.BlockSpec((512, 256), row),
            pl.BlockSpec((2048, CAP), row),
            pl.BlockSpec((512, 768), row),
        ],
        out_specs=[
            pl.BlockSpec((512, 384), row),
            pl.BlockSpec((512, D), lambda i: (0, 0)),
            pl.BlockSpec((512, D), lambda i: (0, 0)),
        ],
        out_shape=[
            jax.ShapeDtypeStruct((1024, 384), BF16),
            jax.ShapeDtypeStruct((512, D), BF16),
            jax.ShapeDtypeStruct((512, D), BF16),
        ],
        scratch_shapes=[
            pltpu.VMEM((1024, D), BF16),
            pltpu.VMEM((D, 384), BF16),
            pltpu.VMEM((256, D), BF16),
            pltpu.SemaphoreType.DMA((8,)),
            pltpu.SemaphoreType.DMA((2,)),
        ],
        compiler_params=pltpu.CompilerParams(vmem_limit_bytes=36 * 1024 * 1024),
        cost_estimate=pl.CostEstimate(
            flops=2 * 1024 * D * 640 * 2, bytes_accessed=15 * 2**20, transcendentals=0
        ),
    )(*in_hbm(*parts, qkv_full, out_full), *prepared)


def out_grads_kernel(*refs):
    parts, mixed_hbm, out, g, mixed, sems, in_sems = refs[:8], *refs[8:]
    copies = block_copies(parts, g, sems)
    copies.append(pltpu.make_async_copy(mixed_hbm, mixed, in_sems.at[0]))
    for copy in copies:
        copy.start()
    for copy in copies:
        copy.wait()
    out[...] = dot_tn(mixed[...], g[...]).astype(BF16)


def out_grads(parts, mixed):
    return pl.pallas_call(
        out_grads_kernel,
        in_specs=[HBM] * 9,
        out_specs=pl.BlockSpec(memory_space=pltpu.VMEM),
        out_shape=jax.ShapeDtypeStruct((256, D), BF16),
        scratch_shapes=[
            pltpu.VMEM((1024, D), BF16),
            pltpu.VMEM((1024, 256), BF16),
            pltpu.SemaphoreType.DMA((8,)),
            pltpu.SemaphoreType.DMA((1,)),
        ],
        compiler_params=pltpu.CompilerParams(vmem_limit_bytes=24 * 1024 * 1024),
        cost_estimate=pl.CostEstimate(
            flops=2 * 1024 * D * 256, bytes_accessed=6 * 2**20, transcendentals=0
        ),
    )(*in_hbm(*parts, mixed))


def qkv_grads_kernel(*refs):
    parts, grads_hbm, out, x, grads, sems, in_sems = refs[:8], *refs[8:]
    copies = block_copies(parts, x, sems)
    copies.append(pltpu.make_async_copy(grads_hbm, grads, in_sems.at[0]))
    for copy in copies:
        copy.start()
    for copy in copies:
        copy.wait()
    for k in range(8):
        out[k // 4, k % 4] = dot_tn(x[:, 256 * k : 256 * (k + 1)], grads[...]).astype(BF16)


def qkv_grads(parts, grads):
    return pl.pallas_call(
        qkv_grads_kernel,
        in_specs=[HBM] * 9,
        out_specs=pl.BlockSpec(memory_space=pltpu.VMEM),
        out_shape=jax.ShapeDtypeStruct((2, 4, 256, 384), BF16),
        scratch_shapes=[
            pltpu.VMEM((1024, D), BF16),
            pltpu.VMEM((1024, 384), BF16),
            pltpu.SemaphoreType.DMA((8,)),
            pltpu.SemaphoreType.DMA((1,)),
        ],
        compiler_params=pltpu.CompilerParams(vmem_limit_bytes=24 * 1024 * 1024),
        cost_estimate=pl.CostEstimate(
            flops=2 * 1024 * D * 384, bytes_accessed=6 * 2**20, transcendentals=0
        ),
    )(*in_hbm(*parts, grads))


def norm_back_kernel(own, one, two, three, rows, upstream, grad, low):
    x = rows[...]
    inner = own[...] + one[...].astype(F32) + two[...].astype(F32) + three[...].astype(F32)
    scale = lax.rsqrt(jnp.mean(x * x, axis=1, keepdims=True) + norm_eps)
    slope = jnp.mean(inner * x, axis=1, keepdims=True)
    total = upstream[...].astype(F32) + scale * inner - x * (scale * scale * scale * slope)
    grad[...] = total
    low[...] = total.astype(BF16)


def norm_back_sum(own, came, rows, upstream):
    spec = pl.BlockSpec((32, D), lambda i: (i, 0))
    return pl.pallas_call(
        norm_back_kernel,
        grid=(CAP // 32,),
        in_specs=[spec] * 6,
        out_specs=[spec] * 2,
        out_shape=[pltpu.HBM((CAP, D), F32), pltpu.HBM((CAP, D), BF16)],
        compiler_params=pltpu.CompilerParams(vmem_limit_bytes=16 * 1024 * 1024),
        cost_estimate=pl.CostEstimate(
            flops=20 * CAP * D, bytes_accessed=6 * 2**20, transcendentals=CAP
        ),
    )(*in_hbm(own, *came, rows, upstream))


def finish_kernel(place, here, one, two, three, gain, *refs):
    query_weight, key_weight, value_weight, half, query, key, value, gain_grad, out = refs
    stacked = [here[...], one[...], two[:, :640], three[...]]
    scale = gain[...]
    lane = lane_of((32, CAP), 1)
    parts = []
    for chip in (0, 2, 1, 3):
        which = lax.rem(place[0] - chip + 4, 4)
        item = stacked[0]
        for k in range(1, 4):
            item = jnp.where(which == k, stacked[k], item)
        parts.append(item.astype(F32))
    total = jnp.zeros((32, 1), F32)
    for k, item in enumerate(parts):
        side = slice(512 * k, 512 * (k + 1))
        raw = item[:, :512]
        query[:, side] = raw * scale
        total += jnp.sum(raw * query_weight[:, side].astype(F32), axis=1, keepdims=True)
    for k in range(2):
        side = slice(CAP * k, CAP * (k + 1))
        low, high = parts[2 * k][:, 512:], parts[2 * k + 1][:, 512:]
        raw = jnp.where(lane < HDIM, low, pltpu.roll(high, HDIM, 1))
        key[:, side] = raw * scale
        total += jnp.sum(raw * key_weight[:, side].astype(F32), axis=1, keepdims=True)
        raw = jnp.where(lane < HDIM, pltpu.roll(low, HDIM, 1), high)
        value[:, side] = raw * scale
        total += jnp.sum(raw * value_weight[:, side].astype(F32), axis=1, keepdims=True)
    gain_grad[...] = total
    out[...] = jnp.where(place[1] == 1, half[...], two[:, 640:]).astype(F32)


def finish(place, here, came, gain, weights, half):
    whole = pl.BlockSpec(memory_space=pltpu.VMEM)
    return pl.pallas_call(
        finish_kernel,
        in_specs=[pl.BlockSpec(memory_space=pltpu.SMEM)] + [whole] * 9,
        out_specs=[whole] * 5,
        out_shape=[
            jax.ShapeDtypeStruct((32, D), F32),
            jax.ShapeDtypeStruct((32, 256), F32),
            jax.ShapeDtypeStruct((32, 256), F32),
            jax.ShapeDtypeStruct((32, 1), F32),
            jax.ShapeDtypeStruct((32, D), F32),
        ],
        compiler_params=pltpu.CompilerParams(vmem_limit_bytes=16 * 1024 * 1024),
        cost_estimate=pl.CostEstimate(flops=2**19, bytes_accessed=2**20, transcendentals=0),
    )(place, here, *came, gain, *weights, half)


def feed_finish_kernel(place, here, one, two, three, shuffle, gain, *refs):
    weights, grads, gain_grad = refs[:2], refs[2:4], refs[4]
    stacked = [here[...], one[...], two[:, : 4 * WIDE], three[...]]
    scale = gain[...]

    def part(chip):
        which = lax.rem(place[0] - chip + 4, 4)
        item = stacked[0]
        for k in range(1, 4):
            item = jnp.where(which == k, stacked[k], item)
        return item

    parts = [[part(2 * h + k) for h in range(2)] for k in range(2)]
    rows = []
    for item in range(2):
        for k in range(2):
            for half in range(2):
                start = item * WIDE + half * 384
                pieces = [
                    parts[k][h][:, 2 * WIDE * e + start : 2 * WIDE * e + start + 384]
                    for h in range(2)
                    for e in range(2)
                ]
                rows.append(jnp.concatenate(pieces, axis=1))
    raw = dot_nt(jnp.concatenate(rows, axis=0), shuffle[...])
    total = jnp.zeros((32, 1), F32)
    for item in range(2):
        for k in range(4):
            side = slice(1408 * k, 1408 * (k + 1))
            block = raw[32 * (4 * item + k) : 32 * (4 * item + k + 1)]
            grads[item][:, side] = block * scale
            total += jnp.sum(block * weights[item][:, side].astype(F32), axis=1, keepdims=True)
    gain_grad[...] = total


def feed_finish(place, here, came, shuffle, gain, gate_weight, up_weight):
    whole = pl.BlockSpec(memory_space=pltpu.VMEM)
    return pl.pallas_call(
        feed_finish_kernel,
        in_specs=[pl.BlockSpec(memory_space=pltpu.SMEM)] + [whole] * 8,
        out_specs=[whole] * 3,
        out_shape=[
            jax.ShapeDtypeStruct((32, 5632), F32),
            jax.ShapeDtypeStruct((32, 5632), F32),
            jax.ShapeDtypeStruct((32, 1), F32),
        ],
        compiler_params=pltpu.CompilerParams(vmem_limit_bytes=20 * 1024 * 1024),
        cost_estimate=pl.CostEstimate(flops=2**30, bytes_accessed=2**23, transcendentals=0),
    )(place, here, *came, shuffle, gain, gate_weight, up_weight)


def times(left, right):
    return jnp.dot(left, right, preferred_element_type=F32)


def times_t(left, right):
    return lax.dot_general(left, right, (((1,), (1,)), ((), ())), preferred_element_type=F32)


def t_times(left, right):
    return lax.dot_general(left, right, (((0,), (0,)), ((), ())), preferred_element_type=F32)


def rms_scale(rows):
    return lax.rsqrt(jnp.mean(rows * rows, axis=-1, keepdims=True) + norm_eps)


def norm_back(rows, scale, inner):
    return scale * inner - rows * (scale * scale * scale) * jnp.mean(
        inner * rows, axis=-1, keepdims=True
    )


def from_ring(item, step):
    return lax.ppermute(item, RING, [(i, (i - step) % 4) for i in range(4)])


def to_ring(item, step):
    return lax.ppermute(item, RING, [(i, (i + step) % 4) for i in range(4)])


def swap(item, axis):
    return lax.ppermute(item, axis, SWAP)


def share_parts(item, *first):
    own = swap(item, "c")
    ring = after(tuple(from_ring(item, step) for step in STEPS[1:]), *first)
    return [item, *ring, own] + [swap(part, "c") for part in ring]


def pair_blocks(near, far, *first):
    far = after(swap(far, "c"), *first)

    def block(spot):
        here = slice(spot * CAP, (spot + 1) * CAP)
        return near[here].astype(F32) + far[here].astype(F32)

    return (block(0),) + tuple(block(spot).astype(BF16) for spot in (1, 2, 3))


def ring_sum(blocks, *first):
    came = tuple(to_ring(blocks[spot], STEPS[spot]) for spot in (1, 2, 3))
    return blocks[0] + sum(item.astype(F32) for item in after(came, *first))


def spread_columns(chunks, xl, c):
    mine = [jnp.where(c == 0, pair[0], pair[1]) for pair in chunks]
    away = [jnp.where(c == 0, pair[1], pair[0]) for pair in chunks]
    came = swap(jnp.concatenate(away, axis=0), "c")
    rows = mine[0].shape[0]
    both = []
    for k in range(2):
        other = came[k * rows : (k + 1) * rows]
        both.append(
            jnp.concatenate(
                [jnp.where(c == 0, mine[k], other), jnp.where(c == 0, other, mine[k])], axis=0
            )
        )
    kept = jnp.where(xl == 0, both[0], both[1])
    came = swap(jnp.where(xl == 0, both[1], both[0]), "xl")
    return jnp.stack([jnp.where(xl == 0, kept, came), jnp.where(xl == 0, came, kept)])


def gather_four(item, axis, spot, dim):
    parts = [item]
    for step in (1, 2, 3):
        parts.append(lax.ppermute(item, axis, [(i, (i - step) % 4) for i in range(4)]))
    return jnp.stack([pick(parts, (q - spot) % 4) for q in range(4)], axis=dim)


def pick(parts, which):
    out = parts[0]
    for k in range(1, len(parts)):
        out = jnp.where(which == k, parts[k], out)
    return out


def four_pieces(item, spot, dim):
    return [
        lax.dynamic_index_in_dim(item, (spot + step) % 4, dim, keepdims=False) for step in range(4)
    ]


def shifted(item, axis, step):
    return lax.ppermute(item, axis, [(i, (i + step) % 4) for i in range(4)])


def exchange(pieces, axis):
    return tuple(shifted(pieces[step], axis, step) for step in (1, 2, 3))


def four_sum(pieces, came):
    return pieces[0].astype(F32) + sum(item.astype(F32) for item in came)


def row_pairs(step, back):
    pairs = []
    for h in range(2):
        for e in range(2):
            first = 2 * h + e
            one = (h * 4 + first) * 2 + e
            other = (h * 4 + (first + step) % 4) * 2 + e
            pairs.append((other, one) if back else (one, other))
    return pairs


def after(item, *others):
    return lax.optimization_barrier((item,) + others)[0] if others else item


def order_of_columns(xh):
    place = jnp.arange(768)
    core, owner, row = place // 384, (place % 384) // 48, place % 48
    origin = jnp.where(row < 44, 176 * owner + 88 * core + 44 * xh + row, -1)
    return (jnp.arange(1408)[:, None] == origin[None, :]).astype(BF16)


def column_part(item, width, xh):
    out = []
    for k in range(2):
        start = 2 * width * k
        out.append(
            jnp.where(
                xh == 0, item[:, start : start + width], item[:, start + width : start + 2 * width]
            )
        )
    return out


def on_device(
    tokens,
    doc_ids,
    first_gain,
    query_weight,
    key_weight,
    value_weight,
    out_weight,
    second_gain,
    gate_weight,
    up_weight,
    down_weight,
    cotangent,
):
    xh, xl, y, z, c = (lax.axis_index(name) for name in ("xh", "xl", "y", "z", "c"))
    first_col = first_gain.astype(F32)[:, None]
    second_col = second_gain.astype(F32)[:, None]

    def scaled(item, gain):
        return (item.astype(F32) * gain).astype(BF16)

    q_parts = column_part(scaled(query_weight, first_col), 512, xh)
    k_parts = column_part(scaled(key_weight, first_col), 64, xh)
    v_parts = column_part(scaled(value_weight, first_col), 64, xh)
    chunks = [
        [
            jnp.concatenate([q_parts[k][:, 256 * j : 256 * (j + 1)], k_parts[k], v_parts[k]], axis=1)
            for j in range(2)
        ]
        for k in range(2)
    ]
    spread = spread_columns(chunks, xl, c)

    qkv_full = lax.all_gather(spread, ("y", "z"), axis=1, tiled=True).reshape(D, 384)

    wide = jnp.stack([scaled(gate_weight, second_col), scaled(up_weight, second_col)])
    blocks = jnp.concatenate([wide[:, :, 1408 * k : 1408 * (k + 1)] for k in range(4)], axis=0)
    sorted_columns = times(blocks.reshape(256, 1408), order_of_columns(xh)).astype(BF16)
    sorted_columns = sorted_columns.reshape(2, 2, 2, 32, 768)
    chunks = [
        [
            jnp.concatenate(
                [
                    sorted_columns[k, h, item, :, 384 * j : 384 * (j + 1)]
                    for item in range(2)
                    for h in range(2)
                ],
                axis=1,
            )
            for j in range(2)
        ]
        for k in range(2)
    ]
    down_half = jnp.where(xh == 0, down_weight[:44], down_weight[44:])
    down_half = jnp.pad(down_half, ((0, 4), (0, 0)))
    corner = jnp.concatenate(
        [down_half[16 * k : 16 * (k + 1), 2 * WIDE :] for k in range(3)], axis=1
    )
    feed_spread = spread_columns(chunks, xl, c).reshape(128, 2 * WIDE)
    packed = jnp.concatenate([feed_spread, down_half[:, : 2 * WIDE], corner], axis=0)

    source = 2 * xh + c
    came = swap(out_weight, "c")
    head = jnp.concatenate(
        [jnp.where(c == 0, out_weight, came), jnp.where(c == 0, came, out_weight)], axis=0
    )
    lines = [head]
    for step in (1, 2, 3):
        lines.append(lax.ppermute(head, ("xh", "y", "c"), row_pairs(step, False)))
    head = pick(lines, (y - source) % 4)
    out_full = gather_four(head, "z", z, 0).reshape(256, D)

    table = rotary_table()
    rows = tokens.astype(F32)
    first_scale = rms_scale(rows)
    id_rows = jnp.pad(doc_ids.astype(BF16)[None], ((0, 15), (0, D - CAP)))
    payload = jnp.concatenate([(rows * first_scale).astype(BF16), id_rows], axis=0)
    first = share_parts(after(payload, spread, feed_spread))
    packed = after(packed, qkv_full, out_full, *first[1:4])
    packed = lax.all_gather(packed, ("y", "z"), axis=0, tiled=True)

    queries, key_values, mixed, far, near = attend(first, table, qkv_full, out_full)
    upstream = share_parts(after(cotangent, *first[1:4]), mixed)
    far = after(far, upstream[1])
    shuffle = after(jnp.concatenate([order_of_columns(0), order_of_columns(1)], axis=1), mixed)
    blocks = pair_blocks(near, far)
    prepared = prepare_back(first, table, after(queries, *blocks), key_values)
    midway = rows + ring_sum(blocks, shuffle, *prepared)

    second_scale = rms_scale(midway)
    back, down_full = feed_back(upstream, packed)
    second = share_parts((midway * second_scale).astype(BF16), back)
    hidden, grad_feed, far, near = feed_forward(second, packed, back)
    blocks = pair_blocks(near, far)
    pack = feed_grads(second, upstream, after(hidden, *blocks), grad_feed)
    came = tuple(to_ring(blocks[spot], STEPS[spot]) for spot in (1, 2, 3))
    out_far, out_near = output_product(after(hidden, pack), down_full)
    grad_mid, grad_low = norm_back_sum(blocks[0], after(came, pack, out_far), midway, cotangent)
    out_blocks = pair_blocks(out_near, after(out_far, grad_low))
    third = share_parts(grad_low, *out_blocks)
    pack = lax.psum_scatter(after(pack, *came, out_far), ("y", "z"), scatter_dimension=0, tiled=True)

    out_term = out_grads(third, mixed).reshape(4, 64, D)
    out_sent = four_pieces(out_term, z, 0)
    out_came = tuple(shifted(out_sent[step], "z", step) for step in (1, 2))
    grad_qkv, far, near = attend_back(
        third, qkv_full, after(out_full, *out_sent, *out_blocks), prepared
    )
    product = ring_sum(out_blocks, grad_qkv)
    output = (midway + product).astype(BF16)
    out_came += (shifted(after(out_sent[3], grad_qkv), "z", 3),)
    out_part = four_sum(out_sent, after(out_came, product))
    far = after(far, out_part)
    sent = out_part.astype(BF16)
    out_came = tuple(
        lax.ppermute(sent, ("xh", "y", "c"), row_pairs(step, True)) for step in (1, 2, 3)
    )
    qkv_term = qkv_grads(first, after(grad_qkv, sent))
    blocks = pair_blocks(near, far, qkv_term)
    out_came = after(out_came, *blocks)
    out_part = (out_part + sum(item.astype(F32) for item in out_came)).astype(BF16)

    def halves(item):
        low, high = item[:, :32], item[:, 32:]
        return jnp.where(c == 0, low, high), jnp.where(c == 0, high, low)

    sent = four_pieces(after(qkv_term, out_part, *blocks), y, 1)
    came = exchange(sent, "y")
    ring_came = (to_ring(blocks[1], STEPS[1]), to_ring(blocks[2], STEPS[2]))
    corner = jnp.concatenate([pack[176:, 512 * k : 512 * (k + 1)] for k in range(3)], axis=0)
    down_part = jnp.concatenate([pack[128:176], corner], axis=1)
    feed_part = pack[:128].reshape(2, 64, 2 * WIDE)
    feed_mine, feed_away = halves(feed_part)
    came, ring_came, feed_mine, feed_away, down_part = lax.optimization_barrier(
        (came, ring_came, feed_mine, feed_away, down_part)
    )
    sent = four_pieces(four_sum(sent, came).astype(BF16).reshape(2, 4, 64, 384), z, 1)
    came = exchange(sent, "z")
    last_came = to_ring(blocks[3], STEPS[3])
    feed_came = swap(feed_away, "c")
    came, last_came, feed_came = lax.optimization_barrier((came, last_came, feed_came))

    def in_order(mine, came):
        return jnp.where(c == 0, mine, came), jnp.where(c == 0, came, mine)

    def along_ring(both, more):
        here = jnp.where(xl == 0, both[0], both[1])
        there = jnp.where(xl == 0, both[1], both[0])
        across = jnp.concatenate([here, more], axis=1)
        return here, (to_ring(there, 1), to_ring(across, 2), to_ring(there, 3))

    down_wide = jnp.concatenate(
        [down_part[:32], jnp.concatenate([down_part[32:, :1024], down_part[32:, 1024:]], axis=0)],
        axis=1,
    )
    feed_here, feed_came = along_ring(
        jnp.concatenate(in_order(feed_mine, feed_came), axis=2), down_wide
    )

    qkv_part = four_sum(sent, came).astype(BF16)
    qkv_mine, qkv_away = halves(qkv_part)
    away = jnp.where(c == 0, out_part[32:], out_part[:32])
    sent = jnp.concatenate(
        [
            qkv_away.reshape(64, 384),
            jnp.concatenate([away[:, :1024], away[:, 1024:]], axis=0),
        ],
        axis=1,
    )
    came = swap(sent, "c")
    zero, one = in_order(qkv_mine, came[:, :384].reshape(2, 32, 384))
    pair = zero[:, :, 256:].astype(F32) + one[:, :, 256:].astype(F32)
    both = jnp.concatenate([zero[:, :, :256], one[:, :, :256], pair.astype(BF16)], axis=2)
    out_half = jnp.where(
        y % 2 == c,
        jnp.where(c == 0, out_part[:32], out_part[32:]),
        jnp.concatenate([came[:32, 384:], came[32:, 384:]], axis=1),
    )
    both, out_half = lax.optimization_barrier((both, out_half))
    qkv_here, came = along_ring(both, out_half)
    feed_came = after(feed_came, both)

    inner_one = blocks[0] + sum(item.astype(F32) for item in ring_came + (last_came,))
    tokens_grad = grad_mid + norm_back(rows, first_scale, inner_one)
    down_other = feed_came[1][:, 3072:]
    down_other = jnp.concatenate(
        [
            down_other[:, :2048],
            jnp.concatenate([down_other[:16, 2048:], down_other[16:, 2048:]], axis=1),
        ],
        axis=0,
    )
    down_grad = jnp.concatenate(
        [
            jnp.where(xh == 0, down_part, down_other)[:44],
            jnp.where(xh == 0, down_other, down_part)[:44],
        ],
        axis=0,
    ).astype(F32)
    place = jnp.stack([2 * xh + xl, (y // 2 == xh).astype(jnp.int32)]).astype(jnp.int32)
    gate_grad, up_grad, second_grad = feed_finish(
        place, feed_here, feed_came, shuffle, second_col, gate_weight, up_weight
    )
    weights = (query_weight, key_weight, value_weight)
    came = after(came, gate_grad, up_grad, second_grad, down_grad)
    query_grad, key_grad, value_grad, first_grad, out_grad = finish(
        place, qkv_here, came, first_col, weights, out_half
    )

    return (
        output,
        tokens_grad,
        first_grad[:, 0],
        query_grad,
        key_grad,
        value_grad,
        out_grad,
        second_grad[:, 0],
        gate_grad,
        up_grad,
        down_grad,
    )


def solution(mesh):
    fine = Mesh(mesh.devices.reshape(2, 2, 4, 4, 2), ("xh", "xl", "y", "z", "c"))
    everyone = ("xh", "xl", "y", "z", "c")
    group = ("xl", "y", "z", "c")
    in_specs = (
        P(everyone, None),
        P(everyone),
        P(group),
        P(group, None),
        P(group, None),
        P(group, None),
        P(group, None),
        P(group),
        P(group, None),
        P(group, None),
        P(group, None),
        P(everyone, None),
    )
    out_specs = (
        P(everyone, None),
        P(everyone, None),
        P(group),
        P(group, None),
        P(group, None),
        P(group, None),
        P(group, None),
        P(group),
        P(group, None),
        P(group, None),
        P(group, None),
    )
    return jax.shard_map(
        on_device, mesh=fine, in_specs=in_specs, out_specs=out_specs, check_vma=False
    )
```

```python
import jax
import jax.numpy as jnp
import ml_dtypes
import numpy as np
from jax import lax
from jax.experimental import pallas as pl
from jax.experimental.pallas import tpu as pltpu
from jax.sharding import Mesh, PartitionSpec as P

D = 2048
HDIM = 64
CAP = 128
WIDE = 768
BF16 = jnp.bfloat16
F32 = jnp.float32

norm_eps = 1e-05

RING = ("xh", "xl")
SWAP = [(0, 1), (1, 0)]
STEPS = (0, 1, 3, 2)


def dot_nn(left, right):
    return lax.dot_general(left, right, (((1,), (0,)), ((), ())), preferred_element_type=F32)


def dot_nt(left, right):
    return lax.dot_general(left, right, (((1,), (1,)), ((), ())), preferred_element_type=F32)


def dot_tn(left, right):
    return lax.dot_general(left, right, (((0,), (0,)), ((), ())), preferred_element_type=F32)


HBM = pl.BlockSpec(memory_space=pltpu.HBM)


def in_hbm(*items):
    return [pltpu.with_memory_space_constraint(item, pltpu.HBM) for item in items]


def block_copies(parts, whole, sems):
    return [
        pltpu.make_async_copy(
            part.at[pl.ds(0, CAP)], whole.at[pl.ds(CAP * spot, CAP)], sems.at[spot]
        )
        for spot, part in enumerate(parts)
    ]


def id_copies(parts, ids, sems):
    return [
        pltpu.make_async_copy(part.at[pl.ds(CAP, 16), pl.ds(0, CAP)], ids.at[spot], sems.at[spot])
        for spot, part in enumerate(parts)
    ]


def feed_copies(packed, feed, sems):
    copies = []
    for k in range(16):
        for h in range(2):
            copies.append(
                pltpu.make_async_copy(
                    packed.at[pl.ds(192 * k + 64 * h, 64)],
                    feed.at[pl.ds(1024 * h + 64 * k, 64)],
                    sems.at[2 * k + h],
                )
            )
    return copies


def down_copies(packed, down, sems):
    copies = []
    for k in range(16):
        copies.append(
            pltpu.make_async_copy(
                packed.at[pl.ds(192 * k + 128, 48)],
                down.at[pl.ds(48 * k, 48), pl.ds(0, 1536)],
                sems.at[4 * k],
            )
        )
        for h in range(3):
            copies.append(
                pltpu.make_async_copy(
                    packed.at[pl.ds(192 * k + 176, 16), pl.ds(512 * h, 512)],
                    down.at[pl.ds(48 * k + 16 * h, 16), pl.ds(1536, 512)],
                    sems.at[4 * k + 1 + h],
                )
            )
    return copies


def back_kernel(*refs):
    parts, packed, out, down_out, c, down, c_sems, d_sems, out_sems = refs[:8], *refs[8:]
    step = pl.program_id(0)
    loads = block_copies(parts, c, c_sems)
    keep = pltpu.make_async_copy(down, down_out, out_sems.at[0])

    @pl.when(step == 0)
    def _():
        rows = down_copies(packed, down, d_sems)
        for copy in loads[:4] + rows + loads[4:]:
            copy.start()
        for copy in loads[:4] + rows:
            copy.wait()
        keep.start()

    @pl.when(step == 1)
    def _():
        for copy in loads[4:]:
            copy.wait()

    rows = pl.ds(pl.multiple_of(step * 512, 512), 512)
    out[...] = dot_nt(c[rows, :], down[...])

    @pl.when(step == 1)
    def _():
        keep.wait()


def feed_back(c_parts, packed):
    return pl.pallas_call(
        back_kernel,
        grid=(2,),
        in_specs=[HBM] * 9,
        out_specs=[pl.BlockSpec((512, WIDE), lambda i: (i, 0)), HBM],
        out_shape=[jax.ShapeDtypeStruct((1024, WIDE), F32), pltpu.HBM((WIDE, D), BF16)],
        scratch_shapes=[
            pltpu.VMEM((1024, D), BF16),
            pltpu.VMEM((WIDE, D), BF16),
            pltpu.SemaphoreType.DMA((8,)),
            pltpu.SemaphoreType.DMA((64,)),
            pltpu.SemaphoreType.DMA((1,)),
        ],
        compiler_params=pltpu.CompilerParams(vmem_limit_bytes=24 * 1024 * 1024),
        cost_estimate=pl.CostEstimate(
            flops=2 * 1024 * D * WIDE, bytes_accessed=10 * 2**20, transcendentals=0
        ),
    )(*in_hbm(*c_parts, packed))


def feed_kernel(*refs):
    x_parts, packed, back = refs[:8], refs[8], refs[9]
    hidden, grads, far, near, x, feed, x_sems, f_sems = refs[10:]
    step = pl.program_id(0)
    first = block_copies(x_parts, x, x_sems)

    @pl.when(step == 0)
    def _():
        second = feed_copies(packed, feed, f_sems)
        for copy in first[4:6] + second + first[6:] + first[:4]:
            copy.start()
        for copy in first[4:6] + second:
            copy.wait()

    for k in range(1, 4):

        @pl.when(step == k)
        def _(k=k):
            spot = (2 * k + 4) % 8
            for copy in first[spot : spot + 2]:
                copy.wait()

    rows = pl.ds(pl.multiple_of(((step + 2) % 4) * 256, 256), 256)
    block = x[rows, :]
    for k in range(0, WIDE, 256):
        here, beside = slice(k, k + 256), slice(WIDE + k, WIDE + k + 256)
        gate = dot_nn(block, feed[:, here])
        up = dot_nn(block, feed[:, beside])
        slope = back[:, here]
        sig = jax.nn.sigmoid(gate)
        silu = gate * sig
        hidden[:, here] = (silu * up).astype(BF16)
        grads[:, here] = (slope * up * (sig * (1.0 + gate * (1.0 - sig)))).astype(BF16)
        grads[:, beside] = (slope * silu).astype(BF16)
    inner = dot_nt(grads[...], feed[...])

    @pl.when(step < 2)
    def _():
        far[...] = inner.astype(BF16)

    @pl.when(step >= 2)
    def _():
        near[...] = inner.astype(BF16)


def feed_forward(x_parts, packed, back):
    row = lambda i: ((i + 2) % 4, 0)
    return pl.pallas_call(
        feed_kernel,
        grid=(4,),
        in_specs=[HBM] * 9 + [pl.BlockSpec((256, WIDE), row)],
        out_specs=[
            pl.BlockSpec((256, WIDE), row),
            pl.BlockSpec((256, 2 * WIDE), row),
            pl.BlockSpec((256, D), lambda i: (jnp.minimum(i, 1), 0)),
            pl.BlockSpec((256, D), lambda i: (jnp.maximum(i - 2, 0), 0)),
        ],
        out_shape=[
            jax.ShapeDtypeStruct((1024, WIDE), BF16),
            jax.ShapeDtypeStruct((1024, 2 * WIDE), BF16),
            jax.ShapeDtypeStruct((512, D), BF16),
            jax.ShapeDtypeStruct((512, D), BF16),
        ],
        scratch_shapes=[
            pltpu.VMEM((1024, D), BF16),
            pltpu.VMEM((D, 2 * WIDE), BF16),
            pltpu.SemaphoreType.DMA((8,)),
            pltpu.SemaphoreType.DMA((32,)),
        ],
        compiler_params=pltpu.CompilerParams(vmem_limit_bytes=36 * 1024 * 1024),
        cost_estimate=pl.CostEstimate(
            flops=2 * 1024 * D * WIDE * 4, bytes_accessed=24 * 2**20, transcendentals=1024 * WIDE
        ),
    )(*in_hbm(*x_parts, packed), back)


def grads_kernel(*refs):
    x_parts, c_parts, hidden_hbm, grads_hbm = refs[:8], refs[8:16], refs[16], refs[17]
    out = refs[18]
    x, c, hidden, grads, pack, x_sems, c_sems, in_sems, sems = refs[19:]
    first = block_copies(x_parts, x, x_sems)
    second = block_copies(c_parts, c, c_sems)
    loads = [
        pltpu.make_async_copy(grads_hbm, grads, in_sems.at[0]),
        pltpu.make_async_copy(hidden_hbm, hidden, in_sems.at[1]),
    ]
    for copy in first + loads + second:
        copy.start()
    for copy in first + loads[:1]:
        copy.wait()
    stores = []

    def store(row, rows):
        copy = pltpu.make_async_copy(
            pack.at[pl.ds(row, rows)], out.at[pl.ds(row, rows)], sems.at[len(stores)]
        )
        copy.start()
        stores.append(copy)

    for k in range(8):
        tile = dot_tn(x[:, 256 * k : 256 * (k + 1)], grads[...]).astype(BF16)
        half, spot = k // 4, (k % 4) * 4
        for j in range(4):
            row = 192 * (spot + j) + 64 * half
            pack[row : row + 64, :] = tile[64 * j : 64 * (j + 1)]
            store(row, 64)
    for copy in second + loads[1:]:
        copy.wait()
    for k in range(2):
        tile = dot_tn(hidden[:, 384 * k : 384 * (k + 1)], c[...]).astype(BF16)
        for j in range(8):
            row = 192 * (8 * k + j) + 128
            piece = tile[48 * j : 48 * (j + 1)]
            pack[row : row + 48, :] = piece[:, :1536]
            for h in range(3):
                pack[row + 48 : row + 64, 512 * h : 512 * (h + 1)] = piece[
                    16 * h : 16 * (h + 1), 1536:
                ]
            store(row, 64)
    for copy in stores:
        copy.wait()


def feed_grads(x_parts, c_parts, hidden, grads):
    return pl.pallas_call(
        grads_kernel,
        in_specs=[HBM] * 18,
        out_specs=HBM,
        out_shape=jax.ShapeDtypeStruct((3072, 1536), BF16),
        scratch_shapes=[
            pltpu.VMEM((1024, D), BF16),
            pltpu.VMEM((1024, D), BF16),
            pltpu.VMEM((1024, WIDE), BF16),
            pltpu.VMEM((1024, 2 * WIDE), BF16),
            pltpu.VMEM((3072, 2 * WIDE), BF16),
            pltpu.SemaphoreType.DMA((8,)),
            pltpu.SemaphoreType.DMA((8,)),
            pltpu.SemaphoreType.DMA((2,)),
            pltpu.SemaphoreType.DMA((48,)),
        ],
        compiler_params=pltpu.CompilerParams(vmem_limit_bytes=60 * 1024 * 1024),
        cost_estimate=pl.CostEstimate(
            flops=2 * 1024 * D * WIDE * 3, bytes_accessed=22 * 2**20, transcendentals=0
        ),
    )(*in_hbm(*x_parts, *c_parts, hidden, grads))


def output_kernel(hidden_hbm, down_hbm, far, near, hidden, down, total, sems, out_sems):
    copies = [
        pltpu.make_async_copy(down_hbm, down, sems.at[0]),
        pltpu.make_async_copy(hidden_hbm, hidden, sems.at[1]),
    ]
    for copy in copies:
        copy.start()
    for copy in copies:
        copy.wait()
    stores = []
    for k, out in ((1, far), (0, near)):
        total[k] = dot_nn(hidden[512 * k : 512 * (k + 1)], down[...]).astype(BF16)
        stores.append(pltpu.make_async_copy(total.at[k], out, out_sems.at[k]))
        stores[-1].start()
    for copy in stores:
        copy.wait()


def output_product(hidden, down_full):
    return pl.pallas_call(
        output_kernel,
        in_specs=[HBM, HBM],
        out_specs=[HBM, HBM],
        out_shape=[pltpu.HBM((512, D), BF16), pltpu.HBM((512, D), BF16)],
        scratch_shapes=[
            pltpu.VMEM((1024, WIDE), BF16),
            pltpu.VMEM((WIDE, D), BF16),
            pltpu.VMEM((2, 512, D), BF16),
            pltpu.SemaphoreType.DMA((2,)),
            pltpu.SemaphoreType.DMA((2,)),
        ],
        compiler_params=pltpu.CompilerParams(vmem_limit_bytes=24 * 1024 * 1024),
        cost_estimate=pl.CostEstimate(
            flops=2 * 1024 * D * WIDE, bytes_accessed=11 * 2**20, transcendentals=0
        ),
    )(*in_hbm(hidden, down_full))


def rotary_table():
    place = np.arange(CAP, dtype=np.float32)[:, None]
    inverse = np.float32(10000.0) ** (np.arange(32, dtype=np.float32) * np.float32(-2.0 / HDIM))
    angle = (place * inverse).astype(np.float32)
    cosine, sine = np.cos(angle), np.sin(angle)
    zero, one = np.zeros((CAP, 64), np.float32), np.ones((CAP, 64), np.float32)
    ahead = np.concatenate([-sine, zero[:, :32]], axis=1)
    behind = np.concatenate([zero[:, :32], sine], axis=1)
    cosine = np.concatenate([cosine, cosine], axis=1)
    table = np.concatenate(
        [cosine, cosine, ahead, ahead, behind, behind, cosine, one, ahead, zero, behind, zero], axis=1
    )
    high = table.astype(ml_dtypes.bfloat16)
    rest = (table - high.astype(np.float32)).astype(ml_dtypes.bfloat16)
    return jnp.asarray(np.stack([high, rest]))


def lane_of(shape, dim):
    return lax.broadcasted_iota(jnp.int32, shape, dim)


def block_tables(ids, table):
    row = jnp.broadcast_to(ids.astype(F32)[:1], (CAP, CAP))
    same = row == row.T
    to, frm = lane_of((CAP, CAP), 0), lane_of((CAP, CAP), 1)
    place = jnp.sum(jnp.where(same & (frm < to), 1.0, 0.0), axis=1, keepdims=True)
    chosen = (frm.astype(F32) == place).astype(BF16)
    factors = dot_nn(chosen, table[0]) + dot_nn(chosen, table[1])
    return same & (frm <= to), factors


def turned(item, factors, sign):
    def three(k):
        pair = factors[:, CAP * k : CAP * (k + 1)]
        return jnp.concatenate([pair, pair, factors[:, CAP * (k + 3) : CAP * (k + 4)]], axis=1)

    other = pltpu.roll(item, 352, 1) * three(1) + pltpu.roll(item, 32, 1) * three(2)
    return item * three(0) + sign * other


def stack_heads(item):
    head = lane_of((CAP, 256), 1) // 64
    return jnp.concatenate([jnp.where(head == h, item, 0).astype(BF16) for h in range(4)], axis=0)


def spreads():
    lane, own = lane_of((CAP, 256), 1) % 64, lane_of((CAP, 256), 0)
    return (lane == own).astype(BF16), (lane + 64 == own).astype(BF16)


def softmax_heads(queries, keys, allowed):
    scores = dot_nt(stack_heads(queries), keys) * 0.125
    out = []
    for h in range(4):
        part = jnp.where(allowed, scores[CAP * h : CAP * (h + 1)], -1e30)
        expo = jnp.exp(part - jnp.max(part, axis=1, keepdims=True))
        out.append(expo / jnp.sum(expo, axis=1, keepdims=True))
    return out


def attend_kernel(*refs):
    parts, table, w_hbm, o_hbm = refs[:8], refs[8], refs[9], refs[10]
    queries, key_values, mixed, far, near = refs[11:16]
    x, ids, w, o, x_sems, i_sems, w_sems = refs[16:]
    step = pl.program_id(0)
    blocks, numbers = block_copies(parts, x, x_sems), id_copies(parts, ids, i_sems)
    loads = [
        pltpu.make_async_copy(w_hbm, w, w_sems.at[0]),
        pltpu.make_async_copy(o_hbm, o, w_sems.at[1]),
    ]

    @pl.when(step == 0)
    def _():
        for copy in loads[:1] + blocks[4:] + numbers[4:] + loads[1:] + blocks[:4] + numbers[:4]:
            copy.start()
        for copy in loads[:1] + blocks[4:] + numbers[4:]:
            copy.wait()

    @pl.when(step == 1)
    def _():
        for copy in blocks[:4] + numbers[:4]:
            copy.wait()

    half = 1 - step
    rows = pl.ds(pl.multiple_of(half * 512, 512), 512)
    qkv = dot_nn(x[rows, :], w[...])
    to_key, to_value = spreads()
    for k in range(4):
        allowed, factors = block_tables(ids[half * 4 + k], table)
        block = turned(qkv[CAP * k : CAP * (k + 1)], factors, 1.0).astype(BF16)
        here = slice(CAP * k, CAP * (k + 1))
        queries[here, :] = block[:, :256]
        key_values[here, :] = block[:, 256:]
        keys = dot_nn(block[:, 256:], to_key).astype(BF16)
        values = dot_nn(block[:, 256:], to_value).astype(BF16)
        probs = softmax_heads(block[:, :256], keys, allowed)
        probs = jnp.concatenate([item.astype(BF16) for item in probs], axis=1)
        mixed[here, :] = dot_nn(probs, stack_heads(values)).astype(BF16)

    @pl.when(step == 0)
    def _():
        loads[1].wait()

    total = dot_nn(mixed[...], o[...])

    @pl.when(step == 0)
    def _():
        far[...] = total.astype(BF16)

    @pl.when(step == 1)
    def _():
        near[...] = total.astype(BF16)


def attend(parts, table, qkv_full, out_full):
    row = lambda i: (1 - i, 0)
    still = lambda i: (0, 0)
    return pl.pallas_call(
        attend_kernel,
        grid=(2,),
        in_specs=[HBM] * 8 + [pl.BlockSpec((2, CAP, 768), lambda i: (0, 0, 0))] + [HBM] * 2,
        out_specs=[
            pl.BlockSpec((512, 256), row),
            pl.BlockSpec((512, CAP), row),
            pl.BlockSpec((512, 256), row),
            pl.BlockSpec((512, D), still),
            pl.BlockSpec((512, D), still),
        ],
        out_shape=[
            jax.ShapeDtypeStruct((1024, 256), BF16),
            jax.ShapeDtypeStruct((1024, CAP), BF16),
            jax.ShapeDtypeStruct((1024, 256), BF16),
            jax.ShapeDtypeStruct((512, D), BF16),
            jax.ShapeDtypeStruct((512, D), BF16),
        ],
        scratch_shapes=[
            pltpu.VMEM((1024, D), BF16),
            pltpu.VMEM((8, 16, CAP), BF16),
            pltpu.VMEM((D, 384), BF16),
            pltpu.VMEM((256, D), BF16),
            pltpu.SemaphoreType.DMA((8,)),
            pltpu.SemaphoreType.DMA((8,)),
            pltpu.SemaphoreType.DMA((2,)),
        ],
        compiler_params=pltpu.CompilerParams(vmem_limit_bytes=32 * 1024 * 1024),
        cost_estimate=pl.CostEstimate(
            flops=2 * 1024 * D * 640 * 2, bytes_accessed=15 * 2**20, transcendentals=2**19
        ),
    )(*in_hbm(*parts), table, *in_hbm(qkv_full, out_full))


def prepare_kernel(*refs):
    parts, table, queries, key_values = refs[:8], *refs[8:11]
    probs, keys, values, folded, factors, ids, i_sems = refs[11:]
    step = pl.program_id(0)

    @pl.when(step == 0)
    def _():
        copies = id_copies(parts, ids, i_sems)
        for copy in copies:
            copy.start()
        for copy in copies:
            copy.wait()

    to_key, to_value = spreads()
    allowed, around = block_tables(ids[step], table)
    factors[...] = around
    both = key_values[...]
    keys[...] = dot_nn(both, to_key).astype(BF16)
    values[...] = dot_nn(both, to_value).astype(BF16)
    folded[...] = dot_nt(stack_heads(queries[...]), to_key).astype(BF16)
    for h, item in enumerate(softmax_heads(queries[...], keys[...], allowed)):
        probs[CAP * h : CAP * (h + 1), :] = item


def prepare_back(id_parts, table, queries, key_values):
    row = lambda i: (i, 0)
    sizes = ((512, CAP, F32), (CAP, 256, BF16), (CAP, 256, BF16), (512, CAP, BF16), (CAP, 768, F32))
    return pl.pallas_call(
        prepare_kernel,
        grid=(8,),
        in_specs=[HBM] * 8
        + [pl.BlockSpec((2, CAP, 768), lambda i: (0, 0, 0))]
        + [pl.BlockSpec((CAP, 256), row), pl.BlockSpec((CAP, CAP), row)],
        out_specs=[pl.BlockSpec((rows, lanes), row) for rows, lanes, _ in sizes],
        out_shape=[jax.ShapeDtypeStruct((8 * rows, lanes), kind) for rows, lanes, kind in sizes],
        scratch_shapes=[pltpu.VMEM((8, 16, CAP), BF16), pltpu.SemaphoreType.DMA((8,))],
        compiler_params=pltpu.CompilerParams(vmem_limit_bytes=20 * 1024 * 1024),
        cost_estimate=pl.CostEstimate(
            flops=2**30, bytes_accessed=9 * 2**20, transcendentals=2**19
        ),
    )(*in_hbm(*id_parts), table, queries, key_values)


def attend_back_kernel(*refs):
    parts, w_hbm, o_hbm = refs[:8], refs[8], refs[9]
    probs, keys, values, folded, factors = refs[10:15]
    grads, far, near, g, w, o, g_sems, w_sems = refs[15:]
    step = pl.program_id(0)
    blocks = block_copies(parts, g, g_sems)
    loads = [
        pltpu.make_async_copy(o_hbm, o, w_sems.at[0]),
        pltpu.make_async_copy(w_hbm, w, w_sems.at[1]),
    ]

    @pl.when(step == 0)
    def _():
        for copy in loads[:1] + blocks[4:] + loads[1:] + blocks[:4]:
            copy.start()
        for copy in loads[:1] + blocks[4:]:
            copy.wait()

    @pl.when(step == 1)
    def _():
        for copy in blocks[:4]:
            copy.wait()

    rows = pl.ds(pl.multiple_of((1 - step) * 512, 512), 512)
    grad_mixed = dot_nt(g[rows, :], o[...]).astype(BF16)
    to_value = spreads()[1]
    for k in range(4):
        here, heads = slice(CAP * k, CAP * (k + 1)), slice(512 * k, 512 * (k + 1))
        grad_heads = stack_heads(grad_mixed[here])
        part = dot_nt(grad_heads, values[here, :])
        prob = probs[heads, :]
        scores = (prob * (part - jnp.sum(prob * part, axis=1, keepdims=True))).astype(BF16)
        beside = jnp.concatenate([scores[CAP * h : CAP * (h + 1)] for h in range(4)], axis=1)
        grad_query = dot_nn(beside, stack_heads(keys[here, :])) * 0.125
        grad_folded = dot_nt(grad_heads, to_value).astype(BF16)
        grad_both = dot_tn(scores, folded[heads, :]) * 0.125 + dot_tn(prob.astype(BF16), grad_folded)
        item = jnp.concatenate([grad_query, grad_both], axis=1)
        grads[here, :] = turned(item, factors[here, :], -1.0).astype(BF16)

    @pl.when(step == 0)
    def _():
        loads[1].wait()

    total = dot_nt(grads[...], w[...]).astype(BF16)

    @pl.when(step == 0)
    def _():
        far[...] = total

    @pl.when(step == 1)
    def _():
        near[...] = total


def attend_back(parts, qkv_full, out_full, prepared):
    row = lambda i: (1 - i, 0)
    return pl.pallas_call(
        attend_back_kernel,
        grid=(2,),
        in_specs=[HBM] * 10
        + [
            pl.BlockSpec((2048, CAP), row),
            pl.BlockSpec((512, 256), row),
            pl.BlockSpec((512, 256), row),
            pl.BlockSpec((2048, CAP), row),
            pl.BlockSpec((512, 768), row),
        ],
        out_specs=[
            pl.BlockSpec((512, 384), row),
            pl.BlockSpec((512, D), lambda i: (0, 0)),
            pl.BlockSpec((512, D), lambda i: (0, 0)),
        ],
        out_shape=[
            jax.ShapeDtypeStruct((1024, 384), BF16),
            jax.ShapeDtypeStruct((512, D), BF16),
            jax.ShapeDtypeStruct((512, D), BF16),
        ],
        scratch_shapes=[
            pltpu.VMEM((1024, D), BF16),
            pltpu.VMEM((D, 384), BF16),
            pltpu.VMEM((256, D), BF16),
            pltpu.SemaphoreType.DMA((8,)),
            pltpu.SemaphoreType.DMA((2,)),
        ],
        compiler_params=pltpu.CompilerParams(vmem_limit_bytes=36 * 1024 * 1024),
        cost_estimate=pl.CostEstimate(
            flops=2 * 1024 * D * 640 * 2, bytes_accessed=15 * 2**20, transcendentals=0
        ),
    )(*in_hbm(*parts, qkv_full, out_full), *prepared)


def out_grads_kernel(*refs):
    parts, mixed_hbm, out, g, mixed, sems, in_sems = refs[:8], *refs[8:]
    copies = block_copies(parts, g, sems)
    copies.append(pltpu.make_async_copy(mixed_hbm, mixed, in_sems.at[0]))
    for copy in copies:
        copy.start()
    for copy in copies:
        copy.wait()
    out[...] = dot_tn(mixed[...], g[...]).astype(BF16)


def out_grads(parts, mixed):
    return pl.pallas_call(
        out_grads_kernel,
        in_specs=[HBM] * 9,
        out_specs=pl.BlockSpec(memory_space=pltpu.VMEM),
        out_shape=jax.ShapeDtypeStruct((256, D), BF16),
        scratch_shapes=[
            pltpu.VMEM((1024, D), BF16),
            pltpu.VMEM((1024, 256), BF16),
            pltpu.SemaphoreType.DMA((8,)),
            pltpu.SemaphoreType.DMA((1,)),
        ],
        compiler_params=pltpu.CompilerParams(vmem_limit_bytes=24 * 1024 * 1024),
        cost_estimate=pl.CostEstimate(
            flops=2 * 1024 * D * 256, bytes_accessed=6 * 2**20, transcendentals=0
        ),
    )(*in_hbm(*parts, mixed))


def qkv_grads_kernel(*refs):
    parts, grads_hbm, out, x, grads, sems, in_sems = refs[:8], *refs[8:]
    copies = block_copies(parts, x, sems)
    copies.append(pltpu.make_async_copy(grads_hbm, grads, in_sems.at[0]))
    for copy in copies:
        copy.start()
    for copy in copies:
        copy.wait()
    for k in range(8):
        out[k // 4, k % 4] = dot_tn(x[:, 256 * k : 256 * (k + 1)], grads[...]).astype(BF16)


def qkv_grads(parts, grads):
    return pl.pallas_call(
        qkv_grads_kernel,
        in_specs=[HBM] * 9,
        out_specs=pl.BlockSpec(memory_space=pltpu.VMEM),
        out_shape=jax.ShapeDtypeStruct((2, 4, 256, 384), BF16),
        scratch_shapes=[
            pltpu.VMEM((1024, D), BF16),
            pltpu.VMEM((1024, 384), BF16),
            pltpu.SemaphoreType.DMA((8,)),
            pltpu.SemaphoreType.DMA((1,)),
        ],
        compiler_params=pltpu.CompilerParams(vmem_limit_bytes=24 * 1024 * 1024),
        cost_estimate=pl.CostEstimate(
            flops=2 * 1024 * D * 384, bytes_accessed=6 * 2**20, transcendentals=0
        ),
    )(*in_hbm(*parts, grads))


def norm_back_kernel(own, one, two, three, rows, upstream, grad, low):
    x = rows[...]
    inner = own[...] + one[...].astype(F32) + two[...].astype(F32) + three[...].astype(F32)
    scale = lax.rsqrt(jnp.mean(x * x, axis=1, keepdims=True) + norm_eps)
    slope = jnp.mean(inner * x, axis=1, keepdims=True)
    total = upstream[...].astype(F32) + scale * inner - x * (scale * scale * scale * slope)
    grad[...] = total
    low[...] = total.astype(BF16)


def norm_back_sum(own, came, rows, upstream):
    spec = pl.BlockSpec((32, D), lambda i: (i, 0))
    return pl.pallas_call(
        norm_back_kernel,
        grid=(CAP // 32,),
        in_specs=[spec] * 6,
        out_specs=[spec] * 2,
        out_shape=[pltpu.HBM((CAP, D), F32), pltpu.HBM((CAP, D), BF16)],
        compiler_params=pltpu.CompilerParams(vmem_limit_bytes=16 * 1024 * 1024),
        cost_estimate=pl.CostEstimate(
            flops=20 * CAP * D, bytes_accessed=6 * 2**20, transcendentals=CAP
        ),
    )(*in_hbm(own, *came), rows, upstream)


def finish_kernel(place, here, one, two, three, gain, *refs):
    query_weight, key_weight, value_weight, half, query, key, value, gain_grad, out = refs
    stacked = [here[...], one[...], two[:, :640], three[...]]
    scale = gain[...]
    lane = lane_of((32, CAP), 1)
    parts = []
    for chip in (0, 2, 1, 3):
        which = lax.rem(place[0] - chip + 4, 4)
        item = stacked[0]
        for k in range(1, 4):
            item = jnp.where(which == k, stacked[k], item)
        parts.append(item.astype(F32))
    total = jnp.zeros((32, 1), F32)
    for k, item in enumerate(parts):
        side = slice(512 * k, 512 * (k + 1))
        raw = item[:, :512]
        query[:, side] = raw * scale
        total += jnp.sum(raw * query_weight[:, side].astype(F32), axis=1, keepdims=True)
    for k in range(2):
        side = slice(CAP * k, CAP * (k + 1))
        low, high = parts[2 * k][:, 512:], parts[2 * k + 1][:, 512:]
        raw = jnp.where(lane < HDIM, low, pltpu.roll(high, HDIM, 1))
        key[:, side] = raw * scale
        total += jnp.sum(raw * key_weight[:, side].astype(F32), axis=1, keepdims=True)
        raw = jnp.where(lane < HDIM, pltpu.roll(low, HDIM, 1), high)
        value[:, side] = raw * scale
        total += jnp.sum(raw * value_weight[:, side].astype(F32), axis=1, keepdims=True)
    gain_grad[...] = total
    out[...] = jnp.where(place[1] == 1, half[...], two[:, 640:]).astype(F32)


def finish(place, here, came, gain, weights, half):
    whole = pl.BlockSpec(memory_space=pltpu.VMEM)
    return pl.pallas_call(
        finish_kernel,
        in_specs=[pl.BlockSpec(memory_space=pltpu.SMEM)] + [whole] * 9,
        out_specs=[whole] * 5,
        out_shape=[
            jax.ShapeDtypeStruct((32, D), F32),
            jax.ShapeDtypeStruct((32, 256), F32),
            jax.ShapeDtypeStruct((32, 256), F32),
            jax.ShapeDtypeStruct((32, 1), F32),
            jax.ShapeDtypeStruct((32, D), F32),
        ],
        compiler_params=pltpu.CompilerParams(vmem_limit_bytes=16 * 1024 * 1024),
        cost_estimate=pl.CostEstimate(flops=2**19, bytes_accessed=2**20, transcendentals=0),
    )(place, here, *came, gain, *weights, half)


def feed_finish_kernel(place, here, one, two, three, shuffle, gain, *refs):
    weights, grads, gain_grad = refs[:2], refs[2:4], refs[4]
    stacked = [here[...], one[...], two[:, : 4 * WIDE], three[...]]
    scale = gain[...]

    def part(chip):
        which = lax.rem(place[0] - chip + 4, 4)
        item = stacked[0]
        for k in range(1, 4):
            item = jnp.where(which == k, stacked[k], item)
        return item

    parts = [[part(2 * h + k) for h in range(2)] for k in range(2)]
    rows = []
    for item in range(2):
        for k in range(2):
            for half in range(2):
                start = item * WIDE + half * 384
                pieces = [
                    parts[k][h][:, 2 * WIDE * e + start : 2 * WIDE * e + start + 384]
                    for h in range(2)
                    for e in range(2)
                ]
                rows.append(jnp.concatenate(pieces, axis=1))
    raw = dot_nt(jnp.concatenate(rows, axis=0), shuffle[...])
    total = jnp.zeros((32, 1), F32)
    for item in range(2):
        for k in range(4):
            side = slice(1408 * k, 1408 * (k + 1))
            block = raw[32 * (4 * item + k) : 32 * (4 * item + k + 1)]
            grads[item][:, side] = block * scale
            total += jnp.sum(block * weights[item][:, side].astype(F32), axis=1, keepdims=True)
    gain_grad[...] = total


def feed_finish(place, here, came, shuffle, gain, gate_weight, up_weight):
    whole = pl.BlockSpec(memory_space=pltpu.VMEM)
    return pl.pallas_call(
        feed_finish_kernel,
        in_specs=[pl.BlockSpec(memory_space=pltpu.SMEM)] + [whole] * 8,
        out_specs=[whole] * 3,
        out_shape=[
            jax.ShapeDtypeStruct((32, 5632), F32),
            jax.ShapeDtypeStruct((32, 5632), F32),
            jax.ShapeDtypeStruct((32, 1), F32),
        ],
        compiler_params=pltpu.CompilerParams(vmem_limit_bytes=20 * 1024 * 1024),
        cost_estimate=pl.CostEstimate(flops=2**30, bytes_accessed=2**23, transcendentals=0),
    )(place, here, *came, shuffle, gain, gate_weight, up_weight)


def times(left, right):
    return jnp.dot(left, right, preferred_element_type=F32)


def times_t(left, right):
    return lax.dot_general(left, right, (((1,), (1,)), ((), ())), preferred_element_type=F32)


def t_times(left, right):
    return lax.dot_general(left, right, (((0,), (0,)), ((), ())), preferred_element_type=F32)


def rms_scale(rows):
    return lax.rsqrt(jnp.mean(rows * rows, axis=-1, keepdims=True) + norm_eps)


def norm_back(rows, scale, inner):
    return scale * inner - rows * (scale * scale * scale) * jnp.mean(
        inner * rows, axis=-1, keepdims=True
    )


def from_ring(item, step):
    return lax.ppermute(item, RING, [(i, (i - step) % 4) for i in range(4)])


def to_ring(item, step):
    return lax.ppermute(item, RING, [(i, (i + step) % 4) for i in range(4)])


def swap(item, axis):
    return lax.ppermute(item, axis, SWAP)


def share_parts(item, *first):
    own = swap(item, "c")
    ring = after(tuple(from_ring(item, step) for step in STEPS[1:]), *first)
    return [item, *ring, own] + [swap(part, "c") for part in ring]


def pair_blocks(near, far, *first):
    far = after(swap(far, "c"), *first)

    def block(spot):
        here = slice(spot * CAP, (spot + 1) * CAP)
        return near[here].astype(F32) + far[here].astype(F32)

    return (block(0),) + tuple(block(spot).astype(BF16) for spot in (1, 2, 3))


def ring_sum(blocks, *first):
    came = tuple(to_ring(blocks[spot], STEPS[spot]) for spot in (1, 2, 3))
    return blocks[0] + sum(item.astype(F32) for item in after(came, *first))


def spread_columns(chunks, xl, c):
    mine = [jnp.where(c == 0, pair[0], pair[1]) for pair in chunks]
    away = [jnp.where(c == 0, pair[1], pair[0]) for pair in chunks]
    came = swap(jnp.concatenate(away, axis=0), "c")
    rows = mine[0].shape[0]
    both = []
    for k in range(2):
        other = came[k * rows : (k + 1) * rows]
        both.append(
            jnp.concatenate(
                [jnp.where(c == 0, mine[k], other), jnp.where(c == 0, other, mine[k])], axis=0
            )
        )
    kept = jnp.where(xl == 0, both[0], both[1])
    came = swap(jnp.where(xl == 0, both[1], both[0]), "xl")
    return jnp.stack([jnp.where(xl == 0, kept, came), jnp.where(xl == 0, came, kept)])


def gather_four(item, axis, spot, dim):
    parts = [item]
    for step in (1, 2, 3):
        parts.append(lax.ppermute(item, axis, [(i, (i - step) % 4) for i in range(4)]))
    return jnp.stack([pick(parts, (q - spot) % 4) for q in range(4)], axis=dim)


def pick(parts, which):
    out = parts[0]
    for k in range(1, len(parts)):
        out = jnp.where(which == k, parts[k], out)
    return out


def four_pieces(item, spot, dim):
    return [
        lax.dynamic_index_in_dim(item, (spot + step) % 4, dim, keepdims=False) for step in range(4)
    ]


def shifted(item, axis, step):
    return lax.ppermute(item, axis, [(i, (i + step) % 4) for i in range(4)])


def exchange(pieces, axis):
    return tuple(shifted(pieces[step], axis, step) for step in (1, 2, 3))


def four_sum(pieces, came):
    return pieces[0].astype(F32) + sum(item.astype(F32) for item in came)


def row_pairs(step, back):
    pairs = []
    for h in range(2):
        for e in range(2):
            first = 2 * h + e
            one = (h * 4 + first) * 2 + e
            other = (h * 4 + (first + step) % 4) * 2 + e
            pairs.append((other, one) if back else (one, other))
    return pairs


def after(item, *others):
    return lax.optimization_barrier((item,) + others)[0] if others else item


def order_of_columns(xh):
    place = jnp.arange(768)
    core, owner, row = place // 384, (place % 384) // 48, place % 48
    origin = jnp.where(row < 44, 176 * owner + 88 * core + 44 * xh + row, -1)
    return (jnp.arange(1408)[:, None] == origin[None, :]).astype(BF16)


def column_part(item, width, xh):
    out = []
    for k in range(2):
        start = 2 * width * k
        out.append(
            jnp.where(
                xh == 0, item[:, start : start + width], item[:, start + width : start + 2 * width]
            )
        )
    return out


def on_device(
    tokens,
    doc_ids,
    first_gain,
    query_weight,
    key_weight,
    value_weight,
    out_weight,
    second_gain,
    gate_weight,
    up_weight,
    down_weight,
    cotangent,
):
    xh, xl, y, z, c = (lax.axis_index(name) for name in ("xh", "xl", "y", "z", "c"))
    first_col = first_gain.astype(F32)[:, None]
    second_col = second_gain.astype(F32)[:, None]

    def scaled(item, gain):
        return (item.astype(F32) * gain).astype(BF16)

    q_parts = column_part(scaled(query_weight, first_col), 512, xh)
    k_parts = column_part(scaled(key_weight, first_col), 64, xh)
    v_parts = column_part(scaled(value_weight, first_col), 64, xh)
    chunks = [
        [
            jnp.concatenate([q_parts[k][:, 256 * j : 256 * (j + 1)], k_parts[k], v_parts[k]], axis=1)
            for j in range(2)
        ]
        for k in range(2)
    ]
    spread = spread_columns(chunks, xl, c)

    qkv_full = lax.all_gather(spread, ("y", "z"), axis=1, tiled=True).reshape(D, 384)

    wide = jnp.stack([scaled(gate_weight, second_col), scaled(up_weight, second_col)])
    blocks = jnp.concatenate([wide[:, :, 1408 * k : 1408 * (k + 1)] for k in range(4)], axis=0)
    sorted_columns = times(blocks.reshape(256, 1408), order_of_columns(xh)).astype(BF16)
    sorted_columns = sorted_columns.reshape(2, 2, 2, 32, 768)
    chunks = [
        [
            jnp.concatenate(
                [
                    sorted_columns[k, h, item, :, 384 * j : 384 * (j + 1)]
                    for item in range(2)
                    for h in range(2)
                ],
                axis=1,
            )
            for j in range(2)
        ]
        for k in range(2)
    ]
    down_half = jnp.where(xh == 0, down_weight[:44], down_weight[44:])
    down_half = jnp.pad(down_half, ((0, 4), (0, 0)))
    corner = jnp.concatenate(
        [down_half[16 * k : 16 * (k + 1), 2 * WIDE :] for k in range(3)], axis=1
    )
    feed_spread = spread_columns(chunks, xl, c).reshape(128, 2 * WIDE)
    packed = jnp.concatenate([feed_spread, down_half[:, : 2 * WIDE], corner], axis=0)

    source = 2 * xh + c
    came = swap(out_weight, "c")
    head = jnp.concatenate(
        [jnp.where(c == 0, out_weight, came), jnp.where(c == 0, came, out_weight)], axis=0
    )
    lines = [head]
    for step in (1, 2, 3):
        lines.append(lax.ppermute(head, ("xh", "y", "c"), row_pairs(step, False)))
    head = pick(lines, (y - source) % 4)
    out_full = gather_four(head, "z", z, 0).reshape(256, D)

    table = rotary_table()
    rows = tokens.astype(F32)
    first_scale = rms_scale(rows)
    id_rows = jnp.pad(doc_ids.astype(BF16)[None], ((0, 15), (0, D - CAP)))
    payload = jnp.concatenate([(rows * first_scale).astype(BF16), id_rows], axis=0)
    first = share_parts(after(payload, spread, feed_spread))
    packed = after(packed, qkv_full, out_full, *first[1:4])
    packed = lax.all_gather(packed, ("y", "z"), axis=0, tiled=True)

    queries, key_values, mixed, far, near = attend(first, table, qkv_full, out_full)
    upstream = share_parts(after(cotangent, *first[1:4]), mixed)
    far = after(far, upstream[1])
    shuffle = after(jnp.concatenate([order_of_columns(0), order_of_columns(1)], axis=1), mixed)
    blocks = pair_blocks(near, far)
    prepared = prepare_back(first, table, after(queries, *blocks), key_values)
    midway = rows + ring_sum(blocks, shuffle, *prepared)

    second_scale = rms_scale(midway)
    back, down_full = feed_back(upstream, packed)
    second = share_parts((midway * second_scale).astype(BF16), back)
    hidden, grad_feed, far, near = feed_forward(second, packed, back)
    blocks = pair_blocks(near, far)
    pack = feed_grads(second, upstream, after(hidden, *blocks), grad_feed)
    came = tuple(to_ring(blocks[spot], STEPS[spot]) for spot in (1, 2, 3))
    out_far, out_near = output_product(after(hidden, pack), down_full)
    grad_mid, grad_low = norm_back_sum(blocks[0], after(came, pack, out_far), midway, cotangent)
    out_blocks = pair_blocks(out_near, after(out_far, grad_low))
    third = share_parts(grad_low, *out_blocks)
    pack = lax.psum_scatter(after(pack, *came, out_far), ("y", "z"), scatter_dimension=0, tiled=True)

    out_term = out_grads(third, mixed).reshape(4, 64, D)
    out_sent = four_pieces(out_term, z, 0)
    out_came = tuple(shifted(out_sent[step], "z", step) for step in (1, 2))
    grad_qkv, far, near = attend_back(
        third, qkv_full, after(out_full, *out_sent, *out_blocks), prepared
    )
    product = ring_sum(out_blocks, grad_qkv)
    output = (midway + product).astype(BF16)
    out_came += (shifted(after(out_sent[3], grad_qkv), "z", 3),)
    out_part = four_sum(out_sent, after(out_came, product))
    far = after(far, out_part)
    sent = out_part.astype(BF16)
    out_came = tuple(
        lax.ppermute(sent, ("xh", "y", "c"), row_pairs(step, True)) for step in (1, 2, 3)
    )
    qkv_term = qkv_grads(first, after(grad_qkv, sent))
    blocks = pair_blocks(near, far, qkv_term)
    out_came = after(out_came, *blocks)
    out_part = (out_part + sum(item.astype(F32) for item in out_came)).astype(BF16)

    def halves(item):
        low, high = item[:, :32], item[:, 32:]
        return jnp.where(c == 0, low, high), jnp.where(c == 0, high, low)

    sent = four_pieces(after(qkv_term, out_part, *blocks), y, 1)
    came = exchange(sent, "y")
    ring_came = (to_ring(blocks[1], STEPS[1]), to_ring(blocks[2], STEPS[2]))
    corner = jnp.concatenate([pack[176:, 512 * k : 512 * (k + 1)] for k in range(3)], axis=0)
    down_part = jnp.concatenate([pack[128:176], corner], axis=1)
    feed_part = pack[:128].reshape(2, 64, 2 * WIDE)
    feed_mine, feed_away = halves(feed_part)
    came, ring_came, feed_mine, feed_away, down_part = lax.optimization_barrier(
        (came, ring_came, feed_mine, feed_away, down_part)
    )
    sent = four_pieces(four_sum(sent, came).astype(BF16).reshape(2, 4, 64, 384), z, 1)
    came = exchange(sent, "z")
    last_came = to_ring(blocks[3], STEPS[3])
    feed_came = swap(feed_away, "c")
    came, last_came, feed_came = lax.optimization_barrier((came, last_came, feed_came))

    def in_order(mine, came):
        return jnp.where(c == 0, mine, came), jnp.where(c == 0, came, mine)

    def along_ring(both, more):
        here = jnp.where(xl == 0, both[0], both[1])
        there = jnp.where(xl == 0, both[1], both[0])
        across = jnp.concatenate([here, more], axis=1)
        return here, (to_ring(there, 1), to_ring(across, 2), to_ring(there, 3))

    down_wide = jnp.concatenate(
        [down_part[:32], jnp.concatenate([down_part[32:, :1024], down_part[32:, 1024:]], axis=0)],
        axis=1,
    )
    feed_here, feed_came = along_ring(
        jnp.concatenate(in_order(feed_mine, feed_came), axis=2), down_wide
    )

    qkv_part = four_sum(sent, came).astype(BF16)
    qkv_mine, qkv_away = halves(qkv_part)
    away = jnp.where(c == 0, out_part[32:], out_part[:32])
    sent = jnp.concatenate(
        [
            qkv_away.reshape(64, 384),
            jnp.concatenate([away[:, :1024], away[:, 1024:]], axis=0),
        ],
        axis=1,
    )
    came = swap(sent, "c")
    zero, one = in_order(qkv_mine, came[:, :384].reshape(2, 32, 384))
    pair = zero[:, :, 256:].astype(F32) + one[:, :, 256:].astype(F32)
    both = jnp.concatenate([zero[:, :, :256], one[:, :, :256], pair.astype(BF16)], axis=2)
    out_half = jnp.where(
        y % 2 == c,
        jnp.where(c == 0, out_part[:32], out_part[32:]),
        jnp.concatenate([came[:32, 384:], came[32:, 384:]], axis=1),
    )
    both, out_half = lax.optimization_barrier((both, out_half))
    qkv_here, came = along_ring(both, out_half)
    feed_came = after(feed_came, both)

    inner_one = blocks[0] + sum(item.astype(F32) for item in ring_came + (last_came,))
    tokens_grad = grad_mid + norm_back(rows, first_scale, inner_one)
    down_other = feed_came[1][:, 3072:]
    down_other = jnp.concatenate(
        [
            down_other[:, :2048],
            jnp.concatenate([down_other[:16, 2048:], down_other[16:, 2048:]], axis=1),
        ],
        axis=0,
    )
    down_grad = jnp.concatenate(
        [
            jnp.where(xh == 0, down_part, down_other)[:44],
            jnp.where(xh == 0, down_other, down_part)[:44],
        ],
        axis=0,
    ).astype(F32)
    place = jnp.stack([2 * xh + xl, (y // 2 == xh).astype(jnp.int32)]).astype(jnp.int32)
    gate_grad, up_grad, second_grad = feed_finish(
        place, feed_here, feed_came, shuffle, second_col, gate_weight, up_weight
    )
    weights = (query_weight, key_weight, value_weight)
    came = after(came, gate_grad, up_grad, second_grad, down_grad)
    query_grad, key_grad, value_grad, first_grad, out_grad = finish(
        place, qkv_here, came, first_col, weights, out_half
    )

    return (
        output,
        tokens_grad,
        first_grad[:, 0],
        query_grad,
        key_grad,
        value_grad,
        out_grad,
        second_grad[:, 0],
        gate_grad,
        up_grad,
        down_grad,
    )


def solution(mesh):
    fine = Mesh(mesh.devices.reshape(2, 2, 4, 4, 2), ("xh", "xl", "y", "z", "c"))
    everyone = ("xh", "xl", "y", "z", "c")
    group = ("xl", "y", "z", "c")
    in_specs = (
        P(everyone, None),
        P(everyone),
        P(group),
        P(group, None),
        P(group, None),
        P(group, None),
        P(group, None),
        P(group),
        P(group, None),
        P(group, None),
        P(group, None),
        P(everyone, None),
    )
    out_specs = (
        P(everyone, None),
        P(everyone, None),
        P(group),
        P(group, None),
        P(group, None),
        P(group, None),
        P(group, None),
        P(group),
        P(group, None),
        P(group, None),
        P(group, None),
    )
    return jax.shard_map(
        on_device, mesh=fine, in_specs=in_specs, out_specs=out_specs, check_vma=False
    )
```
